32 devices in a mesh: dp: 8 (over y, x, core), outer: 4 (over z).
Axes of the slice: x: 2, y: 2, z: 4, core: 2. Of those that a mesh axis runs over, the one named last changes fastest.
Arguments:
- questions: bfloat16 [256, 64, 256], P(('dp', 'outer')), may hold values from -6 to 6
- passages: bfloat16 [256, 256, 256], P(('dp', 'outer')), may hold values from -6 to 6
- q_lengths: int32 [256], P(('dp', 'outer')), may hold values from 16 to 64, as said below
- p_lengths: int32 [256], P(('dp', 'outer')), may hold values from 64 to 256, as said below
- positives: int32 [256, 4], P(('dp', 'outer')), may hold values from 0 to 255
- pos_counts: int32 [256], P(('dp', 'outer')), may hold values from 1 to 4
- attn: float32 [2, 4, 256, 256], replicated, may hold values from -0.375 to 0.375
- w_in: float32 [2, 256, 1024], replicated, may hold values from -0.375 to 0.375
- w_out: float32 [2, 1024, 256], replicated, may hold values from -0.1875 to 0.1875
- gains: float32 [2, 2, 256], replicated, may hold values from 0.5 to 1.5
- biases: float32 [2, 2560], replicated, may hold values from -0.3 to 0.3
- attn_mom: float32 [2, 4, 256, 256], replicated, may hold values from -0.00956832 to 0.00956832
- w_in_mom: float32 [2, 256, 1024], replicated, may hold values from -0.00956832 to 0.00956832
- w_out_mom: float32 [2, 1024, 256], replicated, may hold values from -0.00956832 to 0.00956832
- gain_mom: float32 [2, 2, 256], replicated, may hold values from -0.15309311 to 0.15309311
- bias_mom: float32 [2, 2560], replicated, may hold values from -0.03827328 to 0.03827328
- attn_err: float32 [32, 2, 4, 256, 256], P(('dp', 'outer')), may hold values from -0.12 to 0.12
- w_in_err: float32 [32, 2, 256, 1024], P(('dp', 'outer')), may hold values from -0.12 to 0.12
- w_out_err: float32 [32, 2, 1024, 256], P(('dp', 'outer')), may hold values from -0.12 to 0.12
- attn_start: float32 [2, 4, 256, 8], replicated, may hold values from -6 to 6
- w_in_start: float32 [2, 1024, 8], replicated, may hold values from -6 to 6
- w_out_start: float32 [2, 256, 8], replicated, may hold values from -6 to 6
Outputs:
- question_loss: float32 [256], P(('dp', 'outer'))
- question_grad: float32 [256, 64, 256], P(('dp', 'outer'))
- passage_grad: float32 [256, 256, 256], P(('dp', 'outer'))
- attn_new: float32 [2, 4, 256, 256], replicated
- w_in_new: float32 [2, 256, 1024], replicated
- w_out_new: float32 [2, 1024, 256], replicated
- gains_new: float32 [2, 2, 256], replicated
- biases_new: float32 [2, 2560], replicated
- attn_mom_new: float32 [2, 4, 256, 256], replicated
- w_in_mom_new: float32 [2, 256, 1024], replicated
- w_out_mom_new: float32 [2, 1024, 256], replicated
- gain_mom_new: float32 [2, 2, 256], replicated
- bias_mom_new: float32 [2, 2560], replicated
- attn_err_new: float32 [32, 2, 4, 256, 256], P(('dp', 'outer'))
- w_in_err_new: float32 [32, 2, 256, 1024], P(('dp', 'outer'))
- w_out_err_new: float32 [32, 2, 1024, 256], P(('dp', 'outer'))
- attn_factor: float32 [2, 4, 256, 8], replicated
- w_in_factor: float32 [2, 1024, 8], replicated
- w_out_factor: float32 [2, 256, 8], replicated
- grad_norm: float32 [], replicated
The draws below stay inside these ranges and needn't reach their ends.
Inputs may be any that keep to these rules, and one draw needn't show every extreme that they name: `q_lengths`: at least one question has 64 tokens. `p_lengths`: at least one passage has 256 tokens. `positives`: entries past a row's pos_counts are ignored; a list may name a passage twice.
All inputs are finite; a program needn't handle non-finite values.
Results may differ from the reference program's by a relative error of at most 0.015.
The reference program's roundings to bfloat16 on the way count: a program that leaves them out, or rounds other values in their place, can miss the bound.
Values may be sent and summed in bfloat16 or wider, within the bound.
No kernel may reach another device: no remote copies, remote signals or barrier semaphores. Data moves between devices by JAX's collectives and lax.ppermute only.
A program may use at most 192 MiB of HBM per device.

```python
import jax
import jax.numpy as jnp
from jax import lax

D = 256
HEAD = 64
FF = 1024
QLEN = 64
PLEN = 256
Q_DEV = 8
PSG_DEV = 8
KPOS = 4
RANK = 8
REPLICAS = 32
QUESTIONS = 256
PASSAGES = 256
N_DP = 8
N_OUTER = 4


def fixed_longest(key, entries, longest):
    drawn = jax.random.randint(key, (entries,), longest // 4, longest + 1)
    chosen = jax.random.randint(jax.random.fold_in(key, 11), (), 0, entries)
    return jnp.where(jnp.arange(entries) == chosen, longest, drawn).astype(jnp.int32)


def draw_q_lengths(key, part):
    key = jax.random.fold_in(key, 1)
    return fixed_longest(key, QUESTIONS, QLEN)


def draw_p_lengths(key, part):
    key = jax.random.fold_in(key, 2)
    return fixed_longest(key, PASSAGES, PLEN)


def touch_ends(array, own_key, smallest, largest):
    spot = [jax.random.randint(jax.random.fold_in(own_key, axis), (), 0, length) for axis, length in enumerate(array.shape)]
    widest = array.shape.index(max(array.shape))
    neighbour = spot[:widest] + [(spot[widest] + 1) % array.shape[widest]] + spot[widest + 1:]
    return array.at[tuple(spot)].set(smallest).at[tuple(neighbour)].set(largest)


def levels(own_key, shape, split, least, largest):
    loudness = 1.0
    for axis_at, blocks in split:
        draws = jax.random.uniform(jax.random.fold_in(jax.random.fold_in(own_key, 6), axis_at), (blocks,), jnp.float32, least / len(split), largest / len(split))
        loudness = loudness * jnp.repeat(jnp.exp(draws), shape[axis_at] // blocks).reshape((-1,) + (1,) * (len(shape) - 1 - axis_at))
    return loudness


def normal_values(key, shape, spread, bound, split=(), kind=jnp.bfloat16):
    array = spread * jax.random.normal(key, shape, jnp.float32)
    if split:
        array = array * levels(key, shape, split, -0.22, 0.18)
    return jnp.clip(array, -bound, bound).astype(kind)


def setup_inputs(seed: int = 0) -> dict:
    arg_keys = jax.random.split(jax.random.key(seed), 23)
    return {
        "questions": normal_values(arg_keys[0], (QUESTIONS, QLEN, D), 1.0, 6.0, ((0, 32),)),
        "passages": normal_values(arg_keys[1], (PASSAGES, PLEN, D), 1.0, 6.0, ((0, 32),)),
        "q_lengths": draw_q_lengths(jax.random.fold_in(arg_keys[22], 71), 0),
        "p_lengths": draw_p_lengths(jax.random.fold_in(arg_keys[22], 71), 0),
        "positives": touch_ends(jax.random.randint(arg_keys[4], (QUESTIONS, KPOS), 0, PASSAGES), jax.random.fold_in(arg_keys[4], 1), 0, PASSAGES - 1).astype(jnp.int32),
        "pos_counts": touch_ends(jax.random.randint(arg_keys[5], (QUESTIONS,), 1, KPOS + 1), jax.random.fold_in(arg_keys[5], 1), 1, KPOS).astype(jnp.int32),
        "attn": normal_values(arg_keys[6], (2, 4, D, D), D ** -0.5, 0.375, (), jnp.float32),
        "w_in": normal_values(arg_keys[7], (2, D, FF), D ** -0.5, 0.375, (), jnp.float32),
        "w_out": normal_values(arg_keys[8], (2, FF, D), FF ** -0.5, 0.1875, (), jnp.float32),
        "gains": jnp.clip(1.0 + 0.1 * jax.random.normal(arg_keys[9], (2, 2, D), jnp.float32), 0.5, 1.5),
        "biases": normal_values(arg_keys[10], (2, 6 * D + FF), 0.05, 0.3, (), jnp.float32),
        "attn_mom": normal_values(arg_keys[11], (2, 4, D, D), (2.0 / (8 * D * D + 4 * D * FF) ** 0.5), 0.00956832, (), jnp.float32),
        "w_in_mom": normal_values(arg_keys[12], (2, D, FF), (2.0 / (8 * D * D + 4 * D * FF) ** 0.5), 0.00956832, (), jnp.float32),
        "w_out_mom": normal_values(arg_keys[13], (2, FF, D), (2.0 / (8 * D * D + 4 * D * FF) ** 0.5), 0.00956832, (), jnp.float32),
        "gain_mom": normal_values(arg_keys[14], (2, 2, D), (32.0 / (8 * D * D + 4 * D * FF) ** 0.5), 0.15309311, (), jnp.float32),
        "bias_mom": normal_values(arg_keys[15], (2, 6 * D + FF), (8.0 / (8 * D * D + 4 * D * FF) ** 0.5), 0.03827328, (), jnp.float32),
        "attn_err": normal_values(arg_keys[16], (REPLICAS, 2, 4, D, D), 0.02, 0.12, ((0, 32),), jnp.float32),
        "w_in_err": normal_values(arg_keys[17], (REPLICAS, 2, D, FF), 0.02, 0.12, ((0, 32),), jnp.float32),
        "w_out_err": normal_values(arg_keys[18], (REPLICAS, 2, FF, D), 0.02, 0.12, ((0, 32),), jnp.float32),
        "attn_start": normal_values(arg_keys[19], (2, 4, D, RANK), 1.0, 6.0, (), jnp.float32),
        "w_in_start": normal_values(arg_keys[20], (2, FF, RANK), 1.0, 6.0, (), jnp.float32),
        "w_out_start": normal_values(arg_keys[21], (2, D, RANK), 1.0, 6.0, (), jnp.float32),
    }


NORM_EPSILON = 1e-06
UNIT_EPSILON = 1e-06
SCORE_SCALE = 20.0
MOMENTUM_DECAY = 0.9
LEARNING_RATE = 10.0
CLIP_NORM = 2.0
MASKED_SCORE = -1e+30
HIGHEST = lax.Precision.HIGHEST

@jax.custom_vjp
def low(v):
    return lax.optimization_barrier(v.astype(jnp.bfloat16)).astype(jnp.float32)

@jax.custom_vjp
def low_back(v):
    return v

def low_keep(v):
    return (low(v), None)

def low_pass(kept, grad):
    return (grad,)

def back_keep(v):
    return (v, None)

def back_low(kept, grad):
    return (low(grad),)
low.defvjp(low_keep, low_pass)
low_back.defvjp(back_keep, back_low)

def rounded_both(values):
    return low(low_back(values))

def matmul_high(left_side, right_side):
    return jnp.matmul(left_side, right_side, precision=HIGHEST)

def split_shifts(shifts, features):
    return [shifts[features * offset:features * (offset + 1)] for offset in range(6)] + [shifts[6 * features:]]

def layer_norm(hidden, gain, shift):
    center = hidden - lax.optimization_barrier(jnp.mean(hidden, axis=-1, keepdims=True))
    inverse = lax.rsqrt(lax.optimization_barrier(jnp.mean(center * center, axis=-1, keepdims=True)) + NORM_EPSILON)
    return center * inverse * gain + shift

def encoder(inputs, lengths, attn, inner, outer, gain_pair, shifts):
    seq_count, length, features = inputs.shape
    head_count = features // HEAD
    query_shift, value_shift, output_shift, first_shift, down_shift, second_shift, up_shift = split_shifts(shifts, features)
    head_shape = (seq_count, length, head_count, HEAD)
    query = rounded_both(matmul_high(inputs, low(attn[0])) + query_shift).reshape(head_shape)
    key_heads = rounded_both(matmul_high(inputs, low(attn[1]))).reshape(head_shape)
    value = rounded_both(matmul_high(inputs, low(attn[2])) + value_shift).reshape(head_shape)
    raw = low_back(jnp.einsum('bqhe,bkhe->bhqk', query, key_heads, precision=HIGHEST))
    valid_keys = lax.broadcasted_iota(jnp.int32, (seq_count, length), 1) < lengths[:, None]
    scores = jnp.where(valid_keys[:, None, None, :], raw * HEAD ** (-0.5), MASKED_SCORE)
    attention = jax.nn.softmax(scores, axis=-1)
    context = rounded_both(jnp.einsum('bhqk,bkhe->bqhe', low(attention), value, precision=HIGHEST).reshape(seq_count, length, features))
    branch = low_back(matmul_high(context, low(attn[3])) + output_shift)
    first = layer_norm(inputs + branch, gain_pair[0], first_shift)
    upper_in = low_back(matmul_high(low(first), low(inner)) + up_shift)
    active = low(jax.nn.gelu(upper_in, approximate=False))
    down = low_back(matmul_high(active, low(outer)) + down_shift)
    second = layer_norm(first + down, gain_pair[1], second_shift)
    position_share = valid_keys.astype(jnp.float32) / lengths[:, None].astype(jnp.float32)
    pooled = lax.optimization_barrier(jnp.sum(second * position_share[:, :, None], axis=1))
    unit = pooled * lax.rsqrt(lax.optimization_barrier(jnp.sum(pooled * pooled, axis=-1, keepdims=True)) + UNIT_EPSILON)
    return low(unit)

def orthonormalize(factor):
    columns = []
    for column_index in range(factor.shape[-1]):
        column = factor[..., column_index]
        for earlier in columns:
            column = column - lax.optimization_barrier(jnp.sum(earlier * column, axis=-1, keepdims=True)) * earlier
        column = column * lax.rsqrt(lax.optimization_barrier(jnp.sum(column * column, axis=-1, keepdims=True)) + 1e-06)
        columns.append(column)
    return jnp.stack(columns, axis=-1)

def momentum_step(weight, moment, gradient, clip_factor):
    moment_new = MOMENTUM_DECAY * moment + clip_factor * gradient
    return (weight - LEARNING_RATE * moment_new, moment_new)

def reference(questions, passages, q_lengths, p_lengths, positives, pos_counts, attn, w_in, w_out, gains, biases, attn_mom, w_in_mom, w_out_mom, gain_mom, bias_mom, attn_err, w_in_err, w_out_err, attn_start, w_in_start, w_out_start):
    replicas = N_DP * N_OUTER
    question_in = questions.astype(jnp.float32).reshape(replicas, Q_DEV, QLEN, D)
    passage_in = passages.astype(jnp.float32).reshape(replicas, PSG_DEV, PLEN, D)
    question_len = q_lengths.reshape(replicas, Q_DEV)
    passage_len = p_lengths.reshape(replicas, PSG_DEV)

    def copies(weight):
        return jnp.broadcast_to(weight, (replicas,) + weight.shape)

    def total_loss(question_x, passage_x, attn_copies, inner_copies, outer_copies, gain_copies, shift_copies):
        question_units = jax.vmap(encoder)(question_x, question_len, attn_copies[:, 0], inner_copies[:, 0], outer_copies[:, 0], gain_copies[:, 0], shift_copies[:, 0]).reshape(QUESTIONS, D)
        passage_units = jax.vmap(encoder)(passage_x, passage_len, attn_copies[:, 1], inner_copies[:, 1], outer_copies[:, 1], gain_copies[:, 1], shift_copies[:, 1]).reshape(PASSAGES, D)
        raw = low_back(jnp.dot(question_units, passage_units.T, precision=HIGHEST))
        scores = SCORE_SCALE * raw
        slot_live = lax.broadcasted_iota(jnp.int32, (QUESTIONS, KPOS), 1) < pos_counts[:, None]
        columns = lax.broadcasted_iota(jnp.int32, (1, 1, PASSAGES), 2)
        is_positive = jnp.any((positives[:, :, None] == columns) & slot_live[:, :, None], axis=1)
        whole_lse = jax.nn.logsumexp(scores, axis=1)
        within = jax.nn.logsumexp(jnp.where(is_positive, scores, MASKED_SCORE), axis=1)
        return whole_lse - within
    question_loss, pullback = jax.vjp(total_loss, question_in, passage_in, copies(attn), copies(w_in), copies(w_out), copies(gains), copies(biases))
    grads = pullback(jnp.ones_like(question_loss))
    question_grad = grads[0].reshape(QUESTIONS, QLEN, D)
    passage_grad = grads[1].reshape(PASSAGES, PLEN, D)
    gain_sum = lax.optimization_barrier(jnp.sum(grads[5], axis=0))
    shift_sum = lax.optimization_barrier(jnp.sum(grads[6], axis=0))
    merged_attn = grads[2] + attn_err
    merged_inner = grads[3] + w_in_err
    merged_outer = grads[4] + w_out_err
    basis_attn = orthonormalize(jnp.einsum('rtkmn,tknj->tkmj', merged_attn, attn_start, precision=HIGHEST))
    basis_inner = orthonormalize(jnp.einsum('rtmn,tnj->tmj', merged_inner, w_in_start, precision=HIGHEST))
    basis_outer = orthonormalize(jnp.einsum('rtmn,tnj->tmj', merged_outer, w_out_start, precision=HIGHEST))
    right_attn = jnp.einsum('rtkmn,tkmj->tknj', merged_attn, basis_attn, precision=HIGHEST)
    right_inner = jnp.einsum('rtmn,tmj->tnj', merged_inner, basis_inner, precision=HIGHEST)
    right_outer = jnp.einsum('rtmn,tmj->tnj', merged_outer, basis_outer, precision=HIGHEST)
    approx_attn = jnp.einsum('tkmj,tknj->tkmn', basis_attn, right_attn, precision=HIGHEST)
    approx_inner = jnp.einsum('tmj,tnj->tmn', basis_inner, right_inner, precision=HIGHEST)
    approx_outer = jnp.einsum('tmj,tnj->tmn', basis_outer, right_outer, precision=HIGHEST)
    attn_err_new = merged_attn - approx_attn[None] / replicas
    w_in_err_new = merged_inner - approx_inner[None] / replicas
    w_out_err_new = merged_outer - approx_outer[None] / replicas
    norm_square = jnp.sum(approx_attn * approx_attn) + jnp.sum(approx_inner * approx_inner) + jnp.sum(approx_outer * approx_outer) + jnp.sum(gain_sum * gain_sum) + jnp.sum(shift_sum * shift_sum)
    grad_norm = jnp.sqrt(norm_square)
    clip_factor = jnp.minimum(1.0, CLIP_NORM / grad_norm)
    attn_new, attn_mom_new = momentum_step(attn, attn_mom, approx_attn, clip_factor)
    w_in_new, w_in_mom_new = momentum_step(w_in, w_in_mom, approx_inner, clip_factor)
    w_out_new, w_out_mom_new = momentum_step(w_out, w_out_mom, approx_outer, clip_factor)
    gains_new, gain_mom_new = momentum_step(gains, gain_mom, gain_sum, clip_factor)
    biases_new, bias_mom_new = momentum_step(biases, bias_mom, shift_sum, clip_factor)
    return (question_loss, question_grad, passage_grad, attn_new, w_in_new, w_out_new, gains_new, biases_new, attn_mom_new, w_in_mom_new, w_out_mom_new, gain_mom_new, bias_mom_new, attn_err_new, w_in_err_new, w_out_err_new, right_attn, right_inner, right_outer, grad_norm)
```

```python
import functools
import math

import jax
import jax.numpy as jnp
from jax import lax
from jax.experimental import pallas as pl
from jax.experimental.pallas import tpu as pltpu
from jax.sharding import PartitionSpec as P

HEAD = 64
TOK = 256
ONES = 16

NORM_EPSILON = 1e-06
UNIT_EPSILON = 1e-06
SCORE_SCALE = 20.0
MOMENTUM_DECAY = 0.9
LEARNING_RATE = 10.0
CLIP_NORM = 2.0
MASKED_SCORE = -1e30
HIGHEST = lax.Precision.HIGHEST
AXES = ("dp", "outer")
F32 = jnp.float32
BF16 = jnp.bfloat16
VMEM_LIMIT = 56 << 20


def mm(a, b, precision=None):
    return lax.dot_general(a, b, (((1,), (0,)), ((), ())), precision=precision, preferred_element_type=F32)


def mm_nt(a, b, precision=None):
    return lax.dot_general(a, b, (((1,), (1,)), ((), ())), precision=precision, preferred_element_type=F32)


def mm_tn(a, b, precision=None):
    return lax.dot_general(a, b, (((0,), (0,)), ((), ())), precision=precision, preferred_element_type=F32)


def wide(column):
    return jnp.concatenate([column, column], axis=1)


def split_two(v):
    high = v.astype(BF16)
    return high, (v - high.astype(F32)).astype(BF16)


def split_three(v):
    high = v.astype(BF16)
    rest = v - high.astype(F32)
    middle = rest.astype(BF16)
    return high, middle, (rest - middle.astype(F32)).astype(BF16)


def norm_columns(hidden, gain, shift):
    share = 1.0 / hidden.shape[0]
    center = hidden - jnp.sum(hidden, axis=0, keepdims=True) * share
    inverse = lax.rsqrt(jnp.sum(center * center, axis=0, keepdims=True) * share + NORM_EPSILON)
    normed = center * inverse
    return normed * gain + shift, normed, inverse


def norm_columns_back(grad, normed, inverse, gain):
    share = 1.0 / grad.shape[0]
    scaled = grad * gain
    mean = jnp.sum(scaled, axis=0, keepdims=True) * share
    along = jnp.sum(scaled * normed, axis=0, keepdims=True) * share
    return inverse * (scaled - mean - normed * along)


def gelu_and_slope(u):
    d = 1.0 + (0.3275911 * 0.5**0.5) * jnp.abs(u)
    t = pl.reciprocal(d, approx=True)
    t = t * (2.0 - d * t)
    poly = t * (0.127414796 + t * (-0.142248368 + t * (0.7107068705 + t * (-0.7265760135 + t * 0.5307027145))))
    bell = jnp.exp2(u * u * (-0.5 * math.log2(math.e)))
    tail = poly * bell
    phi = jnp.where(u >= 0.0, 1.0 - tail, tail)
    return u * phi, phi + u * bell * (0.5 / math.pi) ** 0.5


def forward_kernel(
    nqu, qlen, plen, xq, xp, attn, w_in, w_out, gains, biases,
    x_out, qk_out, v_out, p_out, ctx_out, n1_out, first_out, slope_out, act_out, n2_out, inv_out, share_out, pooled_out, units_out,
    wproj, wo_t, win_t, wout_t, bias_bc, gain_bc, qblk, xs, away,
):
    i = pl.program_id(0)
    last = pl.num_programs(0) - 1
    is_q = i < nqu
    t = jnp.where(is_q, 0, 1)
    d = xs.shape[1]
    ff = win_t.shape[0]
    heads = d // HEAD
    segs = TOK // HEAD

    @pl.when(i == 0)
    def _():
        qblk[...] = jnp.zeros_like(qblk)

    @pl.when((i == 0) | (i == nqu))
    def _():
        eye = (lax.broadcasted_iota(jnp.int32, (d, d), 0) == lax.broadcasted_iota(jnp.int32, (d, d), 1)).astype(F32).astype(BF16)
        for j in range(3):
            wproj[j * d : (j + 1) * d, :] = mm_nt(eye, attn[0, j].astype(BF16)).astype(BF16)
        wproj[3 * d : 4 * d, :] = eye
        wproj[4 * d : 5 * d, :] = attn[0, 1].astype(BF16)
        wproj[5 * d : 6 * d, :] = attn[0, 2].astype(BF16)
        wo_t[...] = mm_nt(eye, attn[0, 3].astype(BF16)).astype(BF16)
        for c in range(ff // d):
            at = slice(c * d, (c + 1) * d)
            win_t[at, :] = mm_nt(eye, w_in[0, :, at].astype(BF16)).astype(BF16)
            wout_t[:, at] = mm_nt(eye, w_out[0, at, :].astype(BF16)).astype(BF16)
        for c in range(bias_bc.shape[0] // d):
            row = biases[pl.ds(t, 1), c * d : (c + 1) * d]
            bias_bc[c * d : (c + 1) * d, :] = jnp.broadcast_to(row, (128, d)).T
        for c in range(2):
            row = gains[pl.ds(t * 2 + c, 1), :]
            gain_bc[c * d : (c + 1) * d, :] = jnp.broadcast_to(row, (128, d)).T

    @pl.when(is_q)
    def _():
        xs[...] = xq[0]

    @pl.when(jnp.logical_not(is_q))
    def _():
        xs[...] = xp[0]

    lens = [qlen[jnp.minimum(i, nqu - 1) * segs + s] for s in range(segs)]
    whole = plen[jnp.maximum(i - nqu, 0)]

    def length_of(segment):
        out = jnp.full(segment.shape, lens[segs - 1], jnp.int32)
        for s in range(segs - 1):
            out = jnp.where(segment == s, lens[s], out)
        return jnp.where(is_q, out, whole)

    key = lax.broadcasted_iota(jnp.int32, (TOK, TOK), 0)
    ask = lax.broadcasted_iota(jnp.int32, (TOK, TOK), 1)
    bad_far = is_q & ((key // HEAD) != (ask // HEAD))
    place = jnp.where(is_q, key % HEAD, key)
    away[...] = jnp.where(bad_far | (place >= length_of(key // HEAD)), MASKED_SCORE, 0.0)

    row = lax.broadcasted_iota(jnp.int32, (8, TOK), 0)
    token = lax.broadcasted_iota(jnp.int32, (8, TOK), 1)
    live_len = length_of(token // HEAD)
    owner = jnp.where(is_q, token // HEAD, 0)
    place = jnp.where(is_q, token % HEAD, token)
    share = jnp.where((place < live_len) & (row == owner), 1.0 / live_len.astype(F32), 0.0)
    share_out[0] = share

    def bias(at, size):
        return wide(bias_bc[at : at + size, :])

    x = xs[...]
    q_t = (mm_nt(wproj[0:d, :], x) + bias(0, d)).astype(BF16)
    qk_out[0, 0:d, :] = q_t
    qk_out[0, d : 2 * d, :] = mm_nt(wproj[d : 2 * d, :], x).astype(BF16)
    v_t = (mm_nt(wproj[2 * d : 3 * d, :], x) + bias(d, d)).astype(BF16)
    x_t = mm_nt(wproj[3 * d : 4 * d, :], x)
    x_out[0, 0:d, :] = x_t.astype(BF16)
    k_row = mm(x, wproj[4 * d : 5 * d, :]).astype(BF16)
    v_out[0] = (mm(x, wproj[5 * d : 6 * d, :]) + biases[pl.ds(t, 1), d : 2 * d]).astype(BF16)
    for h in range(heads):
        qblk[h * HEAD : (h + 1) * HEAD, h * TOK : (h + 1) * TOK] = q_t[h * HEAD : (h + 1) * HEAD, :] * BF16(HEAD**-0.5)
    for h in range(heads):
        scores = mm(k_row, qblk[:, h * TOK : (h + 1) * TOK]) + away[...]
        exponent = jnp.exp(scores - jnp.max(scores, axis=0, keepdims=True))
        probs = exponent * (1.0 / jnp.sum(exponent, axis=0, keepdims=True))
        p_low = probs.astype(BF16)
        p_out[0, h] = p_low
        ctx_out[0, h * HEAD : (h + 1) * HEAD, :] = mm(v_t[h * HEAD : (h + 1) * HEAD, :], p_low).astype(BF16)
    hidden = x_t + (mm(wo_t[...], ctx_out[0, 0:d, :]) + bias(2 * d, d))
    first, n1, inv1 = norm_columns(hidden, wide(gain_bc[0:d, :]), bias(3 * d, d))
    n1_out[0] = n1
    first_low = first.astype(BF16)
    first_out[0, 0:d, :] = first_low
    hidden = first + bias(4 * d, d)
    for c in range(ff // d):
        at = slice(c * d, (c + 1) * d)
        upper = mm(win_t[at, :], first_low) + bias(6 * d + c * d, d)
        active, slope = gelu_and_slope(upper)
        slope_out[0, at, :] = slope
        active_low = active.astype(BF16)
        act_out[0, at, :] = active_low
        hidden = hidden + mm(wout_t[:, at], active_low)
    second, n2, inv2 = norm_columns(hidden, wide(gain_bc[d : 2 * d, :]), bias(5 * d, d))
    n2_out[0] = n2
    inv_out[0] = jnp.where(row == 0, inv1, inv2)
    pooled = mm_nt(share, second, HIGHEST)
    ones = jnp.ones((ONES, TOK), BF16)
    x_out[0, d:, :] = ones
    ctx_out[0, d:, :] = ones
    first_out[0, d:, :] = ones
    act_out[0, ff:, :] = ones

    @pl.when(is_q)
    def _():
        for s in range(segs):
            pooled_out[pl.ds(i * segs + s, 1), :] = pooled[s : s + 1, :]

    @pl.when(jnp.logical_not(is_q))
    def _():
        pooled_out[pl.ds(nqu * segs + i - nqu, 1), :] = pooled[0:1, :]

    @pl.when(i == last)
    def _():
        rows = pooled_out[...]
        unit = (rows * lax.rsqrt(jnp.sum(rows * rows, axis=1, keepdims=True) + UNIT_EPSILON)).astype(BF16)
        units_out[...] = jnp.broadcast_to(unit[None], units_out.shape)


def tower_of(nqu):
    return lambda i, *_: jnp.where(i < nqu, 0, 1)


def unit_spec(*shape):
    return pl.BlockSpec((1,) + shape, lambda i, *_: (i,) + (0,) * len(shape))


def tower_spec(nqu, *shape):
    return pl.BlockSpec((1,) + shape, lambda i, *_: (jnp.where(i < nqu, 0, 1),) + (0,) * len(shape))


def whole_spec(*shape):
    return pl.BlockSpec(shape, lambda i, *_: (0,) * len(shape))


def forward(devices, q_lengths, p_lengths, xq, xp, attn, w_in, w_out, gains, biases):
    nqu, npu = xq.shape[0], xp.shape[0]
    units = nqu + npu
    d, ff = w_in.shape[1:]
    heads = d // HEAD
    seqs = q_lengths.shape[0] + npu
    outs = [
        ((d + ONES, TOK), BF16),
        ((2 * d, TOK), BF16),
        ((TOK, d), BF16),
        ((heads, TOK, TOK), BF16),
        ((d + ONES, TOK), BF16),
        ((d, TOK), F32),
        ((d + ONES, TOK), BF16),
        ((ff, TOK), F32),
        ((ff + ONES, TOK), BF16),
        ((d, TOK), F32),
        ((8, TOK), F32),
        ((8, TOK), F32),
    ]
    return pl.pallas_call(
        functools.partial(forward_kernel, nqu),
        grid_spec=pltpu.PrefetchScalarGridSpec(
            num_scalar_prefetch=2,
            grid=(units,),
            in_specs=[
                pl.BlockSpec((1, TOK, d), lambda i, *_: (jnp.minimum(i, nqu - 1), 0, 0)),
                pl.BlockSpec((1, TOK, d), lambda i, *_: (jnp.maximum(i - nqu, 0), 0, 0)),
                tower_spec(nqu, 4, d, d),
                tower_spec(nqu, d, ff),
                tower_spec(nqu, ff, d),
                whole_spec(4, d),
                whole_spec(2, biases.shape[1]),
            ],
            out_specs=[unit_spec(*shape) for shape, _ in outs] + [whole_spec(seqs, d), whole_spec(devices, seqs, d)],
            scratch_shapes=[
                pltpu.VMEM((6 * d, d), BF16),
                pltpu.VMEM((d, d), BF16),
                pltpu.VMEM((ff, d), BF16),
                pltpu.VMEM((d, ff), BF16),
                pltpu.VMEM((biases.shape[1], 128), F32),
                pltpu.VMEM((2 * d, 128), F32),
                pltpu.VMEM((d, heads * TOK), BF16),
                pltpu.VMEM((TOK, d), BF16),
                pltpu.VMEM((TOK, TOK), F32),
            ],
        ),
        out_shape=[jax.ShapeDtypeStruct((units,) + shape, kind) for shape, kind in outs]
        + [jax.ShapeDtypeStruct((seqs, d), F32), jax.ShapeDtypeStruct((devices, seqs, d), BF16)],
        compiler_params=pltpu.CompilerParams(vmem_limit_bytes=VMEM_LIMIT),
        name="forward",
    )(q_lengths, p_lengths, xq, xp, attn, w_in, w_out, gains.reshape(4, d), biases)


def contrast_kernel(nqu, index, units, lists, pooled, loss_out, gp_out, low_rows, gup_rows):
    devices, seqs, d = units.shape
    own = lists.shape[0] // devices
    mine = pl.multiple_of(index[0] * own, own)
    pown = seqs - own
    pmine = pl.multiple_of(index[0] * pown, pown)
    both = units[...].astype(F32)
    uq = both[:, :own, :].reshape(devices * own, d).astype(BF16)
    up = both[:, own:, :].reshape(devices * pown, d).astype(BF16)
    scores = SCORE_SCALE * mm_nt(uq, up)
    columns = lax.broadcasted_iota(jnp.int32, scores.shape, 1)
    slots = lists.shape[1] - 1
    positive = None
    for k in range(slots):
        hit = (lists[:, k : k + 1] == columns) & (lists[:, slots : slots + 1] > k)
        positive = hit if positive is None else positive | hit
    highest = jnp.max(scores, axis=1, keepdims=True)
    whole = highest + jnp.log(jnp.sum(jnp.exp(scores - highest), axis=1, keepdims=True))
    chosen = jnp.where(positive, scores, MASKED_SCORE)
    top = jnp.max(chosen, axis=1, keepdims=True)
    within = top + jnp.log(jnp.sum(jnp.exp(chosen - top), axis=1, keepdims=True))
    low = (SCORE_SCALE * (jnp.exp(scores - whole) - jnp.exp(chosen - within))).astype(BF16)
    low_rows[:, : scores.shape[1]] = low.astype(F32)
    low_rows[:, scores.shape[1] :] = jnp.broadcast_to(whole - within, (scores.shape[0], 128))
    loss_out[...] = low_rows[pl.ds(mine, own), scores.shape[1] :]
    grad_q = mm(low_rows[pl.ds(mine, own), : scores.shape[1]].astype(BF16), up)
    gup_rows[...] = mm_tn(low, uq)
    grad_p = gup_rows[pl.ds(pmine, pown), :]
    grad = jnp.concatenate([grad_q, grad_p], axis=0)
    rows = pooled[...]
    inverse = lax.rsqrt(jnp.sum(rows * rows, axis=1, keepdims=True) + UNIT_EPSILON)
    grad = inverse * grad - inverse * inverse * inverse * rows * jnp.sum(rows * grad, axis=1, keepdims=True)
    segs = own // nqu
    gp_out[...] = jnp.zeros_like(gp_out)
    for s in range(own):
        gp_out[s // segs, s % segs : s % segs + 1, :] = grad[s : s + 1, :]
    for s in range(pown):
        gp_out[nqu + s, 0:1, :] = grad[own + s : own + s + 1, :]


def contrast(nqu, npu, index, units, lists, pooled):
    devices, seqs, d = units.shape
    own = lists.shape[0] // devices
    passages = devices * (seqs - own)
    vmem = pl.BlockSpec(memory_space=pltpu.VMEM)
    return pl.pallas_call(
        functools.partial(contrast_kernel, nqu),
        in_specs=[pl.BlockSpec(memory_space=pltpu.SMEM), vmem, vmem, vmem],
        out_specs=[vmem, vmem],
        out_shape=[jax.ShapeDtypeStruct((own, 128), F32), jax.ShapeDtypeStruct((nqu + npu, 8, d), F32)],
        scratch_shapes=[pltpu.VMEM((devices * own, passages + 128), F32), pltpu.VMEM((passages, d), F32)],
        compiler_params=pltpu.CompilerParams(vmem_limit_bytes=VMEM_LIMIT),
        name="contrast",
    )(index, units, lists, pooled)


def left_rows(start_t, matrix):
    s_high, s_low = split_two(start_t)
    m_high, m_low = split_two(matrix)
    both = mm_nt(jnp.concatenate([s_high, s_low], axis=0), m_high)
    return both[:8] + both[8:] + mm_nt(jnp.concatenate([s_high, s_high], axis=0), m_low)[:8]


def right_rows(basis, matrix):
    b_high, b_low = split_two(basis)
    m_high, m_low = split_two(matrix)
    both = mm(jnp.concatenate([b_high, b_low], axis=0), m_high)
    return both[:8] + both[8:] + mm(jnp.concatenate([b_high, b_high], axis=0), m_low)[:8]


def backward_kernel(
    nqu, gp, x_in, qk_in, v_in, p_in, ctx_in, n1_in, first_in, slope_in, act_in, n2_in, inv_in, share_in,
    attn, w_in, w_out, gains, attn_err, in_err, out_err, attn_start, in_start, out_start,
    qgrad, pgrad, attn_m, in_m, out_m, left,
    wqkv, wo, win, wout, gain_bc, gz, graw_s, gqkv, acc_qkv, acc_o, acc_in, acc_out, acc_gain,
):
    i = pl.program_id(0)
    last = pl.num_programs(0) - 1
    is_q = i < nqu
    t = jnp.where(is_q, 0, 1)
    d = wo.shape[0]
    ff = wout.shape[0]
    heads = d // HEAD

    @pl.when(i == 0)
    def _():
        gz[...] = jnp.zeros_like(gz)

    @pl.when((i == 0) | (i == nqu))
    def _():
        for j in range(3):
            wqkv[:, j * d : (j + 1) * d] = attn[0, j].astype(BF16)
        wo[...] = attn[0, 3].astype(BF16)
        win[...] = w_in[0].astype(BF16)
        wout[...] = w_out[0].astype(BF16)
        for c in range(2):
            row = gains[pl.ds(t * 2 + c, 1), :]
            gain_bc[c * d : (c + 1) * d, :] = jnp.broadcast_to(row, (128, d)).T
        acc_qkv[...] = jnp.zeros_like(acc_qkv)
        acc_o[...] = jnp.zeros_like(acc_o)
        acc_in[...] = jnp.zeros_like(acc_in)
        acc_out[...] = jnp.zeros_like(acc_out)
        acc_gain[...] = jnp.zeros_like(acc_gain)

    def add_gain(at, value):
        acc_gain[at * d : (at + 1) * d, :] += value[:, :128] + value[:, 128:]

    grad_second = mm_tn(gp[0], share_in[0], HIGHEST)
    n2 = n2_in[0]
    grad_two = norm_columns_back(grad_second, n2, inv_in[0, 1:2, :], wide(gain_bc[d : 2 * d, :]))
    add_gain(1, grad_second * n2)
    add_gain(3, grad_second)
    down_low = grad_two.astype(BF16)
    acc_out[...] += mm_nt(act_in[0], down_low)
    grad_first = grad_two
    for c in range(ff // d):
        at = slice(c * d, (c + 1) * d)
        up_low = (mm(wout[at, :], down_low) * slope_in[0, at, :]).astype(BF16)
        acc_in[:, at] += mm_nt(first_in[0], up_low)
        grad_first = grad_first + mm(win[:, at], up_low)
    n1 = n1_in[0]
    grad_one = norm_columns_back(grad_first, n1, inv_in[0, 0:1, :], wide(gain_bc[0:d, :]))
    add_gain(0, grad_first * n1)
    add_gain(2, grad_first)
    branch_low = grad_one.astype(BF16)
    acc_o[...] += mm_nt(ctx_in[0], branch_low)
    grad_context = mm(wo[...], branch_low).astype(BF16)
    for h in range(heads):
        at = slice(h * HEAD, (h + 1) * HEAD)
        gz[at, h * TOK : (h + 1) * TOK] = grad_context[at, :]
    for h in range(heads):
        at = slice(h * HEAD, (h + 1) * HEAD)
        p_low = p_in[0, h]
        probs = p_low.astype(F32)
        grad_probs = mm(v_in[0], gz[:, h * TOK : (h + 1) * TOK])
        inner = jnp.sum(grad_probs * probs, axis=0, keepdims=True)
        graw = (probs * (grad_probs - inner) * HEAD**-0.5).astype(BF16)
        gqkv[at, :] = mm(qk_in[0, d + h * HEAD : d + (h + 1) * HEAD, :], graw).astype(BF16)
        gqkv[d + h * HEAD : d + (h + 1) * HEAD, :] = mm_nt(qk_in[0, at, :], graw).astype(BF16)
        gqkv[2 * d + h * HEAD : 2 * d + (h + 1) * HEAD, :] = mm_nt(grad_context[at, :], p_low).astype(BF16)
    acc_qkv[...] += mm_nt(x_in[0], gqkv[...])
    result = (grad_one + mm(wqkv[...], gqkv[...])).T

    @pl.when(is_q)
    def _():
        qgrad[0] = result

    @pl.when(jnp.logical_not(is_q))
    def _():
        pgrad[0] = result

    @pl.when((i == nqu - 1) | (i == last))
    def _():
        base_in = 8 * d
        base_out = base_in + 2 * d
        base_vec = base_out + 2 * ff
        for j in range(4):
            grad = acc_o[0:d, :] if j == 3 else acc_qkv[0:d, j * d : (j + 1) * d]
            merged = grad + attn_err[0, 0, j]
            attn_m[0, j] = merged
            left[:, pl.ds(pl.multiple_of((t * 4 + j) * d, 128), d)] = left_rows(attn_start[0, j], merged)
        merged = acc_in[0:d, :] + in_err[0, 0]
        in_m[0] = merged
        left[:, pl.ds(pl.multiple_of(base_in + t * d, 128), d)] = left_rows(in_start[0], merged)
        merged = acc_out[0:ff, :] + out_err[0, 0]
        out_m[0] = merged
        left[:, pl.ds(pl.multiple_of(base_out + t * ff, 128), ff)] = left_rows(out_start[0], merged)
        sums = mm_nt(jnp.ones((8, 128), F32), acc_gain[...], HIGHEST)

        def vectors():
            yield sums[0:1, 0:d]
            yield sums[0:1, d : 2 * d]
            yield acc_qkv[d : d + 1, 0:d]
            yield acc_qkv[d : d + 1, 2 * d : 3 * d]
            yield acc_o[d : d + 1, :]
            yield sums[0:1, 2 * d : 3 * d]
            yield acc_out[ff : ff + 1, :]
            yield sums[0:1, 3 * d : 4 * d]
            for c in range(ff // d):
                yield acc_in[d : d + 1, c * d : (c + 1) * d]

        for tower in range(2):

            @pl.when(t == tower)
            def _(tower=tower):
                for v, vector in enumerate(vectors()):
                    at = tower * 12 + v
                    left[at // 3 : at // 3 + 1, base_vec + (at % 3) * d : base_vec + (at % 3 + 1) * d] = vector


def backward(nqu, npu, gp, saved, attn, w_in, w_out, gains, attn_err, in_err, out_err, starts):
    units = nqu + npu
    d, ff = w_in.shape[1:]
    heads = d // HEAD
    width = 8 * d + 2 * d + 2 * ff + 3 * d
    tower = functools.partial(tower_spec, nqu)

    def error_spec(*shape):
        return pl.BlockSpec((1, 1) + shape, lambda i: (0, jnp.where(i < nqu, 0, 1)) + (0,) * len(shape))

    return pl.pallas_call(
        functools.partial(backward_kernel, nqu),
        grid=(units,),
        in_specs=[unit_spec(8, d)]
        + [unit_spec(*array.shape[1:]) for array in saved]
        + [tower(4, d, d), tower(d, ff), tower(ff, d), whole_spec(4, d)]
        + [error_spec(4, d, d), error_spec(d, ff), error_spec(ff, d)]
        + [tower(4, 8, d), tower(8, ff), tower(8, d)],
        out_specs=[
            pl.BlockSpec((1, TOK, d), lambda i: (jnp.minimum(i, nqu - 1), 0, 0)),
            pl.BlockSpec((1, TOK, d), lambda i: (jnp.maximum(i - nqu, 0), 0, 0)),
            tower(4, d, d),
            tower(d, ff),
            tower(ff, d),
            whole_spec(8, width),
        ],
        out_shape=[
            jax.ShapeDtypeStruct((nqu, TOK, d), F32),
            jax.ShapeDtypeStruct((npu, TOK, d), F32),
            jax.ShapeDtypeStruct((2, 4, d, d), F32),
            jax.ShapeDtypeStruct((2, d, ff), F32),
            jax.ShapeDtypeStruct((2, ff, d), F32),
            jax.ShapeDtypeStruct((8, width), F32),
        ],
        scratch_shapes=[
            pltpu.VMEM((d, 3 * d), BF16),
            pltpu.VMEM((d, d), BF16),
            pltpu.VMEM((d, ff), BF16),
            pltpu.VMEM((ff, d), BF16),
            pltpu.VMEM((2 * d, 128), F32),
            pltpu.VMEM((d, heads * TOK), BF16),
            pltpu.VMEM((TOK, TOK), BF16),
            pltpu.VMEM((3 * d, TOK), BF16),
            pltpu.VMEM((d + ONES, 3 * d), F32),
            pltpu.VMEM((d + ONES, d), F32),
            pltpu.VMEM((d + ONES, ff), F32),
            pltpu.VMEM((ff + ONES, d), F32),
            pltpu.VMEM((4 * d, 128), F32),
        ],
        compiler_params=pltpu.CompilerParams(vmem_limit_bytes=VMEM_LIMIT),
        name="backward",
    )(gp, *saved, attn, w_in, w_out, gains.reshape(4, d), attn_err, in_err, out_err, *starts)


def right_kernel(left, attn_m, in_m, out_m, basis, right):
    d, ff = in_m.shape[1:]
    places = [(j * d, d) for j in range(8)] + [(8 * d + t * d, d) for t in range(2)] + [(10 * d + t * ff, ff) for t in range(2)]
    blocks = [left[:, at : at + size] for at, size in places]
    for j in range(8):
        for b, block in enumerate(blocks):
            order = lax.broadcasted_iota(jnp.int32, (8, 1), 0)
            column = block[j : j + 1, :]
            dots = jnp.sum(block * column, axis=1, keepdims=True)
            scale = lax.rsqrt(dots[j : j + 1, :] + 1e-06)
            unit = column * scale
            step = jnp.where(order > j, dots * scale, 0.0)
            blocks[b] = jnp.where(order == j, unit, block - step * unit)
    for (at, size), block in zip(places, blocks):
        basis[:, at : at + size] = block
    for j in range(8):
        right[:, j * d : (j + 1) * d] = right_rows(blocks[j], attn_m[j // 4, j % 4])
    for t in range(2):
        right[:, 8 * d + t * ff : 8 * d + (t + 1) * ff] = right_rows(blocks[8 + t], in_m[t])
        right[:, 8 * d + 2 * ff + t * d : 8 * d + 2 * ff + (t + 1) * d] = right_rows(blocks[10 + t], out_m[t])


def right_factors(left, attn_m, in_m, out_m):
    d, ff = in_m.shape[1:]
    vmem = pl.BlockSpec(memory_space=pltpu.VMEM)
    return pl.pallas_call(
        right_kernel,
        in_specs=[vmem] * 4,
        out_specs=[vmem] * 2,
        out_shape=[jax.ShapeDtypeStruct((8, 10 * d + 2 * ff), F32), jax.ShapeDtypeStruct((8, 10 * d + 2 * ff), F32)],
        compiler_params=pltpu.CompilerParams(vmem_limit_bytes=VMEM_LIMIT),
        name="right",
    )(left, attn_m, in_m, out_m)


def update_kernel(
    replicas, basis, right, left, attn_m, in_m, out_m, attn, w_in, w_out, attn_mom, in_mom, out_mom,
    attn_new, in_new, out_new, attn_mom_new, in_mom_new, out_mom_new, attn_err, in_err, out_err, norm_out, clip_s,
):
    i = pl.program_id(0)
    d = attn.shape[2]
    ff = (right.shape[1] - 10 * d) // 2
    t, c = i // 4, i % 4

    @pl.when(i == 0)
    def _():
        places = [((j * d, d), (j * d, d)) for j in range(8)]
        places += [((8 * d + s * d, d), (8 * d + s * ff, ff)) for s in range(2)]
        places += [((10 * d + s * ff, ff), (8 * d + 2 * ff + s * d, d)) for s in range(2)]
        total = jnp.zeros((8, 8), F32)
        for (b_at, b_size), (r_at, r_size) in places:
            b = basis[:, b_at : b_at + b_size]
            r = right[:, r_at : r_at + r_size]
            total = total + mm_nt(b, b, HIGHEST) * mm_nt(r, r, HIGHEST)
        vector = left[:, 10 * d + 2 * ff :]
        square = jnp.sum(jnp.sum(total, axis=1, keepdims=True), axis=0, keepdims=True)
        square = square + jnp.sum(jnp.sum(vector * vector, axis=1, keepdims=True), axis=0, keepdims=True)
        norm = jnp.sqrt(jnp.broadcast_to(square, (8, 128)))
        norm_out[...] = norm
        clip_s[...] = jnp.minimum(1.0, CLIP_NORM / norm)

    clip = clip_s[0:1, 0:1]

    def step(b_at, r_at, merged, weight, moment, weight_new, moment_new, error):
        b1, b2, b3 = split_three(basis[:, pl.ds(pl.multiple_of(b_at, 128), d)])
        r1, r2, r3 = split_three(right[:, pl.ds(pl.multiple_of(r_at, 128), d)])
        approx = mm_tn(jnp.concatenate([b1, b1, b2, b1, b2, b3], axis=0), jnp.concatenate([r1, r2, r1, r3, r2, r1], axis=0))
        moved = MOMENTUM_DECAY * moment + clip * approx
        moment_new[...] = moved.reshape(moment_new.shape)
        weight_new[...] = (weight - LEARNING_RATE * moved).reshape(weight_new.shape)
        error[...] = (merged - approx * (1.0 / replicas)).reshape(error.shape)

    step(i * d, i * d, attn_m[0, 0], attn[0, 0], attn_mom[0, 0], attn_new, attn_mom_new, attn_err)
    step((8 + t) * d, 8 * d + t * ff + c * d, in_m[0], w_in[0], in_mom[0], in_new, in_mom_new, in_err)
    step(10 * d + t * ff + c * d, 8 * d + 2 * ff + t * d, out_m[0], w_out[0], out_mom[0], out_new, out_mom_new, out_err)


def update(replicas, basis, right, left, attn_m, in_m, out_m, attn, w_in, w_out, attn_mom, in_mom, out_mom):
    d, ff = w_in.shape[1:]
    a_spec = pl.BlockSpec((1, 1, d, d), lambda i: (i // 4, i % 4, 0, 0))
    i_spec = pl.BlockSpec((1, d, d), lambda i: (i // 4, 0, i % 4))
    o_spec = pl.BlockSpec((1, d, d), lambda i: (i // 4, i % 4, 0))
    ae_spec = pl.BlockSpec((1, 1, 1, d, d), lambda i: (0, i // 4, i % 4, 0, 0))
    ie_spec = pl.BlockSpec((1, 1, d, d), lambda i: (0, i // 4, 0, i % 4))
    oe_spec = pl.BlockSpec((1, 1, d, d), lambda i: (0, i // 4, i % 4, 0))
    shape = jax.ShapeDtypeStruct
    return pl.pallas_call(
        functools.partial(update_kernel, replicas),
        grid=(8,),
        in_specs=[whole_spec(*basis.shape), whole_spec(*right.shape), whole_spec(*left.shape)] + [a_spec, i_spec, o_spec] * 3,
        out_specs=[a_spec, i_spec, o_spec] * 2 + [ae_spec, ie_spec, oe_spec, whole_spec(8, 128)],
        out_shape=[shape(a.shape, F32) for a in (attn, w_in, w_out, attn, w_in, w_out)]
        + [shape((1,) + a.shape, F32) for a in (attn, w_in, w_out)]
        + [shape((8, 128), F32)],
        scratch_shapes=[pltpu.VMEM((8, 128), F32)],
        compiler_params=pltpu.CompilerParams(vmem_limit_bytes=VMEM_LIMIT),
        name="update",
    )(basis, right, left, attn_m, in_m, out_m, attn, w_in, w_out, attn_mom, in_mom, out_mom)


def swap_with(x, axis, mask):
    return lax.ppermute(x, axis, [(i, i ^ mask) for i in range(lax.axis_size(axis))])


def sum_over(x):
    half = x.shape[1] // 2
    core = lax.axis_index("dp") % 2
    mine = lax.dynamic_slice_in_dim(x, core * half, half, 1)
    other = lax.dynamic_slice_in_dim(x, (1 - core) * half, half, 1)
    mine = mine + swap_with(other, "dp", 1)
    size = lax.axis_size("dp")
    if size == 8:
        steps = [("dp", (2, 4, 6))]
    else:
        steps = [("dp", (1 << b,)) for b in range(1, size.bit_length() - 1)]
    steps.append(("outer", tuple(range(1, lax.axis_size("outer")))))
    for axis, masks in steps:
        for got in [swap_with(mine, axis, mask) for mask in masks]:
            mine = mine + got
    other = swap_with(mine, "dp", 1)
    low = jnp.where(core == 0, mine, other)
    high = jnp.where(core == 0, other, mine)
    return jnp.concatenate([low, high], axis=1)


def momentum_step(weight, moment, gradient, clip_factor):
    moment_new = MOMENTUM_DECAY * moment + clip_factor * gradient
    return (weight - LEARNING_RATE * moment_new, moment_new)


def per_device(
    questions, passages, q_lengths, p_lengths, positives, pos_counts, attn, w_in, w_out, gains, biases, attn_mom, w_in_mom,
    w_out_mom, gain_mom, bias_mom, attn_err, w_in_err, w_out_err, attn_start, w_in_start, w_out_start,
):
    devices = lax.axis_size("dp") * lax.axis_size("outer")
    d, ff = w_in.shape[1:]
    xq = questions.reshape(-1, TOK, d)
    xp = passages.reshape(-1, TOK, d)
    nqu, npu = xq.shape[0], xp.shape[0]
    own = positives.shape[0]
    index = (lax.axis_index("dp") * lax.axis_size("outer") + lax.axis_index("outer")).astype(jnp.int32).reshape(1)
    lists = jnp.concatenate([positives, pos_counts[:, None]], axis=1)
    lists = lax.all_to_all(jnp.broadcast_to(lists[None], (devices,) + lists.shape), AXES, 0, 0).reshape(devices * own, -1)
    *saved, pooled, units = forward(devices, q_lengths, p_lengths, xq, xp, attn, w_in, w_out, gains, biases)
    units = lax.all_to_all(units, AXES, 0, 0)
    loss, gp = contrast(nqu, npu, index, units, lists, pooled)
    starts = [jnp.swapaxes(start, -1, -2) for start in (attn_start, w_in_start, w_out_start)]
    qgrad, pgrad, attn_m, in_m, out_m, left = backward(
        nqu, npu, gp, saved, attn, w_in, w_out, gains, attn_err, w_in_err, w_out_err, starts
    )
    left = sum_over(left)
    basis, right = right_factors(left, attn_m, in_m, out_m)
    right = sum_over(right)
    *new, norm = update(devices, basis, right, left, attn_m, in_m, out_m, attn, w_in, w_out, attn_mom, w_in_mom, w_out_mom)
    attn_new, w_in_new, w_out_new, attn_mom_new, w_in_mom_new, w_out_mom_new, attn_err_new, w_in_err_new, w_out_err_new = new
    grad_norm = norm[0, 0]
    clip = jnp.minimum(1.0, CLIP_NORM / grad_norm)
    vector = left[:, 10 * d + 2 * ff :].reshape(2, 12, d)
    gains_new, gain_mom_new = momentum_step(gains, gain_mom, vector[:, :2], clip)
    biases_new, bias_mom_new = momentum_step(biases, bias_mom, vector[:, 2:].reshape(biases.shape), clip)
    attn_factor = jnp.transpose(right[:, : 8 * d].reshape(8, 2, 4, d), (1, 2, 3, 0))
    w_in_factor = jnp.transpose(right[:, 8 * d : 8 * d + 2 * ff].reshape(8, 2, ff), (1, 2, 0))
    w_out_factor = jnp.transpose(right[:, 8 * d + 2 * ff :].reshape(8, 2, d), (1, 2, 0))
    return (
        loss[:, 0], qgrad.reshape(questions.shape), pgrad.reshape(passages.shape),
        attn_new, w_in_new, w_out_new, gains_new, biases_new,
        attn_mom_new, w_in_mom_new, w_out_mom_new, gain_mom_new, bias_mom_new,
        attn_err_new, w_in_err_new, w_out_err_new, attn_factor, w_in_factor, w_out_factor, grad_norm,
    )


def solution(mesh):
    split = ("dp", "outer")
    share = P(split)
    return jax.shard_map(
        per_device,
        mesh=mesh,
        in_specs=(share,) * 6 + (P(),) * 10 + (share,) * 3 + (P(),) * 3,
        out_specs=(share,) * 3 + (P(),) * 10 + (share,) * 3 + (P(),) * 4,
        check_vma=False,
    )
```

```python
import functools
import math

import jax
import jax.numpy as jnp
from jax import lax
from jax.experimental import pallas as pl
from jax.experimental.pallas import tpu as pltpu
from jax.sharding import PartitionSpec as P

HEAD = 64
TOK = 256
GROUP = 2
PART = 64
ONES = 16

NORM_EPSILON = 1e-06
UNIT_EPSILON = 1e-06
SCORE_SCALE = 20.0
MOMENTUM_DECAY = 0.9
LEARNING_RATE = 10.0
CLIP_NORM = 2.0
MASKED_SCORE = -1e30
HIGHEST = lax.Precision.HIGHEST
AXES = ("dp", "outer")
F32 = jnp.float32
BF16 = jnp.bfloat16
VMEM_LIMIT = 56 << 20
SEND = F32


def mm(a, b, precision=None):
    return lax.dot_general(a, b, (((1,), (0,)), ((), ())), precision=precision, preferred_element_type=F32)


def mm_nt(a, b, precision=None):
    return lax.dot_general(a, b, (((1,), (1,)), ((), ())), precision=precision, preferred_element_type=F32)


def mm_tn(a, b, precision=None):
    return lax.dot_general(a, b, (((0,), (0,)), ((), ())), precision=precision, preferred_element_type=F32)


def wide(column):
    return jnp.concatenate([column] * (GROUP * TOK // 128), axis=1)


def split_two(v):
    high = v.astype(BF16)
    return high, (v - high.astype(F32)).astype(BF16)


def split_three(v):
    high = v.astype(BF16)
    rest = v - high.astype(F32)
    middle = rest.astype(BF16)
    return high, middle, (rest - middle.astype(F32)).astype(BF16)


def norm_columns(hidden, gain, shift):
    share = 1.0 / hidden.shape[0]
    center = hidden - jnp.sum(hidden, axis=0, keepdims=True) * share
    inverse = lax.rsqrt(jnp.sum(center * center, axis=0, keepdims=True) * share + NORM_EPSILON)
    normed = center * inverse
    return normed * gain + shift, normed, inverse


def norm_columns_back(grad, normed, inverse, gain):
    share = 1.0 / grad.shape[0]
    scaled = grad * gain
    mean = jnp.sum(scaled, axis=0, keepdims=True) * share
    along = jnp.sum(scaled * normed, axis=0, keepdims=True) * share
    return inverse * (scaled - mean - normed * along)


def gelu_and_slope(u):
    d = 1.0 + (0.3275911 * 0.5**0.5) * jnp.abs(u)
    t = pl.reciprocal(d, approx=True)
    t = t * (2.0 - d * t)
    poly = t * (0.127414796 + t * (-0.142248368 + t * (0.7107068705 + t * (-0.7265760135 + t * 0.5307027145))))
    bell = jnp.exp2(u * u * (-0.5 * math.log2(math.e)))
    tail = poly * bell
    phi = jnp.where(u >= 0.0, 1.0 - tail, tail)
    return u * phi, phi + u * bell * (0.5 / math.pi) ** 0.5


def forward_kernel(
    nqs, qlen, plen, xq, xp, attn, w_in, w_out, gains, biases, lists, counts,
    x_out, qk_out, v_out, p_out, ctx_out, n1_out, first_out, slope_out, act_out, n2_out, inv_out, live_out, pooled_out, units_out,
    wproj, wo_t, win_t, wout_t, bias_bc, gain_bc, qblk, xs, away, score_s, turn,
):
    i = pl.program_id(0)
    last = pl.num_programs(0) - 1
    is_q = i < nqs
    t = jnp.where(is_q, 0, 1)
    d = xs.shape[1]
    ff = win_t.shape[0]
    heads = d // HEAD
    segs = TOK // HEAD
    span = GROUP * TOK

    @pl.when(i == 0)
    def _():
        qblk[...] = jnp.zeros_like(qblk)

    @pl.when((i == 0) | (i == nqs))
    def _():
        eye = (lax.broadcasted_iota(jnp.int32, (d, d), 0) == lax.broadcasted_iota(jnp.int32, (d, d), 1)).astype(F32).astype(BF16)
        for j in range(3):
            wproj[j * d : (j + 1) * d, :] = mm_nt(eye, attn[0, j].astype(BF16)).astype(BF16)
        wproj[3 * d : 4 * d, :] = eye
        wproj[4 * d : 5 * d, :] = attn[0, 1].astype(BF16)
        wproj[5 * d : 6 * d, :] = attn[0, 2].astype(BF16)
        wo_t[...] = mm_nt(eye, attn[0, 3].astype(BF16)).astype(BF16)
        for c in range(ff // d):
            at = slice(c * d, (c + 1) * d)
            win_t[at, :] = mm_nt(eye, w_in[0, :, at].astype(BF16)).astype(BF16)
            wout_t[:, at] = mm_nt(eye, w_out[0, at, :].astype(BF16)).astype(BF16)
        for c in range(bias_bc.shape[0] // d):
            row = biases[pl.ds(t, 1), c * d : (c + 1) * d]
            bias_bc[c * d : (c + 1) * d, :] = jnp.broadcast_to(row, (128, d)).T
        for c in range(2):
            row = gains[t, c : c + 1, :]
            gain_bc[c * d : (c + 1) * d, :] = jnp.broadcast_to(row, (128, d)).T

    @pl.when(is_q)
    def _():
        xs[...] = xq[...].reshape(span, d)

    @pl.when(jnp.logical_not(is_q))
    def _():
        xs[...] = xp[...].reshape(span, d)

    def length_of(u, segment):
        base = (jnp.minimum(i, nqs - 1) * GROUP + u) * segs
        out = jnp.full(segment.shape, qlen[base + segs - 1], jnp.int32)
        for s in range(segs - 1):
            out = jnp.where(segment == s, qlen[base + s], out)
        return jnp.where(is_q, out, plen[jnp.maximum(i - nqs, 0) * GROUP + u])

    key = lax.broadcasted_iota(jnp.int32, (TOK, TOK), 0)
    ask = lax.broadcasted_iota(jnp.int32, (TOK, TOK), 1)
    row = lax.broadcasted_iota(jnp.int32, (16, TOK), 0)
    token = lax.broadcasted_iota(jnp.int32, (16, TOK), 1)
    key_col = lax.broadcasted_iota(jnp.int32, (TOK, 1), 0)
    far = is_q & ((key // HEAD) != (ask // HEAD))
    owner = jnp.where(is_q, token // HEAD, 0)
    place = jnp.where(is_q, token % HEAD, token)
    seg_row = lax.broadcasted_iota(jnp.int32, (16, 1), 0)
    for u in range(GROUP):
        dead = jnp.where(is_q, key_col % HEAD, key_col) >= length_of(u, key_col // HEAD)
        away[u] = jnp.where(far | dead, MASKED_SCORE, 0.0)
        live = ((place < length_of(u, token // HEAD)) & (row == owner)).astype(F32)
        live_out[0, :, u * TOK : (u + 1) * TOK] = live.astype(BF16)

    def bias(at, size):
        return wide(bias_bc[at : at + size, :])

    x = xs[...]
    q_t = (mm_nt(wproj[0:d, :], x) + bias(0, d)).astype(BF16)
    qk_out[0, 0:d, :] = q_t
    for u in range(GROUP):
        for h in range(heads):
            piece = q_t[h * HEAD : (h + 1) * HEAD, u * TOK : (u + 1) * TOK]
            qblk[u, h * HEAD : (h + 1) * HEAD, h * TOK : (h + 1) * TOK] = piece * BF16(HEAD**-0.5)
    k_row = mm(x, wproj[4 * d : 5 * d, :]).astype(BF16)
    for u in range(GROUP):
        for h in range(heads):
            score_s[u, h] = mm(k_row[u * TOK : (u + 1) * TOK, :], qblk[u, :, h * TOK : (h + 1) * TOK])
    v_t = (mm_nt(wproj[2 * d : 3 * d, :], x) + bias(d, d)).astype(BF16)
    qk_out[0, d : 2 * d, :] = mm_nt(wproj[d : 2 * d, :], x).astype(BF16)
    v_out[0] = (mm(x, wproj[5 * d : 6 * d, :]) + biases[pl.ds(t, 1), d : 2 * d]).astype(BF16)
    x_t = mm_nt(wproj[3 * d : 4 * d, :], x)
    x_out[0, 0:d, :] = x_t.astype(BF16)
    for u in range(GROUP):
        for h in range(heads):
            scores = score_s[u, h] + away[u]
            exponent = jnp.exp(scores - jnp.max(scores, axis=0, keepdims=True))
            probs = exponent * (1.0 / jnp.sum(exponent, axis=0, keepdims=True))
            p_out[0, u, h] = probs.astype(BF16)
    for u in range(GROUP):
        for h in range(heads):
            at = slice(h * HEAD, (h + 1) * HEAD)
            over = slice(u * TOK, (u + 1) * TOK)
            ctx_out[0, at, over] = mm(v_t[at, over], p_out[0, u, h]).astype(BF16)
    hidden = x_t + (mm(wo_t[...], ctx_out[0, 0:d, :]) + bias(2 * d, d))
    first, n1, inv1 = norm_columns(hidden, wide(gain_bc[0:d, :]), bias(3 * d, d))
    n1_out[0] = n1
    first_low = first.astype(BF16)
    first_out[0, 0:d, :] = first_low
    hidden = first + bias(4 * d, d)
    for c in range(ff // d):
        at = slice(c * d, (c + 1) * d)
        upper = mm(win_t[at, :], first_low) + bias(6 * d + c * d, d)
        active, slope = gelu_and_slope(upper)
        slope_out[0, at, :] = slope
        active_low = active.astype(BF16)
        act_out[0, at, :] = active_low
        hidden = hidden + mm(wout_t[:, at], active_low)
    second, n2, inv2 = norm_columns(hidden, wide(gain_bc[d : 2 * d, :]), bias(5 * d, d))
    n2_out[0] = n2
    which = lax.broadcasted_iota(jnp.int32, (8, span), 0)
    inv_out[0] = jnp.where(which == 0, inv1, inv2)
    second_high, second_low = split_two(second)
    ones = jnp.ones((ONES, span), BF16)
    x_out[0, d:, :] = ones
    ctx_out[0, d:, :] = ones
    first_out[0, d:, :] = ones
    act_out[0, ff:, :] = ones
    for u in range(GROUP):
        over = slice(u * TOK, (u + 1) * TOK)
        live = live_out[0, :, over]
        pooled = mm_nt(live, second_high[:, over]) + mm_nt(live, second_low[:, over])
        pooled = pooled / length_of(u, seg_row).astype(F32)

        @pl.when(is_q)
        def _(pooled=pooled, u=u):
            for s in range(segs):
                pooled_out[pl.ds((i * GROUP + u) * segs + s, 1), :] = pooled[s : s + 1, :]

        @pl.when(jnp.logical_not(is_q))
        def _(pooled=pooled, u=u):
            pooled_out[pl.ds(nqs * GROUP * segs + (i - nqs) * GROUP + u, 1), :] = pooled[0:1, :]

    @pl.when(i == last)
    def _():
        rows = pooled_out[...]
        unit = rows * lax.rsqrt(jnp.sum(rows * rows, axis=1, keepdims=True) + UNIT_EPSILON)
        slots, own = lists.shape
        turn[...] = jnp.zeros_like(turn)
        turn[0:slots, 0:own] = (lists[...] // PART).astype(F32)
        turn[slots : 2 * slots, 0:own] = (lists[...] % PART).astype(F32)
        turn[2 * slots : 2 * slots + 1, 0:own] = counts[...].astype(F32)
        extra = turn[...].T[0:own, :]
        sent = jnp.concatenate([unit[:, c * 128 : (c + 1) * 128] for c in range(d // 128)] + [extra], axis=0)
        units_out[...] = jnp.broadcast_to(sent.astype(BF16)[None], units_out.shape)


def step_spec(*shape):
    return pl.BlockSpec((1,) + shape, lambda i, *_: (i,) + (0,) * len(shape))


def tower_spec(nqs, *shape):
    return pl.BlockSpec((1,) + shape, lambda i, *_: (jnp.where(i < nqs, 0, 1),) + (0,) * len(shape))


def whole_spec(*shape):
    return pl.BlockSpec(shape, lambda i, *_: (0,) * len(shape))


def forward(devices, q_lengths, p_lengths, xq, xp, attn, w_in, w_out, gains, biases, positives, counts):
    nqs, nps = xq.shape[0] // GROUP, xp.shape[0] // GROUP
    steps = nqs + nps
    span = GROUP * TOK
    d, ff = w_in.shape[1:]
    heads = d // HEAD
    seqs = q_lengths.shape[0] + xp.shape[0]
    sent = seqs * d // 128 + positives.shape[1]
    outs = [
        ((d + ONES, span), BF16),
        ((2 * d, span), BF16),
        ((span, d), BF16),
        ((GROUP, heads, TOK, TOK), BF16),
        ((d + ONES, span), BF16),
        ((d, span), F32),
        ((d + ONES, span), BF16),
        ((ff, span), F32),
        ((ff + ONES, span), BF16),
        ((d, span), F32),
        ((8, span), F32),
        ((16, span), BF16),
    ]
    return pl.pallas_call(
        functools.partial(forward_kernel, nqs),
        grid_spec=pltpu.PrefetchScalarGridSpec(
            num_scalar_prefetch=2,
            grid=(steps,),
            in_specs=[
                pl.BlockSpec((GROUP, TOK, d), lambda i, *_: (jnp.minimum(i, nqs - 1), 0, 0)),
                pl.BlockSpec((GROUP, TOK, d), lambda i, *_: (jnp.maximum(i - nqs, 0), 0, 0)),
                tower_spec(nqs, 4, d, d),
                tower_spec(nqs, d, ff),
                tower_spec(nqs, ff, d),
                whole_spec(2, 2, d),
                whole_spec(2, biases.shape[1]),
                whole_spec(*positives.shape),
                whole_spec(1, positives.shape[1]),
            ],
            out_specs=[step_spec(*shape) for shape, _ in outs] + [whole_spec(seqs, d), whole_spec(devices, sent, 128)],
            scratch_shapes=[
                pltpu.VMEM((6 * d, d), BF16),
                pltpu.VMEM((d, d), BF16),
                pltpu.VMEM((ff, d), BF16),
                pltpu.VMEM((d, ff), BF16),
                pltpu.VMEM((biases.shape[1], 128), F32),
                pltpu.VMEM((2 * d, 128), F32),
                pltpu.VMEM((GROUP, d, heads * TOK), BF16),
                pltpu.VMEM((span, d), BF16),
                pltpu.VMEM((GROUP, TOK, TOK), F32),
                pltpu.VMEM((GROUP, heads, TOK, TOK), F32),
                pltpu.VMEM((128, 128), F32),
            ],
        ),
        out_shape=[jax.ShapeDtypeStruct((steps,) + shape, kind) for shape, kind in outs]
        + [jax.ShapeDtypeStruct((seqs, d), F32), jax.ShapeDtypeStruct((devices, sent, 128), BF16)],
        compiler_params=pltpu.CompilerParams(vmem_limit_bytes=VMEM_LIMIT),
        name="forward",
    )(q_lengths, p_lengths, xq, xp, attn, w_in, w_out, gains, biases, positives, counts)


def contrast_kernel(nqu, slots, index, qlen, plen, units, pooled, loss_out, gp_out, low_rows, gup_rows, gp_rows, turn):
    devices = units.shape[0]
    seqs, d = pooled.shape
    own = qlen.shape[0]
    mine = pl.multiple_of(index[0] * own, own)
    pown = seqs - own
    pmine = pl.multiple_of(index[0] * pown, pown)
    both = units[...].astype(F32)
    parts = range(0, seqs * d // 128, seqs)
    uq = jnp.concatenate([both[:, at : at + own, :] for at in parts], axis=2).reshape(devices * own, d).astype(BF16)
    up = jnp.concatenate([both[:, at + own : at + seqs, :] for at in parts], axis=2).reshape(devices * pown, d).astype(BF16)
    lists = both[:, seqs * d // 128 :, :].reshape(devices * own, 128)
    scores = SCORE_SCALE * mm_nt(uq, up)
    columns = lax.broadcasted_iota(jnp.int32, scores.shape, 1).astype(F32)
    positive = None
    for k in range(slots):
        listed = lists[:, k : k + 1] * PART + lists[:, slots + k : slots + k + 1]
        hit = (listed == columns) & (lists[:, 2 * slots : 2 * slots + 1] > k)
        positive = hit if positive is None else positive | hit
    highest = jnp.max(scores, axis=1, keepdims=True)
    whole = highest + jnp.log(jnp.sum(jnp.exp(scores - highest), axis=1, keepdims=True))
    chosen = jnp.where(positive, scores, MASKED_SCORE)
    top = jnp.max(chosen, axis=1, keepdims=True)
    within = top + jnp.log(jnp.sum(jnp.exp(chosen - top), axis=1, keepdims=True))
    low = (SCORE_SCALE * (jnp.exp(scores - whole) - jnp.exp(chosen - within))).astype(BF16)
    low_rows[:, : scores.shape[1]] = low.astype(F32)
    low_rows[:, scores.shape[1] :] = jnp.broadcast_to(whole - within, (scores.shape[0], 128))
    turn[...] = jnp.zeros_like(turn)
    turn[0:own, :] = low_rows[pl.ds(mine, own), scores.shape[1] :]
    loss_out[...] = turn[...].T[0:1, 0:own]
    grad_q = mm(low_rows[pl.ds(mine, own), : scores.shape[1]].astype(BF16), up)
    gup_rows[...] = mm_tn(low, uq)
    grad_p = gup_rows[pl.ds(pmine, pown), :]
    grad = jnp.concatenate([grad_q, grad_p], axis=0)
    rows = pooled[...]
    inverse = lax.rsqrt(jnp.sum(rows * rows, axis=1, keepdims=True) + UNIT_EPSILON)
    grad = inverse * grad - inverse * inverse * inverse * rows * jnp.sum(rows * grad, axis=1, keepdims=True)
    segs = own // nqu
    gp_rows[...] = jnp.zeros_like(gp_rows)
    for s in range(own):
        gp_rows[s // segs, s % segs : s % segs + 1, :] = grad[s : s + 1, :] / jnp.full((1, d), qlen[s], jnp.int32).astype(F32)
    for s in range(pown):
        gp_rows[nqu + s, 0:1, :] = grad[own + s : own + s + 1, :] / jnp.full((1, d), plen[s], jnp.int32).astype(F32)
    for term, value in enumerate(split_three(gp_rows[...])):
        gp_out[:, term * 16 : (term + 1) * 16, :] = value


def contrast(nqu, npu, slots, index, q_lengths, p_lengths, units, pooled):
    devices = units.shape[0]
    seqs, d = pooled.shape
    own = q_lengths.shape[0]
    passages = devices * (seqs - own)
    vmem = pl.BlockSpec(memory_space=pltpu.VMEM)
    return pl.pallas_call(
        functools.partial(contrast_kernel, nqu, slots),
        in_specs=[pl.BlockSpec(memory_space=pltpu.SMEM)] * 3 + [vmem, vmem],
        out_specs=[vmem, vmem],
        out_shape=[jax.ShapeDtypeStruct((1, own), F32), jax.ShapeDtypeStruct((nqu + npu, 48, d), BF16)],
        scratch_shapes=[
            pltpu.VMEM((devices * own, passages + 128), F32),
            pltpu.VMEM((passages, d), F32),
            pltpu.VMEM((nqu + npu, 16, d), F32),
            pltpu.VMEM((128, 128), F32),
        ],
        compiler_params=pltpu.CompilerParams(vmem_limit_bytes=VMEM_LIMIT),
        name="contrast",
    )(index, q_lengths, p_lengths, units, pooled)


def left_rows(start_t, matrix):
    s_high, s_low = split_two(start_t)
    m_high, m_low = split_two(matrix)
    both = mm_nt(jnp.concatenate([s_high, s_low], axis=0), m_high)
    return both[:8] + both[8:] + mm_nt(jnp.concatenate([s_high, s_high], axis=0), m_low)[:8]


def right_rows(basis, matrix):
    b_high, b_low = split_two(basis)
    m_high, m_low = split_two(matrix)
    both = mm(jnp.concatenate([b_high, b_low], axis=0), m_high)
    return both[:8] + both[8:] + mm(jnp.concatenate([b_high, b_high], axis=0), m_low)[:8]


def core_of(index, outer):
    return (index[0] // outer) % 2


def part_halves(core, whole, mine, other):
    half = whole.shape[1] // 2
    for c in range(2):

        @pl.when(core == c)
        def _(c=c):
            mine[...] = whole[:, c * half : (c + 1) * half]
            other[...] = whole[:, (1 - c) * half : (2 - c) * half]


def join_halves(core, whole, mine, other):
    half = whole.shape[1] // 2
    for c in range(2):

        @pl.when(core == c)
        def _(c=c):
            whole[:, c * half : (c + 1) * half] = mine[...]
            whole[:, (1 - c) * half : (2 - c) * half] = other[...]


def backward_kernel(
    nqs, outer, index, gp, x_in, qk_in, v_in, p_in, ctx_in, n1_in, first_in, slope_in, act_in, n2_in, inv_in, live_in,
    attn, w_in, w_out, gains, attn_err, in_err, out_err, attn_start, in_start, out_start,
    qgrad, pgrad, attn_m, in_m, out_m, left_mine, left_other,
    left, wqkv, wo, win, wout, gain_bc, gz, gp_s, graw_s, gqkv, acc_qkv, acc_o, acc_in, acc_out, acc_gain,
):
    i = pl.program_id(0)
    last = pl.num_programs(0) - 1
    is_q = i < nqs
    t = jnp.where(is_q, 0, 1)
    d = wo.shape[0]
    ff = wout.shape[0]
    heads = d // HEAD
    span = GROUP * TOK

    @pl.when(i == 0)
    def _():
        gz[...] = jnp.zeros_like(gz)

    @pl.when((i == 0) | (i == nqs))
    def _():
        for j in range(3):
            wqkv[:, j * d : (j + 1) * d] = attn[0, j].astype(BF16)
        wo[...] = attn[0, 3].astype(BF16)
        win[...] = w_in[0].astype(BF16)
        wout[...] = w_out[0].astype(BF16)
        for c in range(2):
            row = gains[t, c : c + 1, :]
            gain_bc[c * d : (c + 1) * d, :] = jnp.broadcast_to(row, (128, d)).T
        acc_qkv[...] = jnp.zeros_like(acc_qkv)
        acc_o[...] = jnp.zeros_like(acc_o)
        acc_in[...] = jnp.zeros_like(acc_in)
        acc_out[...] = jnp.zeros_like(acc_out)
        acc_gain[...] = jnp.zeros_like(acc_gain)

    def add_gain(at, value):
        total = value[:, :128]
        for c in range(1, span // 128):
            total = total + value[:, c * 128 : (c + 1) * 128]
        acc_gain[at * d : (at + 1) * d, :] += total

    pieces = []
    for u in range(GROUP):
        live = live_in[0, :, u * TOK : (u + 1) * TOK]
        pieces.append(mm_tn(gp[u], jnp.concatenate([live, live, live], axis=0)))
    grad_second = jnp.concatenate(pieces, axis=1)
    n2 = n2_in[0]
    grad_two = norm_columns_back(grad_second, n2, inv_in[0, 1:2, :], wide(gain_bc[d : 2 * d, :]))
    down_low = grad_two.astype(BF16)
    grad_first = grad_two
    for c in range(ff // d):
        at = slice(c * d, (c + 1) * d)
        up_low = (mm(wout[at, :], down_low) * slope_in[0, at, :]).astype(BF16)
        acc_in[:, at] += mm_nt(first_in[0], up_low)
        grad_first = grad_first + mm(win[:, at], up_low)
    add_gain(1, grad_second * n2)
    add_gain(3, grad_second)
    n1 = n1_in[0]
    grad_one = norm_columns_back(grad_first, n1, inv_in[0, 0:1, :], wide(gain_bc[0:d, :]))
    branch_low = grad_one.astype(BF16)
    grad_context = mm(wo[...], branch_low).astype(BF16)
    for u in range(GROUP):
        for h in range(heads):
            at = slice(h * HEAD, (h + 1) * HEAD)
            gz[u, at, h * TOK : (h + 1) * TOK] = grad_context[at, u * TOK : (u + 1) * TOK]
    for u in range(GROUP):
        for h in range(heads):
            gp_s[u, h] = mm(v_in[0, u * TOK : (u + 1) * TOK, :], gz[u, :, h * TOK : (h + 1) * TOK])
    acc_out[...] += mm_nt(act_in[0], down_low)
    add_gain(0, grad_first * n1)
    add_gain(2, grad_first)
    acc_o[...] += mm_nt(ctx_in[0], branch_low)
    for u in range(GROUP):
        for h in range(heads):
            probs = p_in[0, u, h].astype(F32)
            grad_probs = gp_s[u, h]
            inner = jnp.sum(grad_probs * probs, axis=0, keepdims=True)
            graw_s[u, h] = (probs * (grad_probs - inner) * HEAD**-0.5).astype(BF16)
    for u in range(GROUP):
        over = slice(u * TOK, (u + 1) * TOK)
        for h in range(heads):
            at = slice(h * HEAD, (h + 1) * HEAD)
            later = slice(d + h * HEAD, d + (h + 1) * HEAD)
            last_at = slice(2 * d + h * HEAD, 2 * d + (h + 1) * HEAD)
            gqkv[last_at, over] = mm_nt(grad_context[at, over], p_in[0, u, h]).astype(BF16)
            gqkv[at, over] = mm(qk_in[0, later, over], graw_s[u, h]).astype(BF16)
            gqkv[later, over] = mm_nt(qk_in[0, at, over], graw_s[u, h]).astype(BF16)
    acc_qkv[...] += mm_nt(x_in[0], gqkv[...])
    result = (grad_one + mm(wqkv[...], gqkv[...])).T.reshape(GROUP, TOK, d)

    @pl.when(is_q)
    def _():
        qgrad[...] = result

    @pl.when(jnp.logical_not(is_q))
    def _():
        pgrad[...] = result

    @pl.when((i == nqs - 1) | (i == last))
    def _():
        base_in = 8 * d
        base_out = base_in + 2 * d
        base_vec = base_out + 2 * ff
        for j in range(4):
            grad = acc_o[0:d, :] if j == 3 else acc_qkv[0:d, j * d : (j + 1) * d]
            merged = grad + attn_err[0, 0, j]
            attn_m[0, j] = merged
            left[:, pl.ds(pl.multiple_of((t * 4 + j) * d, 128), d)] = left_rows(attn_start[0, j], merged)
        merged = acc_in[0:d, :] + in_err[0, 0]
        in_m[0] = merged
        left[:, pl.ds(pl.multiple_of(base_in + t * d, 128), d)] = left_rows(in_start[0], merged)
        merged = acc_out[0:ff, :] + out_err[0, 0]
        out_m[0] = merged
        left[:, pl.ds(pl.multiple_of(base_out + t * ff, 128), ff)] = left_rows(out_start[0], merged)
        sums = mm_nt(jnp.ones((8, 128), F32), acc_gain[...], HIGHEST)

        def vectors():
            yield sums[0:1, 0:d]
            yield sums[0:1, d : 2 * d]
            yield acc_qkv[d : d + 1, 0:d]
            yield acc_qkv[d : d + 1, 2 * d : 3 * d]
            yield acc_o[d : d + 1, :]
            yield sums[0:1, 2 * d : 3 * d]
            yield acc_out[ff : ff + 1, :]
            yield sums[0:1, 3 * d : 4 * d]
            for c in range(ff // d):
                yield acc_in[d : d + 1, c * d : (c + 1) * d]

        for tower in range(2):

            @pl.when(t == tower)
            def _(tower=tower):
                for v, vector in enumerate(vectors()):
                    at = tower * 12 + v
                    left[at // 3 : at // 3 + 1, base_vec + (at % 3) * d : base_vec + (at % 3 + 1) * d] = vector

    @pl.when(i == last)
    def _():
        part_halves(core_of(index, outer), left, left_mine, left_other)


def backward(nqs, nps, outer, index, gp, saved, attn, w_in, w_out, gains, attn_err, in_err, out_err, starts):
    steps = nqs + nps
    nqu, npu = nqs * GROUP, nps * GROUP
    span = GROUP * TOK
    d, ff = w_in.shape[1:]
    heads = d // HEAD
    width = 8 * d + 2 * d + 2 * ff + 3 * d
    tower = functools.partial(tower_spec, nqs)

    def error_spec(*shape):
        return pl.BlockSpec((1, 1) + shape, lambda i: (0, jnp.where(i < nqs, 0, 1)) + (0,) * len(shape))

    return pl.pallas_call(
        functools.partial(backward_kernel, nqs, outer),
        grid=(steps,),
        in_specs=[pl.BlockSpec(memory_space=pltpu.SMEM), pl.BlockSpec((GROUP, 48, d), lambda i: (i, 0, 0))]
        + [step_spec(*array.shape[1:]) for array in saved]
        + [tower(4, d, d), tower(d, ff), tower(ff, d), whole_spec(2, 2, d)]
        + [error_spec(4, d, d), error_spec(d, ff), error_spec(ff, d)]
        + [tower(4, 8, d), tower(8, ff), tower(8, d)],
        out_specs=[
            pl.BlockSpec((GROUP, TOK, d), lambda i: (jnp.minimum(i, nqs - 1), 0, 0)),
            pl.BlockSpec((GROUP, TOK, d), lambda i: (jnp.maximum(i - nqs, 0), 0, 0)),
            tower(4, d, d),
            tower(d, ff),
            tower(ff, d),
            whole_spec(8, width // 2),
            whole_spec(8, width // 2),
        ],
        out_shape=[
            jax.ShapeDtypeStruct((nqu, TOK, d), F32),
            jax.ShapeDtypeStruct((npu, TOK, d), F32),
            jax.ShapeDtypeStruct((2, 4, d, d), F32),
            jax.ShapeDtypeStruct((2, d, ff), F32),
            jax.ShapeDtypeStruct((2, ff, d), F32),
            jax.ShapeDtypeStruct((8, width // 2), F32),
            jax.ShapeDtypeStruct((8, width // 2), F32),
        ],
        scratch_shapes=[
            pltpu.VMEM((8, width), F32),
            pltpu.VMEM((d, 3 * d), BF16),
            pltpu.VMEM((d, d), BF16),
            pltpu.VMEM((d, ff), BF16),
            pltpu.VMEM((ff, d), BF16),
            pltpu.VMEM((2 * d, 128), F32),
            pltpu.VMEM((GROUP, d, heads * TOK), BF16),
            pltpu.VMEM((GROUP, heads, TOK, TOK), F32),
            pltpu.VMEM((GROUP, heads, TOK, TOK), BF16),
            pltpu.VMEM((3 * d, span), BF16),
            pltpu.VMEM((d + ONES, 3 * d), F32),
            pltpu.VMEM((d + ONES, d), F32),
            pltpu.VMEM((d + ONES, ff), F32),
            pltpu.VMEM((ff + ONES, d), F32),
            pltpu.VMEM((4 * d, 128), F32),
        ],
        compiler_params=pltpu.CompilerParams(vmem_limit_bytes=VMEM_LIMIT),
        name="backward",
    )(index, gp, *saved, attn, w_in, w_out, gains, attn_err, in_err, out_err, *starts)


def right_kernel(outer, index, left_mine, left_other, attn_m, in_m, out_m, basis, right_mine, right_other, vector, left, right):
    d, ff = in_m.shape[1:]
    core = core_of(index, outer)
    join_halves(core, left, left_mine, left_other)
    vector[...] = left[:, 10 * d + 2 * ff :]
    places = [(j * d, d) for j in range(8)] + [(8 * d + t * d, d) for t in range(2)] + [(10 * d + t * ff, ff) for t in range(2)]
    blocks = [left[:, at : at + size] for at, size in places]
    for j in range(8):
        for b, block in enumerate(blocks):
            order = lax.broadcasted_iota(jnp.int32, (8, 1), 0)
            column = block[j : j + 1, :]
            dots = jnp.sum(block * column, axis=1, keepdims=True)
            scale = lax.rsqrt(dots[j : j + 1, :] + 1e-06)
            unit = column * scale
            step = jnp.where(order > j, dots * scale, 0.0)
            blocks[b] = jnp.where(order == j, unit, block - step * unit)
    for (at, size), block in zip(places, blocks):
        basis[:, at : at + size] = block
    for j in range(8):
        right[:, j * d : (j + 1) * d] = right_rows(blocks[j], attn_m[j // 4, j % 4])
    for t in range(2):
        right[:, 8 * d + t * ff : 8 * d + (t + 1) * ff] = right_rows(blocks[8 + t], in_m[t])
        right[:, 8 * d + 2 * ff + t * d : 8 * d + 2 * ff + (t + 1) * d] = right_rows(blocks[10 + t], out_m[t])
    part_halves(core, right, right_mine, right_other)


def right_factors(outer, index, left_mine, left_other, attn_m, in_m, out_m):
    d, ff = in_m.shape[1:]
    vmem = pl.BlockSpec(memory_space=pltpu.VMEM)
    width = 10 * d + 2 * ff
    rows = functools.partial(jax.ShapeDtypeStruct, dtype=F32)
    return pl.pallas_call(
        functools.partial(right_kernel, outer),
        in_specs=[pl.BlockSpec(memory_space=pltpu.SMEM)] + [vmem] * 5,
        out_specs=[vmem] * 4,
        out_shape=[rows((8, width)), rows((8, width // 2)), rows((8, width // 2)), rows((8, 3 * d))],
        scratch_shapes=[pltpu.VMEM((8, width + 3 * d), F32), pltpu.VMEM((8, width), F32)],
        compiler_params=pltpu.CompilerParams(vmem_limit_bytes=VMEM_LIMIT),
        name="right",
    )(index, left_mine, left_other, attn_m, in_m, out_m)


def update_kernel(
    replicas, outer, index, basis, right_mine, right_other, vector, gains, biases, gain_mom, bias_mom,
    attn_m, in_m, out_m, attn, w_in, w_out, attn_mom, in_mom, out_mom,
    attn_new, in_new, out_new, attn_mom_new, in_mom_new, out_mom_new, attn_err, in_err, out_err,
    gains_new, biases_new, gain_mom_new, bias_mom_new, attn_factor, in_factor, out_factor, norm_out,
    right, clip_s,
):
    i = pl.program_id(0)
    d = attn.shape[2]
    ff = (right.shape[1] - 10 * d) // 2
    t, c = i // 4, i % 4

    @pl.when(i == 0)
    def _():
        join_halves(core_of(index, outer), right, right_mine, right_other)
        for j in range(8):
            attn_factor[j // 4, j % 4] = right[:, j * d : (j + 1) * d]
        for s in range(2):
            in_factor[s] = right[:, 8 * d + s * ff : 8 * d + (s + 1) * ff]
            out_factor[s] = right[:, 8 * d + 2 * ff + s * d : 8 * d + 2 * ff + (s + 1) * d]
        places = [((j * d, d), (j * d, d)) for j in range(8)]
        places += [((8 * d + s * d, d), (8 * d + s * ff, ff)) for s in range(2)]
        places += [((10 * d + s * ff, ff), (8 * d + 2 * ff + s * d, d)) for s in range(2)]
        total = jnp.zeros((8, 8), F32)
        for (b_at, b_size), (r_at, r_size) in places:
            b = basis[:, b_at : b_at + b_size]
            r = right[:, r_at : r_at + r_size]
            total = total + mm_nt(b, b, HIGHEST) * mm_nt(r, r, HIGHEST)
        sums = vector[...]
        square = jnp.sum(jnp.sum(total, axis=1, keepdims=True), axis=0, keepdims=True)
        square = square + jnp.sum(jnp.sum(sums * sums, axis=1, keepdims=True), axis=0, keepdims=True)
        norm = jnp.sqrt(jnp.broadcast_to(square, (8, 128)))
        norm_out[0] = norm[0, 0]
        clip_s[...] = jnp.minimum(1.0, CLIP_NORM / norm)
        held = clip_s[0:1, 0:1]
        for s in range(2):
            for v in range(12):
                at = s * 12 + v
                reduced = vector[at // 3 : at // 3 + 1, (at % 3) * d : (at % 3 + 1) * d]
                if v < 2:
                    moved = MOMENTUM_DECAY * gain_mom[s, v : v + 1, :] + held * reduced
                    gain_mom_new[s, v : v + 1, :] = moved
                    gains_new[s, v : v + 1, :] = gains[s, v : v + 1, :] - LEARNING_RATE * moved
                else:
                    over = slice((v - 2) * d, (v - 1) * d)
                    moved = MOMENTUM_DECAY * bias_mom[s : s + 1, over] + held * reduced
                    bias_mom_new[s : s + 1, over] = moved
                    biases_new[s : s + 1, over] = biases[s : s + 1, over] - LEARNING_RATE * moved

    clip = clip_s[0:1, 0:1]

    def step(b_at, r_at, merged, weight, moment, weight_new, moment_new, error):
        b1, b2, b3 = split_three(basis[:, pl.ds(pl.multiple_of(b_at, 128), d)])
        r1, r2, r3 = split_three(right[:, pl.ds(pl.multiple_of(r_at, 128), d)])
        approx = mm_tn(jnp.concatenate([b1, b1, b2, b1, b2, b3], axis=0), jnp.concatenate([r1, r2, r1, r3, r2, r1], axis=0))
        moved = MOMENTUM_DECAY * moment + clip * approx
        moment_new[...] = moved.reshape(moment_new.shape)
        weight_new[...] = (weight - LEARNING_RATE * moved).reshape(weight_new.shape)
        error[...] = (merged - approx * (1.0 / replicas)).reshape(error.shape)

    step(i * d, i * d, attn_m[0, 0], attn[0, 0], attn_mom[0, 0], attn_new, attn_mom_new, attn_err)
    step((8 + t) * d, 8 * d + t * ff + c * d, in_m[0], w_in[0], in_mom[0], in_new, in_mom_new, in_err)
    step(10 * d + t * ff + c * d, 8 * d + 2 * ff + t * d, out_m[0], w_out[0], out_mom[0], out_new, out_mom_new, out_err)


def update(replicas, outer, index, basis, right_mine, right_other, vector, gains, biases, gain_mom, bias_mom, merged, weights, moments):
    d, ff = weights[1].shape[1:]
    a_spec = pl.BlockSpec((1, 1, d, d), lambda i: (i // 4, i % 4, 0, 0))
    i_spec = pl.BlockSpec((1, d, d), lambda i: (i // 4, 0, i % 4))
    o_spec = pl.BlockSpec((1, d, d), lambda i: (i // 4, i % 4, 0))
    ae_spec = pl.BlockSpec((1, 1, 1, d, d), lambda i: (0, i // 4, i % 4, 0, 0))
    ie_spec = pl.BlockSpec((1, 1, d, d), lambda i: (0, i // 4, 0, i % 4))
    oe_spec = pl.BlockSpec((1, 1, d, d), lambda i: (0, i // 4, i % 4, 0))
    rows = functools.partial(jax.ShapeDtypeStruct, dtype=F32)
    small = (basis, right_mine, right_other, vector, gains, biases, gain_mom, bias_mom)
    finals = [gains.shape, biases.shape] * 2 + [(2, 4, 8, d), (2, 8, ff), (2, 8, d)]
    return pl.pallas_call(
        functools.partial(update_kernel, replicas, outer),
        grid=(8,),
        in_specs=[pl.BlockSpec(memory_space=pltpu.SMEM)] + [whole_spec(*a.shape) for a in small] + [a_spec, i_spec, o_spec] * 3,
        out_specs=[a_spec, i_spec, o_spec] * 2
        + [ae_spec, ie_spec, oe_spec]
        + [whole_spec(*shape) for shape in finals]
        + [pl.BlockSpec(memory_space=pltpu.SMEM)],
        out_shape=[rows(a.shape) for a in weights * 2]
        + [rows((1,) + a.shape) for a in weights]
        + [rows(shape) for shape in finals]
        + [rows((1,))],
        scratch_shapes=[pltpu.VMEM(basis.shape, F32), pltpu.VMEM((8, 128), F32)],
        compiler_params=pltpu.CompilerParams(vmem_limit_bytes=VMEM_LIMIT),
        name="update",
    )(index, *small, *merged, *weights, *moments)


def swap_with(x, axis, mask):
    return lax.ppermute(x, axis, [(i, i ^ mask) for i in range(lax.axis_size(axis))])


def sum_halves(mine, other):
    mine = mine + swap_with(other, "dp", 1)
    size = lax.axis_size("dp")
    if size == 8:
        steps = [("dp", (2, 4, 6))]
    else:
        steps = [("dp", (1 << b,)) for b in range(1, size.bit_length() - 1)]
    steps.append(("outer", tuple(range(1, lax.axis_size("outer")))))
    for axis, masks in steps:
        sent = mine.astype(SEND)
        for got in [swap_with(sent, axis, mask) for mask in masks]:
            mine = mine + got.astype(F32)
    return mine, swap_with(mine, "dp", 1)


def per_device(
    questions, passages, q_lengths, p_lengths, positives, pos_counts, attn, w_in, w_out, gains, biases, attn_mom, w_in_mom,
    w_out_mom, gain_mom, bias_mom, attn_err, w_in_err, w_out_err, attn_start, w_in_start, w_out_start,
):
    devices = lax.axis_size("dp") * lax.axis_size("outer")
    d, ff = w_in.shape[1:]
    xq = questions.reshape(-1, TOK, d)
    xp = passages.reshape(-1, TOK, d)
    nqu, npu = xq.shape[0], xp.shape[0]
    index = (lax.axis_index("dp") * lax.axis_size("outer") + lax.axis_index("outer")).astype(jnp.int32).reshape(1)
    *saved, pooled, units = forward(
        devices, q_lengths, p_lengths, xq, xp, attn, w_in, w_out, gains, biases, positives.T, pos_counts.reshape(1, -1)
    )
    units = lax.all_to_all(units, AXES, 0, 0)
    loss, gp = contrast(nqu, npu, positives.shape[1], index, q_lengths, p_lengths, units, pooled)
    starts = [jnp.swapaxes(start, -1, -2) for start in (attn_start, w_in_start, w_out_start)]
    outer = lax.axis_size("outer")
    qgrad, pgrad, attn_m, in_m, out_m, *left = backward(
        nqu // GROUP, npu // GROUP, outer, index, gp, saved, attn, w_in, w_out, gains, attn_err, w_in_err, w_out_err, starts
    )
    basis, *right, vector = right_factors(outer, index, *sum_halves(*left), attn_m, in_m, out_m)
    *new, attn_factor, in_factor, out_factor, norm = update(
        devices, outer, index, basis, *sum_halves(*right), vector, gains, biases, gain_mom, bias_mom,
        (attn_m, in_m, out_m), (attn, w_in, w_out), (attn_mom, w_in_mom, w_out_mom),
    )
    weights_new, moments_new, errors_new, vectors_new = new[:3], new[3:6], new[6:9], new[9:]
    factors = [jnp.swapaxes(factor, -1, -2) for factor in (attn_factor, in_factor, out_factor)]
    return (
        loss.reshape(-1), qgrad.reshape(questions.shape), pgrad.reshape(passages.shape),
        *weights_new, *vectors_new[:2], *moments_new, *vectors_new[2:], *errors_new, *factors, norm.reshape(()),
    )


def solution(mesh):
    split = ("dp", "outer")
    share = P(split)
    return jax.shard_map(
        per_device,
        mesh=mesh,
        in_specs=(share,) * 6 + (P(),) * 10 + (share,) * 3 + (P(),) * 3,
        out_specs=(share,) * 3 + (P(),) * 10 + (share,) * 3 + (P(),) * 4,
        check_vma=False,
    )
```

```python
import functools
import math

import jax
import jax.numpy as jnp
from jax import lax
from jax.experimental import pallas as pl
from jax.experimental.pallas import tpu as pltpu
from jax.sharding import PartitionSpec as P

HEAD = 64
TOK = 256
GROUP = 2
PART = 64
ONES = 16

NORM_EPSILON = 1e-06
UNIT_EPSILON = 1e-06
SCORE_SCALE = 20.0
MOMENTUM_DECAY = 0.9
LEARNING_RATE = 10.0
CLIP_NORM = 2.0
MASKED_SCORE = -1e30
HIGHEST = lax.Precision.HIGHEST
AXES = ("dp", "outer")
F32 = jnp.float32
BF16 = jnp.bfloat16
VMEM_LIMIT = 56 << 20
SEND = BF16


def mm(a, b, precision=None):
    return lax.dot_general(a, b, (((1,), (0,)), ((), ())), precision=precision, preferred_element_type=F32)


def mm_nt(a, b, precision=None):
    return lax.dot_general(a, b, (((1,), (1,)), ((), ())), precision=precision, preferred_element_type=F32)


def mm_tn(a, b, precision=None):
    return lax.dot_general(a, b, (((0,), (0,)), ((), ())), precision=precision, preferred_element_type=F32)


def wide(column):
    return jnp.concatenate([column] * (GROUP * TOK // 128), axis=1)


def split_two(v):
    high = v.astype(BF16)
    return high, (v - high.astype(F32)).astype(BF16)


def split_three(v):
    high = v.astype(BF16)
    rest = v - high.astype(F32)
    middle = rest.astype(BF16)
    return high, middle, (rest - middle.astype(F32)).astype(BF16)


def norm_columns(hidden, gain, shift):
    share = 1.0 / hidden.shape[0]
    center = hidden - jnp.sum(hidden, axis=0, keepdims=True) * share
    inverse = lax.rsqrt(jnp.sum(center * center, axis=0, keepdims=True) * share + NORM_EPSILON)
    normed = center * inverse
    return normed * gain + shift, normed, inverse


def norm_columns_back(grad, normed, inverse, gain):
    share = 1.0 / grad.shape[0]
    scaled = grad * gain
    mean = jnp.sum(scaled, axis=0, keepdims=True) * share
    along = jnp.sum(scaled * normed, axis=0, keepdims=True) * share
    return inverse * (scaled - mean - normed * along)


def gelu_and_slope(u):
    d = 1.0 + (0.3275911 * 0.5**0.5) * jnp.abs(u)
    t = pl.reciprocal(d, approx=True)
    t = t * (2.0 - d * t)
    poly = t * (0.127414796 + t * (-0.142248368 + t * (0.7107068705 + t * (-0.7265760135 + t * 0.5307027145))))
    bell = jnp.exp2(u * u * (-0.5 * math.log2(math.e)))
    tail = poly * bell
    phi = jnp.where(u >= 0.0, 1.0 - tail, tail)
    return u * phi, phi + u * bell * (0.5 / math.pi) ** 0.5


def forward_kernel(
    nqs, qlen, plen, xq, xp, attn, w_in, w_out, gains, biases, lists, counts,
    x_out, qk_out, v_out, p_out, ctx_out, n1_out, first_out, slope_out, act_out, n2_out, inv_out, live_out, pooled_out, units_out,
    wproj, wo_t, win_t, wout_t, bias_bc, gain_bc, qblk, xs, away, score_s, turn,
):
    i = pl.program_id(0)
    last = pl.num_programs(0) - 1
    is_q = i < nqs
    t = jnp.where(is_q, 0, 1)
    d = xs.shape[1]
    ff = win_t.shape[0]
    heads = d // HEAD
    segs = TOK // HEAD
    span = GROUP * TOK

    @pl.when(i == 0)
    def _():
        qblk[...] = jnp.zeros_like(qblk)

    @pl.when((i == 0) | (i == nqs))
    def _():
        eye = (lax.broadcasted_iota(jnp.int32, (d, d), 0) == lax.broadcasted_iota(jnp.int32, (d, d), 1)).astype(F32).astype(BF16)
        for j in range(3):
            wproj[j * d : (j + 1) * d, :] = mm_nt(eye, attn[0, j].astype(BF16)).astype(BF16)
        wproj[3 * d : 4 * d, :] = eye
        wproj[4 * d : 5 * d, :] = attn[0, 1].astype(BF16)
        wproj[5 * d : 6 * d, :] = attn[0, 2].astype(BF16)
        wo_t[...] = mm_nt(eye, attn[0, 3].astype(BF16)).astype(BF16)
        for c in range(ff // d):
            at = slice(c * d, (c + 1) * d)
            win_t[at, :] = mm_nt(eye, w_in[0, :, at].astype(BF16)).astype(BF16)
            wout_t[:, at] = mm_nt(eye, w_out[0, at, :].astype(BF16)).astype(BF16)
        for c in range(bias_bc.shape[0] // d):
            row = biases[pl.ds(t, 1), c * d : (c + 1) * d]
            bias_bc[c * d : (c + 1) * d, :] = jnp.broadcast_to(row, (128, d)).T
        for c in range(2):
            row = gains[t, c : c + 1, :]
            gain_bc[c * d : (c + 1) * d, :] = jnp.broadcast_to(row, (128, d)).T

    @pl.when(is_q)
    def _():
        xs[...] = xq[...].reshape(span, d)

    @pl.when(jnp.logical_not(is_q))
    def _():
        xs[...] = xp[...].reshape(span, d)

    def length_of(u, segment):
        base = (jnp.minimum(i, nqs - 1) * GROUP + u) * segs
        out = jnp.full(segment.shape, qlen[base + segs - 1], jnp.int32)
        for s in range(segs - 1):
            out = jnp.where(segment == s, qlen[base + s], out)
        return jnp.where(is_q, out, plen[jnp.maximum(i - nqs, 0) * GROUP + u])

    key = lax.broadcasted_iota(jnp.int32, (TOK, TOK), 0)
    ask = lax.broadcasted_iota(jnp.int32, (TOK, TOK), 1)
    row = lax.broadcasted_iota(jnp.int32, (16, TOK), 0)
    token = lax.broadcasted_iota(jnp.int32, (16, TOK), 1)
    key_col = lax.broadcasted_iota(jnp.int32, (TOK, 1), 0)
    far = is_q & ((key // HEAD) != (ask // HEAD))
    owner = jnp.where(is_q, token // HEAD, 0)
    place = jnp.where(is_q, token % HEAD, token)
    seg_row = lax.broadcasted_iota(jnp.int32, (16, 1), 0)
    for u in range(GROUP):
        dead = jnp.where(is_q, key_col % HEAD, key_col) >= length_of(u, key_col // HEAD)
        away[u] = jnp.where(far | dead, MASKED_SCORE, 0.0)
        live = ((place < length_of(u, token // HEAD)) & (row == owner)).astype(F32)
        live_out[0, :, u * TOK : (u + 1) * TOK] = live.astype(BF16)

    def bias(at, size):
        return wide(bias_bc[at : at + size, :])

    x = xs[...]
    q_t = (mm_nt(wproj[0:d, :], x) + bias(0, d)).astype(BF16)
    qk_out[0, 0:d, :] = q_t
    for u in range(GROUP):
        for h in range(heads):
            piece = q_t[h * HEAD : (h + 1) * HEAD, u * TOK : (u + 1) * TOK]
            qblk[u, h * HEAD : (h + 1) * HEAD, h * TOK : (h + 1) * TOK] = piece * BF16(HEAD**-0.5)
    k_row = mm(x, wproj[4 * d : 5 * d, :]).astype(BF16)
    for u in range(GROUP):
        for h in range(heads):
            score_s[u, h] = mm(k_row[u * TOK : (u + 1) * TOK, :], qblk[u, :, h * TOK : (h + 1) * TOK])
    v_t = (mm_nt(wproj[2 * d : 3 * d, :], x) + bias(d, d)).astype(BF16)
    qk_out[0, d : 2 * d, :] = mm_nt(wproj[d : 2 * d, :], x).astype(BF16)
    v_out[0] = (mm(x, wproj[5 * d : 6 * d, :]) + biases[pl.ds(t, 1), d : 2 * d]).astype(BF16)
    x_t = mm_nt(wproj[3 * d : 4 * d, :], x)
    x_out[0, 0:d, :] = x_t.astype(BF16)
    for u in range(GROUP):
        for h in range(heads):
            scores = score_s[u, h] + away[u]
            exponent = jnp.exp(scores - jnp.max(scores, axis=0, keepdims=True))
            probs = exponent * (1.0 / jnp.sum(exponent, axis=0, keepdims=True))
            p_out[0, u, h] = probs.astype(BF16)
    for u in range(GROUP):
        for h in range(heads):
            at = slice(h * HEAD, (h + 1) * HEAD)
            over = slice(u * TOK, (u + 1) * TOK)
            ctx_out[0, at, over] = mm(v_t[at, over], p_out[0, u, h]).astype(BF16)
    hidden = x_t + (mm(wo_t[...], ctx_out[0, 0:d, :]) + bias(2 * d, d))
    first, n1, inv1 = norm_columns(hidden, wide(gain_bc[0:d, :]), bias(3 * d, d))
    n1_out[0] = n1
    first_low = first.astype(BF16)
    first_out[0, 0:d, :] = first_low
    hidden = first + bias(4 * d, d)
    for c in range(ff // d):
        at = slice(c * d, (c + 1) * d)
        upper = mm(win_t[at, :], first_low) + bias(6 * d + c * d, d)
        active, slope = gelu_and_slope(upper)
        slope_out[0, at, :] = slope
        active_low = active.astype(BF16)
        act_out[0, at, :] = active_low
        hidden = hidden + mm(wout_t[:, at], active_low)
    second, n2, inv2 = norm_columns(hidden, wide(gain_bc[d : 2 * d, :]), bias(5 * d, d))
    n2_out[0] = n2
    which = lax.broadcasted_iota(jnp.int32, (8, span), 0)
    inv_out[0] = jnp.where(which == 0, inv1, inv2)
    second_high, second_low = split_two(second)
    ones = jnp.ones((ONES, span), BF16)
    x_out[0, d:, :] = ones
    ctx_out[0, d:, :] = ones
    first_out[0, d:, :] = ones
    act_out[0, ff:, :] = ones
    for u in range(GROUP):
        over = slice(u * TOK, (u + 1) * TOK)
        live = live_out[0, :, over]
        pooled = mm_nt(live, second_high[:, over]) + mm_nt(live, second_low[:, over])
        pooled = pooled / length_of(u, seg_row).astype(F32)

        @pl.when(is_q)
        def _(pooled=pooled, u=u):
            for s in range(segs):
                pooled_out[pl.ds((i * GROUP + u) * segs + s, 1), :] = pooled[s : s + 1, :]

        @pl.when(jnp.logical_not(is_q))
        def _(pooled=pooled, u=u):
            pooled_out[pl.ds(nqs * GROUP * segs + (i - nqs) * GROUP + u, 1), :] = pooled[0:1, :]

    @pl.when(i == last)
    def _():
        rows = pooled_out[...]
        unit = rows * lax.rsqrt(jnp.sum(rows * rows, axis=1, keepdims=True) + UNIT_EPSILON)
        slots, own = lists.shape
        turn[...] = jnp.zeros_like(turn)
        turn[0:slots, 0:own] = (lists[...] // PART).astype(F32)
        turn[slots : 2 * slots, 0:own] = (lists[...] % PART).astype(F32)
        turn[2 * slots : 2 * slots + 1, 0:own] = counts[...].astype(F32)
        extra = turn[...].T[0:own, :]
        sent = jnp.concatenate([unit[:, c * 128 : (c + 1) * 128] for c in range(d // 128)] + [extra], axis=0)
        units_out[...] = jnp.broadcast_to(sent.astype(BF16)[None], units_out.shape)


def step_spec(*shape):
    return pl.BlockSpec((1,) + shape, lambda i, *_: (i,) + (0,) * len(shape))


def tower_spec(nqs, *shape):
    return pl.BlockSpec((1,) + shape, lambda i, *_: (jnp.where(i < nqs, 0, 1),) + (0,) * len(shape))


def whole_spec(*shape):
    return pl.BlockSpec(shape, lambda i, *_: (0,) * len(shape))


def forward(devices, q_lengths, p_lengths, xq, xp, attn, w_in, w_out, gains, biases, positives, counts):
    nqs, nps = xq.shape[0] // GROUP, xp.shape[0] // GROUP
    steps = nqs + nps
    span = GROUP * TOK
    d, ff = w_in.shape[1:]
    heads = d // HEAD
    seqs = q_lengths.shape[0] + xp.shape[0]
    sent = seqs * d // 128 + positives.shape[1]
    outs = [
        ((d + ONES, span), BF16),
        ((2 * d, span), BF16),
        ((span, d), BF16),
        ((GROUP, heads, TOK, TOK), BF16),
        ((d + ONES, span), BF16),
        ((d, span), F32),
        ((d + ONES, span), BF16),
        ((ff, span), F32),
        ((ff + ONES, span), BF16),
        ((d, span), F32),
        ((8, span), F32),
        ((16, span), BF16),
    ]
    return pl.pallas_call(
        functools.partial(forward_kernel, nqs),
        grid_spec=pltpu.PrefetchScalarGridSpec(
            num_scalar_prefetch=2,
            grid=(steps,),
            in_specs=[
                pl.BlockSpec((GROUP, TOK, d), lambda i, *_: (jnp.minimum(i, nqs - 1), 0, 0)),
                pl.BlockSpec((GROUP, TOK, d), lambda i, *_: (jnp.maximum(i - nqs, 0), 0, 0)),
                tower_spec(nqs, 4, d, d),
                tower_spec(nqs, d, ff),
                tower_spec(nqs, ff, d),
                whole_spec(2, 2, d),
                whole_spec(2, biases.shape[1]),
                whole_spec(*positives.shape),
                whole_spec(1, positives.shape[1]),
            ],
            out_specs=[step_spec(*shape) for shape, _ in outs] + [whole_spec(seqs, d), whole_spec(devices, sent, 128)],
            scratch_shapes=[
                pltpu.VMEM((6 * d, d), BF16),
                pltpu.VMEM((d, d), BF16),
                pltpu.VMEM((ff, d), BF16),
                pltpu.VMEM((d, ff), BF16),
                pltpu.VMEM((biases.shape[1], 128), F32),
                pltpu.VMEM((2 * d, 128), F32),
                pltpu.VMEM((GROUP, d, heads * TOK), BF16),
                pltpu.VMEM((span, d), BF16),
                pltpu.VMEM((GROUP, TOK, TOK), F32),
                pltpu.VMEM((GROUP, heads, TOK, TOK), F32),
                pltpu.VMEM((128, 128), F32),
            ],
        ),
        out_shape=[jax.ShapeDtypeStruct((steps,) + shape, kind) for shape, kind in outs]
        + [jax.ShapeDtypeStruct((seqs, d), F32), jax.ShapeDtypeStruct((devices, sent, 128), BF16)],
        compiler_params=pltpu.CompilerParams(vmem_limit_bytes=VMEM_LIMIT),
        name="forward",
    )(q_lengths, p_lengths, xq, xp, attn, w_in, w_out, gains, biases, positives, counts)


def contrast_kernel(nqu, slots, index, qlen, plen, units, pooled, loss_out, gp_out, low_rows, gup_rows, gp_rows, turn):
    devices = units.shape[0]
    seqs, d = pooled.shape
    own = qlen.shape[0]
    mine = pl.multiple_of(index[0] * own, own)
    pown = seqs - own
    pmine = pl.multiple_of(index[0] * pown, pown)
    both = units[...].astype(F32)
    parts = range(0, seqs * d // 128, seqs)
    uq = jnp.concatenate([both[:, at : at + own, :] for at in parts], axis=2).reshape(devices * own, d).astype(BF16)
    up = jnp.concatenate([both[:, at + own : at + seqs, :] for at in parts], axis=2).reshape(devices * pown, d).astype(BF16)
    lists = both[:, seqs * d // 128 :, :].reshape(devices * own, 128)
    scores = SCORE_SCALE * mm_nt(uq, up)
    columns = lax.broadcasted_iota(jnp.int32, scores.shape, 1).astype(F32)
    positive = None
    for k in range(slots):
        listed = lists[:, k : k + 1] * PART + lists[:, slots + k : slots + k + 1]
        hit = (listed == columns) & (lists[:, 2 * slots : 2 * slots + 1] > k)
        positive = hit if positive is None else positive | hit
    highest = jnp.max(scores, axis=1, keepdims=True)
    whole = highest + jnp.log(jnp.sum(jnp.exp(scores - highest), axis=1, keepdims=True))
    chosen = jnp.where(positive, scores, MASKED_SCORE)
    top = jnp.max(chosen, axis=1, keepdims=True)
    within = top + jnp.log(jnp.sum(jnp.exp(chosen - top), axis=1, keepdims=True))
    low = (SCORE_SCALE * (jnp.exp(scores - whole) - jnp.exp(chosen - within))).astype(BF16)
    low_rows[:, : scores.shape[1]] = low.astype(F32)
    low_rows[:, scores.shape[1] :] = jnp.broadcast_to(whole - within, (scores.shape[0], 128))
    turn[...] = jnp.zeros_like(turn)
    turn[0:own, :] = low_rows[pl.ds(mine, own), scores.shape[1] :]
    loss_out[...] = turn[...].T[0:1, 0:own]
    grad_q = mm(low_rows[pl.ds(mine, own), : scores.shape[1]].astype(BF16), up)
    gup_rows[...] = mm_tn(low, uq)
    grad_p = gup_rows[pl.ds(pmine, pown), :]
    grad = jnp.concatenate([grad_q, grad_p], axis=0)
    rows = pooled[...]
    inverse = lax.rsqrt(jnp.sum(rows * rows, axis=1, keepdims=True) + UNIT_EPSILON)
    grad = inverse * grad - inverse * inverse * inverse * rows * jnp.sum(rows * grad, axis=1, keepdims=True)
    segs = own // nqu
    gp_rows[...] = jnp.zeros_like(gp_rows)
    for s in range(own):
        gp_rows[s // segs, s % segs : s % segs + 1, :] = grad[s : s + 1, :] / jnp.full((1, d), qlen[s], jnp.int32).astype(F32)
    for s in range(pown):
        gp_rows[nqu + s, 0:1, :] = grad[own + s : own + s + 1, :] / jnp.full((1, d), plen[s], jnp.int32).astype(F32)
    for term, value in enumerate(split_three(gp_rows[...])):
        gp_out[:, term * 16 : (term + 1) * 16, :] = value


def contrast(nqu, npu, slots, index, q_lengths, p_lengths, units, pooled):
    devices = units.shape[0]
    seqs, d = pooled.shape
    own = q_lengths.shape[0]
    passages = devices * (seqs - own)
    vmem = pl.BlockSpec(memory_space=pltpu.VMEM)
    return pl.pallas_call(
        functools.partial(contrast_kernel, nqu, slots),
        in_specs=[pl.BlockSpec(memory_space=pltpu.SMEM)] * 3 + [vmem, vmem],
        out_specs=[vmem, vmem],
        out_shape=[jax.ShapeDtypeStruct((1, own), F32), jax.ShapeDtypeStruct((nqu + npu, 48, d), BF16)],
        scratch_shapes=[
            pltpu.VMEM((devices * own, passages + 128), F32),
            pltpu.VMEM((passages, d), F32),
            pltpu.VMEM((nqu + npu, 16, d), F32),
            pltpu.VMEM((128, 128), F32),
        ],
        compiler_params=pltpu.CompilerParams(vmem_limit_bytes=VMEM_LIMIT),
        name="contrast",
    )(index, q_lengths, p_lengths, units, pooled)


def left_rows(start_t, matrix):
    s_high, s_low = split_two(start_t)
    m_high, m_low = split_two(matrix)
    both = mm_nt(jnp.concatenate([s_high, s_low], axis=0), m_high)
    return both[:8] + both[8:] + mm_nt(jnp.concatenate([s_high, s_high], axis=0), m_low)[:8]


def right_rows(basis, matrix):
    b_high, b_low = split_two(basis)
    m_high, m_low = split_two(matrix)
    both = mm(jnp.concatenate([b_high, b_low], axis=0), m_high)
    return both[:8] + both[8:] + mm(jnp.concatenate([b_high, b_high], axis=0), m_low)[:8]


def core_of(index, outer):
    return (index[0] // outer) % 2


def part_halves(core, whole, mine, other):
    half = whole.shape[1] // 2
    for c in range(2):

        @pl.when(core == c)
        def _(c=c):
            mine[...] = whole[:, c * half : (c + 1) * half]
            other[...] = whole[:, (1 - c) * half : (2 - c) * half]


def join_halves(core, whole, mine, other):
    half = whole.shape[1] // 2
    for c in range(2):

        @pl.when(core == c)
        def _(c=c):
            whole[:, c * half : (c + 1) * half] = mine[...]
            whole[:, (1 - c) * half : (2 - c) * half] = other[...]


def backward_kernel(
    nqs, outer, index, gp, x_in, qk_in, v_in, p_in, ctx_in, n1_in, first_in, slope_in, act_in, n2_in, inv_in, live_in,
    attn, w_in, w_out, gains, attn_err, in_err, out_err, attn_start, in_start, out_start,
    qgrad, pgrad, attn_m, in_m, out_m, left_mine, left_other,
    left, wqkv, wo, win, wout, gain_bc, gz, gp_s, graw_s, gqkv, acc_qkv, acc_o, acc_in, acc_out, acc_gain,
):
    i = pl.program_id(0)
    last = pl.num_programs(0) - 1
    is_q = i < nqs
    t = jnp.where(is_q, 0, 1)
    d = wo.shape[0]
    ff = wout.shape[0]
    heads = d // HEAD
    span = GROUP * TOK

    @pl.when(i == 0)
    def _():
        gz[...] = jnp.zeros_like(gz)

    @pl.when((i == 0) | (i == nqs))
    def _():
        for j in range(3):
            wqkv[:, j * d : (j + 1) * d] = attn[0, j].astype(BF16)
        wo[...] = attn[0, 3].astype(BF16)
        win[...] = w_in[0].astype(BF16)
        wout[...] = w_out[0].astype(BF16)
        for c in range(2):
            row = gains[t, c : c + 1, :]
            gain_bc[c * d : (c + 1) * d, :] = jnp.broadcast_to(row, (128, d)).T
        acc_qkv[...] = jnp.zeros_like(acc_qkv)
        acc_o[...] = jnp.zeros_like(acc_o)
        acc_in[...] = jnp.zeros_like(acc_in)
        acc_out[...] = jnp.zeros_like(acc_out)
        acc_gain[...] = jnp.zeros_like(acc_gain)

    def add_gain(at, value):
        total = value[:, :128]
        for c in range(1, span // 128):
            total = total + value[:, c * 128 : (c + 1) * 128]
        acc_gain[at * d : (at + 1) * d, :] += total

    pieces = []
    for u in range(GROUP):
        live = live_in[0, :, u * TOK : (u + 1) * TOK]
        pieces.append(mm_tn(gp[u], jnp.concatenate([live, live, live], axis=0)))
    grad_second = jnp.concatenate(pieces, axis=1)
    n2 = n2_in[0]
    grad_two = norm_columns_back(grad_second, n2, inv_in[0, 1:2, :], wide(gain_bc[d : 2 * d, :]))
    down_low = grad_two.astype(BF16)
    grad_first = grad_two
    for c in range(ff // d):
        at = slice(c * d, (c + 1) * d)
        up_low = (mm(wout[at, :], down_low) * slope_in[0, at, :]).astype(BF16)
        acc_in[:, at] += mm_nt(first_in[0], up_low)
        grad_first = grad_first + mm(win[:, at], up_low)
    add_gain(1, grad_second * n2)
    add_gain(3, grad_second)
    n1 = n1_in[0]
    grad_one = norm_columns_back(grad_first, n1, inv_in[0, 0:1, :], wide(gain_bc[0:d, :]))
    branch_low = grad_one.astype(BF16)
    grad_context = mm(wo[...], branch_low).astype(BF16)
    for u in range(GROUP):
        for h in range(heads):
            at = slice(h * HEAD, (h + 1) * HEAD)
            gz[u, at, h * TOK : (h + 1) * TOK] = grad_context[at, u * TOK : (u + 1) * TOK]
    for u in range(GROUP):
        for h in range(heads):
            gp_s[u, h] = mm(v_in[0, u * TOK : (u + 1) * TOK, :], gz[u, :, h * TOK : (h + 1) * TOK])
    acc_out[...] += mm_nt(act_in[0], down_low)
    add_gain(0, grad_first * n1)
    add_gain(2, grad_first)
    acc_o[...] += mm_nt(ctx_in[0], branch_low)
    for u in range(GROUP):
        for h in range(heads):
            probs = p_in[0, u, h].astype(F32)
            grad_probs = gp_s[u, h]
            inner = jnp.sum(grad_probs * probs, axis=0, keepdims=True)
            graw_s[u, h] = (probs * (grad_probs - inner) * HEAD**-0.5).astype(BF16)
    for u in range(GROUP):
        over = slice(u * TOK, (u + 1) * TOK)
        for h in range(heads):
            at = slice(h * HEAD, (h + 1) * HEAD)
            later = slice(d + h * HEAD, d + (h + 1) * HEAD)
            last_at = slice(2 * d + h * HEAD, 2 * d + (h + 1) * HEAD)
            gqkv[last_at, over] = mm_nt(grad_context[at, over], p_in[0, u, h]).astype(BF16)
            gqkv[at, over] = mm(qk_in[0, later, over], graw_s[u, h]).astype(BF16)
            gqkv[later, over] = mm_nt(qk_in[0, at, over], graw_s[u, h]).astype(BF16)
    acc_qkv[...] += mm_nt(x_in[0], gqkv[...])
    result = (grad_one + mm(wqkv[...], gqkv[...])).T.reshape(GROUP, TOK, d)

    @pl.when(is_q)
    def _():
        qgrad[...] = result

    @pl.when(jnp.logical_not(is_q))
    def _():
        pgrad[...] = result

    @pl.when((i == nqs - 1) | (i == last))
    def _():
        base_in = 8 * d
        base_out = base_in + 2 * d
        base_vec = base_out + 2 * ff
        for j in range(4):
            grad = acc_o[0:d, :] if j == 3 else acc_qkv[0:d, j * d : (j + 1) * d]
            merged = grad + attn_err[0, 0, j]
            attn_m[0, j] = merged
            left[:, pl.ds(pl.multiple_of((t * 4 + j) * d, 128), d)] = left_rows(attn_start[0, j], merged)
        merged = acc_in[0:d, :] + in_err[0, 0]
        in_m[0] = merged
        left[:, pl.ds(pl.multiple_of(base_in + t * d, 128), d)] = left_rows(in_start[0], merged)
        merged = acc_out[0:ff, :] + out_err[0, 0]
        out_m[0] = merged
        left[:, pl.ds(pl.multiple_of(base_out + t * ff, 128), ff)] = left_rows(out_start[0], merged)
        sums = mm_nt(jnp.ones((8, 128), F32), acc_gain[...], HIGHEST)

        def vectors():
            yield sums[0:1, 0:d]
            yield sums[0:1, d : 2 * d]
            yield acc_qkv[d : d + 1, 0:d]
            yield acc_qkv[d : d + 1, 2 * d : 3 * d]
            yield acc_o[d : d + 1, :]
            yield sums[0:1, 2 * d : 3 * d]
            yield acc_out[ff : ff + 1, :]
            yield sums[0:1, 3 * d : 4 * d]
            for c in range(ff // d):
                yield acc_in[d : d + 1, c * d : (c + 1) * d]

        for tower in range(2):

            @pl.when(t == tower)
            def _(tower=tower):
                for v, vector in enumerate(vectors()):
                    at = tower * 12 + v
                    left[at // 3 : at // 3 + 1, base_vec + (at % 3) * d : base_vec + (at % 3 + 1) * d] = vector

    @pl.when(i == last)
    def _():
        part_halves(core_of(index, outer), left, left_mine, left_other)


def backward(nqs, nps, outer, index, gp, saved, attn, w_in, w_out, gains, attn_err, in_err, out_err, starts):
    steps = nqs + nps
    nqu, npu = nqs * GROUP, nps * GROUP
    span = GROUP * TOK
    d, ff = w_in.shape[1:]
    heads = d // HEAD
    width = 8 * d + 2 * d + 2 * ff + 3 * d
    tower = functools.partial(tower_spec, nqs)

    def error_spec(*shape):
        return pl.BlockSpec((1, 1) + shape, lambda i: (0, jnp.where(i < nqs, 0, 1)) + (0,) * len(shape))

    return pl.pallas_call(
        functools.partial(backward_kernel, nqs, outer),
        grid=(steps,),
        in_specs=[pl.BlockSpec(memory_space=pltpu.SMEM), pl.BlockSpec((GROUP, 48, d), lambda i: (i, 0, 0))]
        + [step_spec(*array.shape[1:]) for array in saved]
        + [tower(4, d, d), tower(d, ff), tower(ff, d), whole_spec(2, 2, d)]
        + [error_spec(4, d, d), error_spec(d, ff), error_spec(ff, d)]
        + [tower(4, 8, d), tower(8, ff), tower(8, d)],
        out_specs=[
            pl.BlockSpec((GROUP, TOK, d), lambda i: (jnp.minimum(i, nqs - 1), 0, 0)),
            pl.BlockSpec((GROUP, TOK, d), lambda i: (jnp.maximum(i - nqs, 0), 0, 0)),
            tower(4, d, d),
            tower(d, ff),
            tower(ff, d),
            whole_spec(8, width // 2),
            whole_spec(8, width // 2),
        ],
        out_shape=[
            jax.ShapeDtypeStruct((nqu, TOK, d), F32),
            jax.ShapeDtypeStruct((npu, TOK, d), F32),
            pltpu.VMEM((2, 4, d, d), F32),
            pltpu.VMEM((2, d, ff), F32),
            pltpu.VMEM((2, ff, d), F32),
            jax.ShapeDtypeStruct((8, width // 2), F32),
            jax.ShapeDtypeStruct((8, width // 2), F32),
        ],
        scratch_shapes=[
            pltpu.VMEM((8, width), F32),
            pltpu.VMEM((d, 3 * d), BF16),
            pltpu.VMEM((d, d), BF16),
            pltpu.VMEM((d, ff), BF16),
            pltpu.VMEM((ff, d), BF16),
            pltpu.VMEM((2 * d, 128), F32),
            pltpu.VMEM((GROUP, d, heads * TOK), BF16),
            pltpu.VMEM((GROUP, heads, TOK, TOK), F32),
            pltpu.VMEM((GROUP, heads, TOK, TOK), BF16),
            pltpu.VMEM((3 * d, span), BF16),
            pltpu.VMEM((d + ONES, 3 * d), F32),
            pltpu.VMEM((d + ONES, d), F32),
            pltpu.VMEM((d + ONES, ff), F32),
            pltpu.VMEM((ff + ONES, d), F32),
            pltpu.VMEM((4 * d, 128), F32),
        ],
        compiler_params=pltpu.CompilerParams(vmem_limit_bytes=50 << 20),
        name="backward",
    )(index, gp, *saved, attn, w_in, w_out, gains, attn_err, in_err, out_err, *starts)


def right_kernel(outer, index, left_mine, left_other, attn_m, in_m, out_m, basis, right_mine, right_other, vector, left, right):
    d, ff = in_m.shape[1:]
    core = core_of(index, outer)
    join_halves(core, left, left_mine, left_other)
    vector[...] = left[:, 10 * d + 2 * ff :]
    places = [(j * d, d) for j in range(8)] + [(8 * d + t * d, d) for t in range(2)] + [(10 * d + t * ff, ff) for t in range(2)]
    blocks = [left[:, at : at + size] for at, size in places]
    for j in range(8):
        for b, block in enumerate(blocks):
            order = lax.broadcasted_iota(jnp.int32, (8, 1), 0)
            column = block[j : j + 1, :]
            dots = jnp.sum(block * column, axis=1, keepdims=True)
            scale = lax.rsqrt(dots[j : j + 1, :] + 1e-06)
            unit = column * scale
            step = jnp.where(order > j, dots * scale, 0.0)
            blocks[b] = jnp.where(order == j, unit, block - step * unit)
    for (at, size), block in zip(places, blocks):
        basis[:, at : at + size] = block
    for j in range(8):
        right[:, j * d : (j + 1) * d] = right_rows(blocks[j], attn_m[j // 4, j % 4])
    for t in range(2):
        right[:, 8 * d + t * ff : 8 * d + (t + 1) * ff] = right_rows(blocks[8 + t], in_m[t])
        right[:, 8 * d + 2 * ff + t * d : 8 * d + 2 * ff + (t + 1) * d] = right_rows(blocks[10 + t], out_m[t])
    part_halves(core, right, right_mine, right_other)


def right_factors(outer, index, left_mine, left_other, attn_m, in_m, out_m):
    d, ff = in_m.shape[1:]
    vmem = pl.BlockSpec(memory_space=pltpu.VMEM)
    width = 10 * d + 2 * ff
    rows = functools.partial(jax.ShapeDtypeStruct, dtype=F32)
    return pl.pallas_call(
        functools.partial(right_kernel, outer),
        in_specs=[pl.BlockSpec(memory_space=pltpu.SMEM)] + [vmem] * 5,
        out_specs=[vmem] * 4,
        out_shape=[rows((8, width)), rows((8, width // 2)), rows((8, width // 2)), rows((8, 3 * d))],
        scratch_shapes=[pltpu.VMEM((8, width + 3 * d), F32), pltpu.VMEM((8, width), F32)],
        compiler_params=pltpu.CompilerParams(vmem_limit_bytes=12 << 20),
        name="right",
    )(index, left_mine, left_other, attn_m, in_m, out_m)


def update_kernel(
    replicas, outer, index, basis, right_mine, right_other, vector, gains, biases, gain_mom, bias_mom,
    attn_m, in_m, out_m, attn, w_in, w_out, attn_mom, in_mom, out_mom,
    attn_new, in_new, out_new, attn_mom_new, in_mom_new, out_mom_new, attn_err, in_err, out_err,
    gains_new, biases_new, gain_mom_new, bias_mom_new, attn_factor, in_factor, out_factor, norm_out,
    right, clip_s,
):
    i = pl.program_id(0)
    d = attn.shape[2]
    ff = (right.shape[1] - 10 * d) // 2
    t, c = i // 4, i % 4

    @pl.when(i == 0)
    def _():
        join_halves(core_of(index, outer), right, right_mine, right_other)
        for j in range(8):
            attn_factor[j // 4, j % 4] = right[:, j * d : (j + 1) * d]
        for s in range(2):
            in_factor[s] = right[:, 8 * d + s * ff : 8 * d + (s + 1) * ff]
            out_factor[s] = right[:, 8 * d + 2 * ff + s * d : 8 * d + 2 * ff + (s + 1) * d]
        places = [((j * d, d), (j * d, d)) for j in range(8)]
        places += [((8 * d + s * d, d), (8 * d + s * ff, ff)) for s in range(2)]
        places += [((10 * d + s * ff, ff), (8 * d + 2 * ff + s * d, d)) for s in range(2)]
        total = jnp.zeros((8, 8), F32)
        for (b_at, b_size), (r_at, r_size) in places:
            b = basis[:, b_at : b_at + b_size]
            r = right[:, r_at : r_at + r_size]
            total = total + mm_nt(b, b, HIGHEST) * mm_nt(r, r, HIGHEST)
        sums = vector[...]
        square = jnp.sum(jnp.sum(total, axis=1, keepdims=True), axis=0, keepdims=True)
        square = square + jnp.sum(jnp.sum(sums * sums, axis=1, keepdims=True), axis=0, keepdims=True)
        norm = jnp.sqrt(jnp.broadcast_to(square, (8, 128)))
        norm_out[0] = norm[0, 0]
        clip_s[...] = jnp.minimum(1.0, CLIP_NORM / norm)
        held = clip_s[0:1, 0:1]
        for s in range(2):
            for v in range(12):
                at = s * 12 + v
                reduced = vector[at // 3 : at // 3 + 1, (at % 3) * d : (at % 3 + 1) * d]
                if v < 2:
                    moved = MOMENTUM_DECAY * gain_mom[s, v : v + 1, :] + held * reduced
                    gain_mom_new[s, v : v + 1, :] = moved
                    gains_new[s, v : v + 1, :] = gains[s, v : v + 1, :] - LEARNING_RATE * moved
                else:
                    over = slice((v - 2) * d, (v - 1) * d)
                    moved = MOMENTUM_DECAY * bias_mom[s : s + 1, over] + held * reduced
                    bias_mom_new[s : s + 1, over] = moved
                    biases_new[s : s + 1, over] = biases[s : s + 1, over] - LEARNING_RATE * moved

    clip = clip_s[0:1, 0:1]

    def step(b_at, r_at, merged, weight, moment, weight_new, moment_new, error):
        b1, b2, b3 = split_three(basis[:, pl.ds(pl.multiple_of(b_at, 128), d)])
        r1, r2, r3 = split_three(right[:, pl.ds(pl.multiple_of(r_at, 128), d)])
        approx = mm_tn(jnp.concatenate([b1, b1, b2, b1, b2, b3], axis=0), jnp.concatenate([r1, r2, r1, r3, r2, r1], axis=0))
        moved = MOMENTUM_DECAY * moment + clip * approx
        moment_new[...] = moved.reshape(moment_new.shape)
        weight_new[...] = (weight - LEARNING_RATE * moved).reshape(weight_new.shape)
        error[...] = (merged - approx * (1.0 / replicas)).reshape(error.shape)

    step(i * d, i * d, attn_m[0, 0], attn[0, 0], attn_mom[0, 0], attn_new, attn_mom_new, attn_err)
    step((8 + t) * d, 8 * d + t * ff + c * d, in_m[0], w_in[0], in_mom[0], in_new, in_mom_new, in_err)
    step(10 * d + t * ff + c * d, 8 * d + 2 * ff + t * d, out_m[0], w_out[0], out_mom[0], out_new, out_mom_new, out_err)


def update(replicas, outer, index, basis, right_mine, right_other, vector, gains, biases, gain_mom, bias_mom, merged, weights, moments):
    d, ff = weights[1].shape[1:]
    a_spec = pl.BlockSpec((1, 1, d, d), lambda i: (i // 4, i % 4, 0, 0))
    i_spec = pl.BlockSpec((1, d, d), lambda i: (i // 4, 0, i % 4))
    o_spec = pl.BlockSpec((1, d, d), lambda i: (i // 4, i % 4, 0))
    ae_spec = pl.BlockSpec((1, 1, 1, d, d), lambda i: (0, i // 4, i % 4, 0, 0))
    ie_spec = pl.BlockSpec((1, 1, d, d), lambda i: (0, i // 4, 0, i % 4))
    oe_spec = pl.BlockSpec((1, 1, d, d), lambda i: (0, i // 4, i % 4, 0))
    rows = functools.partial(jax.ShapeDtypeStruct, dtype=F32)
    small = (basis, right_mine, right_other, vector, gains, biases, gain_mom, bias_mom)
    finals = [gains.shape, biases.shape] * 2 + [(2, 4, 8, d), (2, 8, ff), (2, 8, d)]
    return pl.pallas_call(
        functools.partial(update_kernel, replicas, outer),
        grid=(8,),
        in_specs=[pl.BlockSpec(memory_space=pltpu.SMEM)] + [whole_spec(*a.shape) for a in small] + [a_spec, i_spec, o_spec] * 3,
        out_specs=[a_spec, i_spec, o_spec] * 2
        + [ae_spec, ie_spec, oe_spec]
        + [whole_spec(*shape) for shape in finals]
        + [pl.BlockSpec(memory_space=pltpu.SMEM)],
        out_shape=[rows(a.shape) for a in weights * 2]
        + [rows((1,) + a.shape) for a in weights]
        + [rows(shape) for shape in finals]
        + [rows((1,))],
        scratch_shapes=[pltpu.VMEM(basis.shape, F32), pltpu.VMEM((8, 128), F32)],
        compiler_params=pltpu.CompilerParams(vmem_limit_bytes=14 << 20),
        name="update",
    )(index, *small, *merged, *weights, *moments)


def in_vmem(*arrays):
    return tuple(pltpu.with_memory_space_constraint(a, pltpu.VMEM) for a in arrays)


def swap_with(x, axis, mask):
    return lax.ppermute(x, axis, [(i, i ^ mask) for i in range(lax.axis_size(axis))])


def sum_halves(mine, other):
    mine = mine + swap_with(other, "dp", 1)
    size = lax.axis_size("dp")
    if size == 8:
        steps = [("dp", (2, 4, 6))]
    else:
        steps = [("dp", (1 << b,)) for b in range(1, size.bit_length() - 1)]
    steps.append(("outer", tuple(range(1, lax.axis_size("outer")))))
    for axis, masks in steps:
        sent = mine.astype(SEND)
        mine = sent.astype(F32)
        for got in [swap_with(sent, axis, mask) for mask in masks]:
            mine = mine + got.astype(F32)
    return mine, swap_with(mine, "dp", 1)


def per_device(
    questions, passages, q_lengths, p_lengths, positives, pos_counts, attn, w_in, w_out, gains, biases, attn_mom, w_in_mom,
    w_out_mom, gain_mom, bias_mom, attn_err, w_in_err, w_out_err, attn_start, w_in_start, w_out_start,
):
    devices = lax.axis_size("dp") * lax.axis_size("outer")
    d, ff = w_in.shape[1:]
    xq = questions.reshape(-1, TOK, d)
    xp = passages.reshape(-1, TOK, d)
    nqu, npu = xq.shape[0], xp.shape[0]
    index = (lax.axis_index("dp") * lax.axis_size("outer") + lax.axis_index("outer")).astype(jnp.int32).reshape(1)
    *saved, pooled, units = forward(
        devices, q_lengths, p_lengths, xq, xp, attn, w_in, w_out, gains, biases, positives.T, pos_counts.reshape(1, -1)
    )
    units = lax.all_to_all(units, AXES, 0, 0)
    loss, gp = contrast(nqu, npu, positives.shape[1], index, q_lengths, p_lengths, *in_vmem(units), pooled)
    starts = [jnp.swapaxes(start, -1, -2) for start in (attn_start, w_in_start, w_out_start)]
    outer = lax.axis_size("outer")
    qgrad, pgrad, attn_m, in_m, out_m, *left = backward(
        nqu // GROUP, npu // GROUP, outer, index, gp, saved, attn, w_in, w_out, gains, attn_err, w_in_err, w_out_err, starts
    )
    weights = (attn, w_in, w_out)
    moments = (attn_mom, w_in_mom, w_out_mom)
    merged = in_vmem(attn_m, in_m, out_m)
    held = in_vmem(*weights, *moments)
    basis, *right, vector = right_factors(outer, index, *sum_halves(*left), *merged)
    *new, attn_factor, in_factor, out_factor, norm = update(
        devices, outer, index, basis, *sum_halves(*right), vector, gains, biases, gain_mom, bias_mom,
        merged, held[:3], held[3:],
    )
    weights_new, moments_new, errors_new, vectors_new = new[:3], new[3:6], new[6:9], new[9:]
    factors = [jnp.swapaxes(factor, -1, -2) for factor in (attn_factor, in_factor, out_factor)]
    return (
        loss.reshape(-1), qgrad.reshape(questions.shape), pgrad.reshape(passages.shape),
        *weights_new, *vectors_new[:2], *moments_new, *vectors_new[2:], *errors_new, *factors, norm.reshape(()),
    )


def solution(mesh):
    split = ("dp", "outer")
    share = P(split)
    return jax.shard_map(
        per_device,
        mesh=mesh,
        in_specs=(share,) * 6 + (P(),) * 10 + (share,) * 3 + (P(),) * 3,
        out_specs=(share,) * 3 + (P(),) * 10 + (share,) * 3 + (P(),) * 4,
        check_vma=False,
    )
```

```python
import functools
import math

import jax
import jax.numpy as jnp
from jax import lax
from jax.experimental import pallas as pl
from jax.experimental.pallas import tpu as pltpu
from jax.sharding import PartitionSpec as P

HEAD = 64
TOK = 256
GROUP = 2
PART = 64
ONES = 16

NORM_EPSILON = 1e-06
UNIT_EPSILON = 1e-06
SCORE_SCALE = 20.0
MOMENTUM_DECAY = 0.9
LEARNING_RATE = 10.0
CLIP_NORM = 2.0
MASKED_SCORE = -1e30
HIGHEST = lax.Precision.HIGHEST
AXES = ("dp", "outer")
F32 = jnp.float32
BF16 = jnp.bfloat16
VMEM_LIMIT = 56 << 20
FORWARD_VMEM = 20 << 20
BACKWARD_VMEM = 20 << 20
SEND = BF16


def mm(a, b, precision=None):
    return lax.dot_general(a, b, (((1,), (0,)), ((), ())), precision=precision, preferred_element_type=F32)


def mm_nt(a, b, precision=None):
    return lax.dot_general(a, b, (((1,), (1,)), ((), ())), precision=precision, preferred_element_type=F32)


def mm_tn(a, b, precision=None):
    return lax.dot_general(a, b, (((0,), (0,)), ((), ())), precision=precision, preferred_element_type=F32)


def wide(column):
    return jnp.concatenate([column] * (GROUP * TOK // 128), axis=1)


def split_two(v):
    high = v.astype(BF16)
    return high, (v - high.astype(F32)).astype(BF16)


def split_three(v):
    high = v.astype(BF16)
    rest = v - high.astype(F32)
    middle = rest.astype(BF16)
    return high, middle, (rest - middle.astype(F32)).astype(BF16)


def norm_columns(hidden, gain, shift):
    share = 1.0 / hidden.shape[0]
    center = hidden - jnp.sum(hidden, axis=0, keepdims=True) * share
    inverse = lax.rsqrt(jnp.sum(center * center, axis=0, keepdims=True) * share + NORM_EPSILON)
    normed = center * inverse
    return normed * gain + shift, normed, inverse


def norm_columns_back(grad, normed, inverse, gain):
    share = 1.0 / grad.shape[0]
    scaled = grad * gain
    mean = jnp.sum(scaled, axis=0, keepdims=True) * share
    along = jnp.sum(scaled * normed, axis=0, keepdims=True) * share
    return inverse * (scaled - mean - normed * along)


def gelu_and_slope(u):
    phi = 0.5 + 0.5 * lax.erf(u * 0.5**0.5)
    bell = jnp.exp(u * u * -0.5) * (0.5 / math.pi) ** 0.5
    return u * phi, phi + u * bell


def forward_kernel(
    nqs, qlen, plen, xq, xp, attn, w_in, w_out, gains, biases, lists, counts,
    x_out, qk_out, v_out, p_out, ctx_out, n1_out, first_out, slope_out, act_out, n2_out, inv1_out, inv2_out, live_out, wqkv_out, wo_out, win_out, wout_out, pooled_out, units_out,
    wproj, wo_t, win_t, wout_t, bias_bc, gain_bc, qblk, xs, away, score_s, first_s, first_low_s, turn,
):
    i = pl.program_id(0)
    steps = pl.num_programs(0) - 1
    d = xs.shape[1]
    ff = win_t.shape[0]
    heads = d // HEAD
    segs = TOK // HEAD
    span = GROUP * TOK
    late = jnp.maximum(i - 1, 0)

    def tower(group):
        return jnp.where(group < nqs, 0, 1)

    def eye():
        return (lax.broadcasted_iota(jnp.int32, (d, d), 0) == lax.broadcasted_iota(jnp.int32, (d, d), 1)).astype(F32).astype(BF16)

    def spread(at, row):
        bias_bc[at : at + d, :] = jnp.broadcast_to(row, (128, d)).T

    @pl.when(i == 0)
    def _():
        qblk[...] = jnp.zeros_like(qblk)

    @pl.when((i == 0) | (i == nqs))
    def _():
        one = eye()
        t = tower(i)
        for j in range(3):
            low = attn[0, j].astype(BF16)
            wqkv_out[t, :, j * d : (j + 1) * d] = low
            wproj[j * d : (j + 1) * d, :] = mm_nt(one, low).astype(BF16)
            if j:
                wproj[(3 + j) * d : (4 + j) * d, :] = low
        wproj[3 * d : 4 * d, :] = one
        low = attn[0, 3].astype(BF16)
        wo_out[t] = low
        wo_t[...] = mm_nt(one, low).astype(BF16)
        for c in range(4):
            spread(c * d, biases[pl.ds(t, 1), c * d : (c + 1) * d])
        gain_bc[0:d, :] = jnp.broadcast_to(gains[t, 0:1, :], (128, d)).T

    @pl.when((i == 1) | (i == nqs + 1))
    def _():
        one = eye()
        t = tower(late)
        for c in range(ff // d):
            at = slice(c * d, (c + 1) * d)
            low = w_in[0, :, at].astype(BF16)
            win_out[t, :, at] = low
            win_t[at, :] = mm_nt(one, low).astype(BF16)
            low = w_out[0, at, :].astype(BF16)
            wout_out[t, at, :] = low
            wout_t[:, at] = mm_nt(one, low).astype(BF16)
        for c in range(4, bias_bc.shape[0] // d):
            spread(c * d, biases[pl.ds(t, 1), c * d : (c + 1) * d])
        gain_bc[d : 2 * d, :] = jnp.broadcast_to(gains[t, 1:2, :], (128, d)).T

    @pl.when(i < nqs)
    def _():
        xs[...] = xq[...].reshape(span, d)

    @pl.when(i >= nqs)
    def _():
        xs[...] = xp[...].reshape(span, d)

    def length_of(group, u, segment):
        base = (jnp.minimum(group, nqs - 1) * GROUP + u) * segs
        out = jnp.full(segment.shape, qlen[base + segs - 1], jnp.int32)
        for s in range(segs - 1):
            out = jnp.where(segment == s, qlen[base + s], out)
        return jnp.where(group < nqs, out, plen[jnp.clip(group - nqs, 0, steps - nqs - 1) * GROUP + u])

    def bias(at, size):
        return wide(bias_bc[at : at + size, :])

    def attention_parts():
        is_q = i < nqs
        key = lax.broadcasted_iota(jnp.int32, (TOK, TOK), 0)
        ask = lax.broadcasted_iota(jnp.int32, (TOK, TOK), 1)
        key_col = lax.broadcasted_iota(jnp.int32, (TOK, 1), 0)
        far = is_q & ((key // HEAD) != (ask // HEAD))
        for u in range(GROUP):
            dead = jnp.where(is_q, key_col % HEAD, key_col) >= length_of(i, u, key_col // HEAD)
            away[u] = jnp.where(far | dead, MASKED_SCORE, 0.0)
        x = xs[...]
        q_t = (mm_nt(wproj[0:d, :], x) + bias(0, d)).astype(BF16)
        qk_out[i, 0:d, :] = q_t
        for u in range(GROUP):
            for h in range(heads):
                piece = q_t[h * HEAD : (h + 1) * HEAD, u * TOK : (u + 1) * TOK]
                qblk[u, h * HEAD : (h + 1) * HEAD, h * TOK : (h + 1) * TOK] = piece * BF16(HEAD**-0.5)
        k_row = mm(x, wproj[4 * d : 5 * d, :]).astype(BF16)
        yield
        v_t = (mm_nt(wproj[2 * d : 3 * d, :], x) + bias(d, d)).astype(BF16)
        for u in range(GROUP):
            for h in range(heads):
                score_s[u, h] = mm(k_row[u * TOK : (u + 1) * TOK, :], qblk[u, :, h * TOK : (h + 1) * TOK])
            yield
        qk_out[i, d : 2 * d, :] = mm_nt(wproj[d : 2 * d, :], x).astype(BF16)
        v_out[i] = (mm(x, wproj[5 * d : 6 * d, :]) + biases[pl.ds(tower(i), 1), d : 2 * d]).astype(BF16)
        x_t = mm_nt(wproj[3 * d : 4 * d, :], x)
        x_out[i, 0:d, :] = x_t.astype(BF16)
        yield
        for u in range(GROUP):
            for h in range(heads):
                scores = score_s[u, h] + away[u]
                exponent = jnp.exp(scores - jnp.max(scores, axis=0, keepdims=True))
                probs = exponent * (1.0 / jnp.sum(exponent, axis=0, keepdims=True))
                p_out[i, u, h] = probs.astype(BF16)
                at = slice(h * HEAD, (h + 1) * HEAD)
                over = slice(u * TOK, (u + 1) * TOK)
                ctx_out[i, at, over] = mm(v_t[at, over], p_out[i, u, h]).astype(BF16)
                if h % 2:
                    yield
        hidden = x_t + (mm(wo_t[...], ctx_out[i, 0:d, :]) + bias(2 * d, d))
        first, n1, inv1 = norm_columns(hidden, wide(gain_bc[0:d, :]), bias(3 * d, d))
        n1_out[i] = n1
        inv1_out[i] = jnp.broadcast_to(inv1, (8, span))
        ones = jnp.ones((ONES, span), BF16)
        x_out[i, d:, :] = ones
        ctx_out[i, d:, :] = ones
        first_out[i, d:, :] = ones
        yield
        first_low = first.astype(BF16)
        first_out[i, 0:d, :] = first_low
        first_low_s[...] = first_low
        first_s[...] = first

    def feed_parts():
        is_q = late < nqs
        first_low = first_low_s[...]
        hidden = first_s[...] + bias(4 * d, d)
        for c in range(ff // d):
            at = slice(c * d, (c + 1) * d)
            for half in range(2):
                rows = slice(c * d + half * (d // 2), c * d + (half + 1) * (d // 2))
                upper = mm(win_t[rows, :], first_low) + bias(6 * d + rows.start, d // 2)
                active, slope = gelu_and_slope(upper)
                slope_out[late, rows, :] = slope
                act_out[late, rows, :] = active.astype(BF16)
                yield
            hidden = hidden + mm(wout_t[:, at], act_out[late, at, :])
        second, n2, inv2 = norm_columns(hidden, wide(gain_bc[d : 2 * d, :]), bias(5 * d, d))
        n2_out[late] = n2
        inv2_out[late] = jnp.broadcast_to(inv2, (8, span))
        act_out[late, ff:, :] = jnp.ones((ONES, span), BF16)
        second_high, second_low = split_two(second)
        row = lax.broadcasted_iota(jnp.int32, (16, TOK), 0)
        token = lax.broadcasted_iota(jnp.int32, (16, TOK), 1)
        owner = jnp.where(is_q, token // HEAD, 0)
        place = jnp.where(is_q, token % HEAD, token)
        seg_row = lax.broadcasted_iota(jnp.int32, (16, 1), 0)
        for u in range(GROUP):
            over = slice(u * TOK, (u + 1) * TOK)
            live = ((place < length_of(late, u, token // HEAD)) & (row == owner)).astype(F32).astype(BF16)
            live_out[late, :, over] = live
            pooled = mm_nt(live, second_high[:, over]) + mm_nt(live, second_low[:, over])
            pooled = pooled / length_of(late, u, seg_row).astype(F32)

            @pl.when(is_q)
            def _(pooled=pooled, u=u):
                for s in range(segs):
                    pooled_out[pl.ds((late * GROUP + u) * segs + s, 1), :] = pooled[s : s + 1, :]

            @pl.when(jnp.logical_not(is_q))
            def _(pooled=pooled, u=u):
                pooled_out[pl.ds(nqs * GROUP * segs + (late - nqs) * GROUP + u, 1), :] = pooled[0:1, :]

    def in_turn(*kinds):
        running = [kind() for kind in kinds]
        while running:
            running = [parts for parts in running if next(parts, running) is not running]

    @pl.when(i == 0)
    def _():
        in_turn(attention_parts)

    @pl.when((i > 0) & (i < steps))
    def _():
        in_turn(feed_parts, attention_parts)

    @pl.when(i == steps)
    def _():
        in_turn(feed_parts)
        rows = pooled_out[...]
        unit = rows * lax.rsqrt(jnp.sum(rows * rows, axis=1, keepdims=True) + UNIT_EPSILON)
        slots, own = lists.shape
        turn[...] = jnp.zeros_like(turn)
        turn[0:slots, 0:own] = (lists[...] // PART).astype(F32)
        turn[slots : 2 * slots, 0:own] = (lists[...] % PART).astype(F32)
        turn[2 * slots : 2 * slots + 1, 0:own] = counts[...].astype(F32)
        extra = turn[...].T[0:own, :]
        sent = jnp.concatenate([unit[:, c * 128 : (c + 1) * 128] for c in range(d // 128)] + [extra], axis=0)
        units_out[0] = sent.astype(BF16)


def step_spec(*shape):
    return pl.BlockSpec((1,) + shape, lambda i, *_: (i,) + (0,) * len(shape))


def tower_spec(nqs, *shape):
    return pl.BlockSpec((1,) + shape, lambda i, *_: (jnp.where(i < nqs, 0, 1),) + (0,) * len(shape))


def whole_spec(*shape):
    return pl.BlockSpec(shape, lambda i, *_: (0,) * len(shape))


def forward(q_lengths, p_lengths, xq, xp, attn, w_in, w_out, gains, biases, positives, counts):
    nqs, nps = xq.shape[0] // GROUP, xp.shape[0] // GROUP
    steps = nqs + nps
    span = GROUP * TOK
    d, ff = w_in.shape[1:]
    heads = d // HEAD
    seqs = q_lengths.shape[0] + xp.shape[0]
    sent = seqs * d // 128 + positives.shape[1]
    early = [
        ((d + ONES, span), BF16),
        ((2 * d, span), BF16),
        ((span, d), BF16),
        ((GROUP, heads, TOK, TOK), BF16),
        ((d + ONES, span), BF16),
        ((d, span), F32),
        ((d + ONES, span), BF16),
    ]
    later = [((ff, span), F32), ((ff + ONES, span), BF16), ((d, span), F32)]
    rows = [((8, span), F32), ((8, span), F32), ((16, span), BF16)]
    outs = early + later + rows

    def second_tower_spec(*shape):
        return pl.BlockSpec((1,) + shape, lambda i, *_: (jnp.where(i - 1 < nqs, 0, 1),) + (0,) * len(shape))

    kept = [pltpu.VMEM((steps,) + shape, kind) for shape, kind in outs]
    kept += [pltpu.VMEM((2,) + shape, BF16) for shape in ((d, 3 * d), (d, d), (d, ff), (ff, d))]
    kept += [pltpu.VMEM((seqs, d), F32)]
    direct = pl.BlockSpec(memory_space=pltpu.VMEM)
    return pl.pallas_call(
        functools.partial(forward_kernel, nqs),
        grid_spec=pltpu.PrefetchScalarGridSpec(
            num_scalar_prefetch=2,
            grid=(steps + 1,),
            in_specs=[
                pl.BlockSpec((GROUP, TOK, d), lambda i, *_: (jnp.minimum(i, nqs - 1), 0, 0)),
                pl.BlockSpec((GROUP, TOK, d), lambda i, *_: (jnp.clip(i - nqs, 0, nps - 1), 0, 0)),
                tower_spec(nqs, 4, d, d),
                second_tower_spec(d, ff),
                second_tower_spec(ff, d),
                whole_spec(2, 2, d),
                whole_spec(2, biases.shape[1]),
                whole_spec(*positives.shape),
                whole_spec(1, positives.shape[1]),
            ],
            out_specs=[direct] * (len(kept) + 1),
            scratch_shapes=[
                pltpu.VMEM((6 * d, d), BF16),
                pltpu.VMEM((d, d), BF16),
                pltpu.VMEM((ff, d), BF16),
                pltpu.VMEM((d, ff), BF16),
                pltpu.VMEM((biases.shape[1], 128), F32),
                pltpu.VMEM((2 * d, 128), F32),
                pltpu.VMEM((GROUP, d, heads * TOK), BF16),
                pltpu.VMEM((span, d), BF16),
                pltpu.VMEM((GROUP, TOK, TOK), F32),
                pltpu.VMEM((GROUP, heads, TOK, TOK), F32),
                pltpu.VMEM((d, span), F32),
                pltpu.VMEM((d, span), BF16),
                pltpu.VMEM((128, 128), F32),
            ],
        ),
        out_shape=kept + [jax.ShapeDtypeStruct((1, sent, 128), BF16)],
        compiler_params=pltpu.CompilerParams(vmem_limit_bytes=FORWARD_VMEM),
        name="forward",
    )(q_lengths, p_lengths, xq, xp, attn, w_in, w_out, gains, biases, positives, counts)


def contrast_kernel(
    nqu, slots, dp, outer, qlen, plen, near, far, pooled, loss_out, gp_out, low_rows, gup_rows, gp_rows, turn
):
    devices = dp * outer
    seqs, d = pooled.shape
    own = qlen.shape[0]
    pown = seqs - own
    both = jnp.concatenate([near[...], far[...]], axis=0).astype(F32)
    parts = range(0, seqs * d // 128, seqs)
    uq = jnp.concatenate([both[:, at : at + own, :] for at in parts], axis=2).reshape(devices * own, d).astype(BF16)
    up = jnp.concatenate([both[:, at + own : at + seqs, :] for at in parts], axis=2).reshape(devices * pown, d).astype(BF16)
    lists = both[:, seqs * d // 128 :, :].reshape(devices * own, 128)
    scores = SCORE_SCALE * mm_nt(uq, up)
    place = lax.broadcasted_iota(jnp.int32, (1, devices * pown), 1)
    block = place // pown
    along = ((block // outer) % (dp // 2)) * 2 + block // (devices // 2)
    device = (lax.axis_index("dp") ^ along) * outer + (lax.axis_index("outer") ^ (block % outer))
    columns = (device * pown + place % pown).astype(F32)
    positive = None
    for k in range(slots):
        listed = lists[:, k : k + 1] * PART + lists[:, slots + k : slots + k + 1]
        hit = (listed == columns) & (lists[:, 2 * slots : 2 * slots + 1] > k)
        positive = hit if positive is None else positive | hit
    highest = jnp.max(scores, axis=1, keepdims=True)
    whole = highest + jnp.log(jnp.sum(jnp.exp(scores - highest), axis=1, keepdims=True))
    chosen = jnp.where(positive, scores, MASKED_SCORE)
    top = jnp.max(chosen, axis=1, keepdims=True)
    within = top + jnp.log(jnp.sum(jnp.exp(chosen - top), axis=1, keepdims=True))
    low = (SCORE_SCALE * (jnp.exp(scores - whole) - jnp.exp(chosen - within))).astype(BF16)
    low_rows[:, : scores.shape[1]] = low.astype(F32)
    low_rows[:, scores.shape[1] :] = jnp.broadcast_to(whole - within, (scores.shape[0], 128))
    turn[...] = jnp.zeros_like(turn)
    turn[0:own, :] = low_rows[0:own, scores.shape[1] :]
    loss_out[...] = turn[...].T[0:1, 0:own]
    grad_q = mm(low_rows[0:own, : scores.shape[1]].astype(BF16), up)
    gup_rows[...] = mm_tn(low, uq)
    grad_p = gup_rows[0:pown, :]
    grad = jnp.concatenate([grad_q, grad_p], axis=0)
    rows = pooled[...]
    inverse = lax.rsqrt(jnp.sum(rows * rows, axis=1, keepdims=True) + UNIT_EPSILON)
    grad = inverse * grad - inverse * inverse * inverse * rows * jnp.sum(rows * grad, axis=1, keepdims=True)
    segs = own // nqu
    gp_rows[...] = jnp.zeros_like(gp_rows)
    for s in range(own):
        gp_rows[s // segs, s % segs : s % segs + 1, :] = grad[s : s + 1, :] / jnp.full((1, d), qlen[s], jnp.int32).astype(F32)
    for s in range(pown):
        gp_rows[nqu + s, 0:1, :] = grad[own + s : own + s + 1, :] / jnp.full((1, d), plen[s], jnp.int32).astype(F32)
    for term, value in enumerate(split_three(gp_rows[...])):
        gp_out[:, term * 16 : (term + 1) * 16, :] = value


def contrast(nqu, npu, slots, dp, outer, q_lengths, p_lengths, near, far, pooled):
    devices = dp * outer
    seqs, d = pooled.shape
    own = q_lengths.shape[0]
    passages = devices * (seqs - own)
    vmem = pl.BlockSpec(memory_space=pltpu.VMEM)
    return pl.pallas_call(
        functools.partial(contrast_kernel, nqu, slots, dp, outer),
        in_specs=[pl.BlockSpec(memory_space=pltpu.SMEM)] * 2 + [vmem] * 3,
        out_specs=[vmem, vmem],
        out_shape=[jax.ShapeDtypeStruct((1, own), F32), pltpu.VMEM((nqu + npu, 48, d), BF16)],
        scratch_shapes=[
            pltpu.VMEM((devices * own, passages + 128), F32),
            pltpu.VMEM((passages, d), F32),
            pltpu.VMEM((nqu + npu, 16, d), F32),
            pltpu.VMEM((128, 128), F32),
        ],
        compiler_params=pltpu.CompilerParams(vmem_limit_bytes=min(VMEM_LIMIT, (6 << 20) + 32 * devices * own * passages)),
        name="contrast",
    )(q_lengths, p_lengths, near, far, pooled)


def left_rows(start_t, matrix):
    s_high, s_low = split_two(start_t)
    m_high, m_low = split_two(matrix)
    both = mm_nt(jnp.concatenate([s_high, s_low], axis=0), m_high)
    return both[:8] + both[8:] + mm_nt(jnp.concatenate([s_high, s_high], axis=0), m_low)[:8]


def right_rows(basis, matrix):
    b_high, b_low = split_two(basis)
    m_high, m_low = split_two(matrix)
    both = mm(jnp.concatenate([b_high, b_low], axis=0), m_high)
    return both[:8] + both[8:] + mm(jnp.concatenate([b_high, b_high], axis=0), m_low)[:8]


def own_core():
    return lax.axis_index("dp") % 2


def part_halves(core, whole, mine, other):
    half = whole.shape[1] // 2
    for c in range(2):

        @pl.when(core == c)
        def _(c=c):
            mine[...] = whole[:, c * half : (c + 1) * half]
            other[...] = whole[:, (1 - c) * half : (2 - c) * half]


def join_halves(core, whole, mine, other):
    half = whole.shape[1] // 2
    for c in range(2):

        @pl.when(core == c)
        def _(c=c):
            whole[:, c * half : (c + 1) * half] = mine[...]
            whole[:, (1 - c) * half : (2 - c) * half] = other[...]


def backward_kernel(
    nqs, gp, x_in, qk_in, v_in, p_in, ctx_in, n1_in, first_in, slope_in, act_in, n2_in, inv1_in, inv2_in, live_in,
    wqkv, wo, win, wout, gains, attn_err, in_err, out_err, attn_start, in_start, out_start,
    qgrad, pgrad, attn_m, in_m, out_m, left_mine, left_other,
    left, gain_bc, gz, gp_s, graw_s, gqkv, acc_qkv, acc_o, acc_in, acc_out, acc_gain, err_sems,
):
    i = pl.program_id(0)
    last = pl.num_programs(0) - 1
    is_q = i < nqs
    t = jnp.where(is_q, 0, 1)
    d = wo.shape[1]
    ff = wout.shape[1]
    errors = [
        pltpu.make_async_copy(source.at[0, tower], target.at[tower], err_sems.at[tower, k])
        for tower in range(2)
        for k, (source, target) in enumerate(((attn_err, attn_m), (in_err, in_m), (out_err, out_m)))
    ]
    heads = d // HEAD
    span = GROUP * TOK

    @pl.when(i == 0)
    def _():
        for copy in errors:
            copy.start()
        gz[...] = jnp.zeros_like(gz)

    @pl.when((i == 0) | (i == nqs))
    def _():
        for c in range(2):
            row = gains[t, c : c + 1, :]
            gain_bc[c * d : (c + 1) * d, :] = jnp.broadcast_to(row, (128, d)).T
        acc_qkv[...] = jnp.zeros_like(acc_qkv)
        acc_o[...] = jnp.zeros_like(acc_o)
        acc_in[...] = jnp.zeros_like(acc_in)
        acc_out[...] = jnp.zeros_like(acc_out)
        acc_gain[...] = jnp.zeros_like(acc_gain)

    def add_gain(at, value):
        total = value[:, :128]
        for c in range(1, span // 128):
            total = total + value[:, c * 128 : (c + 1) * 128]
        acc_gain[at * d : (at + 1) * d, :] += total

    pieces = []
    for u in range(GROUP):
        live = live_in[i, :, u * TOK : (u + 1) * TOK]
        pieces.append(mm_tn(gp[i * GROUP + u], jnp.concatenate([live, live, live], axis=0)))
    grad_second = jnp.concatenate(pieces, axis=1)
    n2 = n2_in[i]
    grad_two = norm_columns_back(grad_second, n2, inv2_in[i, 0:1, :], wide(gain_bc[d : 2 * d, :]))
    down_low = grad_two.astype(BF16)
    grad_first = grad_two
    for c in range(ff // d):
        at = slice(c * d, (c + 1) * d)
        up_low = (mm(wout[t, at, :], down_low) * slope_in[i, at, :]).astype(BF16)
        acc_in[:, at] += mm_nt(first_in[i], up_low)
        grad_first = grad_first + mm(win[t, :, at], up_low)
    add_gain(1, grad_second * n2)
    add_gain(3, grad_second)
    n1 = n1_in[i]
    grad_one = norm_columns_back(grad_first, n1, inv1_in[i, 0:1, :], wide(gain_bc[0:d, :]))
    branch_low = grad_one.astype(BF16)
    grad_context = mm(wo[t], branch_low).astype(BF16)
    for u in range(GROUP):
        for h in range(heads):
            at = slice(h * HEAD, (h + 1) * HEAD)
            gz[u, at, h * TOK : (h + 1) * TOK] = grad_context[at, u * TOK : (u + 1) * TOK]
    for u in range(GROUP):
        for h in range(heads):
            gp_s[u, h] = mm(v_in[i, u * TOK : (u + 1) * TOK, :], gz[u, :, h * TOK : (h + 1) * TOK])
    acc_out[...] += mm_nt(act_in[i], down_low)
    add_gain(0, grad_first * n1)
    add_gain(2, grad_first)
    acc_o[...] += mm_nt(ctx_in[i], branch_low)
    for u in range(GROUP):
        for h in range(heads):
            probs = p_in[i, u, h].astype(F32)
            grad_probs = gp_s[u, h]
            inner = jnp.sum(grad_probs * probs, axis=0, keepdims=True)
            graw_s[u, h] = (probs * (grad_probs - inner) * HEAD**-0.5).astype(BF16)
    for u in range(GROUP):
        over = slice(u * TOK, (u + 1) * TOK)
        for h in range(heads):
            at = slice(h * HEAD, (h + 1) * HEAD)
            later = slice(d + h * HEAD, d + (h + 1) * HEAD)
            last_at = slice(2 * d + h * HEAD, 2 * d + (h + 1) * HEAD)
            gqkv[last_at, over] = mm_nt(grad_context[at, over], p_in[i, u, h]).astype(BF16)
            gqkv[at, over] = mm(qk_in[i, later, over], graw_s[u, h]).astype(BF16)
            gqkv[later, over] = mm_nt(qk_in[i, at, over], graw_s[u, h]).astype(BF16)
    acc_qkv[...] += mm_nt(x_in[i], gqkv[...])
    result = (grad_one + mm(wqkv[t], gqkv[...])).T.reshape(GROUP, TOK, d)

    @pl.when(is_q)
    def _():
        qgrad[...] = result

    @pl.when(jnp.logical_not(is_q))
    def _():
        pgrad[...] = result

    @pl.when((i == nqs - 1) | (i == last))
    def _():
        for tower in range(2):

            @pl.when(t == tower)
            def _(tower=tower):
                for copy in errors[3 * tower : 3 * tower + 3]:
                    copy.wait()

        base_in = 8 * d
        base_out = base_in + 2 * d
        base_vec = base_out + 2 * ff
        for j in range(4):
            grad = acc_o[0:d, :] if j == 3 else acc_qkv[0:d, j * d : (j + 1) * d]
            merged = grad + attn_m[t, j]
            attn_m[t, j] = merged
            left[:, pl.ds(pl.multiple_of((t * 4 + j) * d, 128), d)] = left_rows(attn_start[t, j], merged)
        merged = acc_in[0:d, :] + in_m[t]
        in_m[t] = merged
        left[:, pl.ds(pl.multiple_of(base_in + t * d, 128), d)] = left_rows(in_start[t], merged)
        merged = acc_out[0:ff, :] + out_m[t]
        out_m[t] = merged
        left[:, pl.ds(pl.multiple_of(base_out + t * ff, 128), ff)] = left_rows(out_start[t], merged)
        sums = mm_nt(jnp.ones((8, 128), F32), acc_gain[...], HIGHEST)

        def vectors():
            yield sums[0:1, 0:d]
            yield sums[0:1, d : 2 * d]
            yield acc_qkv[d : d + 1, 0:d]
            yield acc_qkv[d : d + 1, 2 * d : 3 * d]
            yield acc_o[d : d + 1, :]
            yield sums[0:1, 2 * d : 3 * d]
            yield acc_out[ff : ff + 1, :]
            yield sums[0:1, 3 * d : 4 * d]
            for c in range(ff // d):
                yield acc_in[d : d + 1, c * d : (c + 1) * d]

        for tower in range(2):

            @pl.when(t == tower)
            def _(tower=tower):
                for v, vector in enumerate(vectors()):
                    at = tower * 12 + v
                    left[at // 3 : at // 3 + 1, base_vec + (at % 3) * d : base_vec + (at % 3 + 1) * d] = vector

    @pl.when(i == last)
    def _():
        part_halves(own_core(), left, left_mine, left_other)


def backward(nqs, nps, gp, saved, low_weights, gains, errors, starts):
    steps = nqs + nps
    nqu, npu = nqs * GROUP, nps * GROUP
    span = GROUP * TOK
    d, ff = errors[1].shape[2:]
    heads = d // HEAD
    width = 8 * d + 2 * d + 2 * ff + 3 * d
    direct = pl.BlockSpec(memory_space=pltpu.VMEM)
    far = pl.BlockSpec(memory_space=pl.ANY)
    return pl.pallas_call(
        functools.partial(backward_kernel, nqs),
        grid=(steps,),
        in_specs=[direct] * (len(saved) + 6) + [far] * 3 + [direct] * 3,
        out_specs=[
            pl.BlockSpec((GROUP, TOK, d), lambda i: (jnp.minimum(i, nqs - 1), 0, 0)),
            pl.BlockSpec((GROUP, TOK, d), lambda i: (jnp.maximum(i - nqs, 0), 0, 0)),
        ]
        + [direct] * 5,
        out_shape=[
            jax.ShapeDtypeStruct((nqu, TOK, d), F32),
            jax.ShapeDtypeStruct((npu, TOK, d), F32),
            pltpu.VMEM((2, 4, d, d), F32),
            pltpu.VMEM((2, d, ff), F32),
            pltpu.VMEM((2, ff, d), F32),
            jax.ShapeDtypeStruct((8, width // 2), F32),
            jax.ShapeDtypeStruct((8, width // 2), F32),
        ],
        scratch_shapes=[
            pltpu.VMEM((8, width), F32),
            pltpu.VMEM((2 * d, 128), F32),
            pltpu.VMEM((GROUP, d, heads * TOK), BF16),
            pltpu.VMEM((GROUP, heads, TOK, TOK), F32),
            pltpu.VMEM((GROUP, heads, TOK, TOK), BF16),
            pltpu.VMEM((3 * d, span), BF16),
            pltpu.VMEM((d + ONES, 3 * d), F32),
            pltpu.VMEM((d + ONES, d), F32),
            pltpu.VMEM((d + ONES, ff), F32),
            pltpu.VMEM((ff + ONES, d), F32),
            pltpu.VMEM((4 * d, 128), F32),
            pltpu.SemaphoreType.DMA((2, 3)),
        ],
        compiler_params=pltpu.CompilerParams(vmem_limit_bytes=BACKWARD_VMEM),
        name="backward",
    )(gp, *saved, *low_weights, gains, *errors, *starts)


def right_kernel(left_mine, left_other, attn_m, in_m, out_m, _, basis, right_mine, right_other, vector, left, right):
    d, ff = in_m.shape[1:]
    core = own_core()
    join_halves(core, left, left_mine, left_other)
    vector[...] = left[:, 10 * d + 2 * ff :]
    places = [(j * d, d) for j in range(8)] + [(8 * d + t * d, d) for t in range(2)] + [(10 * d + t * ff, ff) for t in range(2)]
    blocks = [left[:, at : at + size] for at, size in places]
    for j in range(8):
        for b, block in enumerate(blocks):
            order = lax.broadcasted_iota(jnp.int32, (8, 1), 0)
            column = block[j : j + 1, :]
            dots = jnp.sum(block * column, axis=1, keepdims=True)
            scale = lax.rsqrt(dots[j : j + 1, :] + 1e-06)
            unit = column * scale
            step = jnp.where(order > j, dots * scale, 0.0)
            blocks[b] = jnp.where(order == j, unit, block - step * unit)
    for (at, size), block in zip(places, blocks):
        basis[:, at : at + size] = block
    for j in range(8):
        right[:, j * d : (j + 1) * d] = right_rows(blocks[j], attn_m[j // 4, j % 4])
    for t in range(2):
        right[:, 8 * d + t * ff : 8 * d + (t + 1) * ff] = right_rows(blocks[8 + t], in_m[t])
        right[:, 8 * d + 2 * ff + t * d : 8 * d + 2 * ff + (t + 1) * d] = right_rows(blocks[10 + t], out_m[t])
    part_halves(core, right, right_mine, right_other)


def right_factors(left_mine, left_other, attn_m, in_m, out_m, earlier):
    d, ff = in_m.shape[1:]
    vmem = pl.BlockSpec(memory_space=pltpu.VMEM)
    width = 10 * d + 2 * ff
    rows = functools.partial(jax.ShapeDtypeStruct, dtype=F32)
    return pl.pallas_call(
        right_kernel,
        in_specs=[vmem] * 6,
        out_specs=[vmem] * 4,
        out_shape=[rows((8, width)), rows((8, width // 2)), rows((8, width // 2)), rows((8, 3 * d))],
        scratch_shapes=[pltpu.VMEM((8, width + 3 * d), F32), pltpu.VMEM((8, width), F32)],
        compiler_params=pltpu.CompilerParams(vmem_limit_bytes=12 << 20),
        name="right",
    )(left_mine, left_other, attn_m, in_m, out_m, earlier)


def update_kernel(
    replicas, basis, right_mine, right_other, vector, gains, biases, gain_mom, bias_mom,
    attn_m, in_m, out_m, attn, w_in, w_out, attn_mom, in_mom, out_mom,
    attn_new, in_new, out_new, attn_mom_new, in_mom_new, out_mom_new, attn_err, in_err, out_err,
    gains_new, biases_new, gain_mom_new, bias_mom_new, attn_factor, in_factor, out_factor, norm_out,
    right, clip_s,
):
    i = pl.program_id(0)
    d = attn.shape[2]
    ff = (right.shape[1] - 10 * d) // 2
    t, c = i // 4, i % 4

    @pl.when(i == 0)
    def _():
        join_halves(own_core(), right, right_mine, right_other)
        for j in range(8):
            attn_factor[j // 4, j % 4] = right[:, j * d : (j + 1) * d]
        for s in range(2):
            in_factor[s] = right[:, 8 * d + s * ff : 8 * d + (s + 1) * ff]
            out_factor[s] = right[:, 8 * d + 2 * ff + s * d : 8 * d + 2 * ff + (s + 1) * d]
        places = [((j * d, d), (j * d, d)) for j in range(8)]
        places += [((8 * d + s * d, d), (8 * d + s * ff, ff)) for s in range(2)]
        places += [((10 * d + s * ff, ff), (8 * d + 2 * ff + s * d, d)) for s in range(2)]
        total = jnp.zeros((8, 8), F32)
        for (b_at, b_size), (r_at, r_size) in places:
            b = basis[:, b_at : b_at + b_size]
            r = right[:, r_at : r_at + r_size]
            total = total + mm_nt(b, b, HIGHEST) * mm_nt(r, r, HIGHEST)
        sums = vector[...]
        square = jnp.sum(jnp.sum(total, axis=1, keepdims=True), axis=0, keepdims=True)
        square = square + jnp.sum(jnp.sum(sums * sums, axis=1, keepdims=True), axis=0, keepdims=True)
        norm = jnp.sqrt(jnp.broadcast_to(square, (8, 128)))
        norm_out[0] = norm[0, 0]
        clip_s[...] = jnp.minimum(1.0, CLIP_NORM / norm)
        held = clip_s[0:1, 0:1]
        for s in range(2):
            for v in range(12):
                at = s * 12 + v
                reduced = vector[at // 3 : at // 3 + 1, (at % 3) * d : (at % 3 + 1) * d]
                if v < 2:
                    moved = MOMENTUM_DECAY * gain_mom[s, v : v + 1, :] + held * reduced
                    gain_mom_new[s, v : v + 1, :] = moved
                    gains_new[s, v : v + 1, :] = gains[s, v : v + 1, :] - LEARNING_RATE * moved
                else:
                    over = slice((v - 2) * d, (v - 1) * d)
                    moved = MOMENTUM_DECAY * bias_mom[s : s + 1, over] + held * reduced
                    bias_mom_new[s : s + 1, over] = moved
                    biases_new[s : s + 1, over] = biases[s : s + 1, over] - LEARNING_RATE * moved

    clip = clip_s[0:1, 0:1]

    def step(b_at, r_at, merged, weight, moment, weight_new, moment_new, error):
        b1, b2, b3 = split_three(basis[:, pl.ds(pl.multiple_of(b_at, 128), d)])
        r1, r2, r3 = split_three(right[:, pl.ds(pl.multiple_of(r_at, 128), d)])
        approx = mm_tn(jnp.concatenate([b1, b1, b2, b1, b2, b3], axis=0), jnp.concatenate([r1, r2, r1, r3, r2, r1], axis=0))
        moved = MOMENTUM_DECAY * moment + clip * approx
        moment_new[...] = moved.reshape(moment_new.shape)
        weight_new[...] = (weight - LEARNING_RATE * moved).reshape(weight_new.shape)
        error[...] = (merged - approx * (1.0 / replicas)).reshape(error.shape)

    step(i * d, i * d, attn_m[0, 0], attn[0, 0], attn_mom[0, 0], attn_new, attn_mom_new, attn_err)
    step((8 + t) * d, 8 * d + t * ff + c * d, in_m[0], w_in[0], in_mom[0], in_new, in_mom_new, in_err)
    step(10 * d + t * ff + c * d, 8 * d + 2 * ff + t * d, out_m[0], w_out[0], out_mom[0], out_new, out_mom_new, out_err)


def update(replicas, basis, right_mine, right_other, vector, gains, biases, gain_mom, bias_mom, merged, weights, moments):
    d, ff = weights[1].shape[1:]
    a_spec = pl.BlockSpec((1, 1, d, d), lambda i: (i // 4, i % 4, 0, 0))
    i_spec = pl.BlockSpec((1, d, d), lambda i: (i // 4, 0, i % 4))
    o_spec = pl.BlockSpec((1, d, d), lambda i: (i // 4, i % 4, 0))
    ae_spec = pl.BlockSpec((1, 1, 1, d, d), lambda i: (0, i // 4, i % 4, 0, 0))
    ie_spec = pl.BlockSpec((1, 1, d, d), lambda i: (0, i // 4, 0, i % 4))
    oe_spec = pl.BlockSpec((1, 1, d, d), lambda i: (0, i // 4, i % 4, 0))
    rows = functools.partial(jax.ShapeDtypeStruct, dtype=F32)
    small = (basis, right_mine, right_other, vector, gains, biases, gain_mom, bias_mom)
    finals = [gains.shape, biases.shape] * 2 + [(2, 4, 8, d), (2, 8, ff), (2, 8, d)]
    return pl.pallas_call(
        functools.partial(update_kernel, replicas),
        grid=(8,),
        in_specs=[whole_spec(*a.shape) for a in small] + [a_spec, i_spec, o_spec] * 3,
        out_specs=[a_spec, i_spec, o_spec] * 2
        + [ae_spec, ie_spec, oe_spec]
        + [whole_spec(*shape) for shape in finals]
        + [pl.BlockSpec(memory_space=pltpu.SMEM)],
        out_shape=[rows(a.shape) for a in weights * 2]
        + [rows((1,) + a.shape) for a in weights]
        + [rows(shape) for shape in finals]
        + [rows((1,))],
        scratch_shapes=[pltpu.VMEM(basis.shape, F32), pltpu.VMEM((8, 128), F32)],
        compiler_params=pltpu.CompilerParams(vmem_limit_bytes=14 << 20),
        name="update",
    )(*small, *merged, *weights, *moments)


def in_vmem(*arrays):
    return tuple(pltpu.with_memory_space_constraint(a, pltpu.VMEM) for a in arrays)


def hold_kernel(count, _, *refs):
    sources, targets, sems = refs[:count], refs[count : 2 * count], refs[2 * count]
    copies = [pltpu.make_async_copy(source, target, sems.at[k]) for k, (source, target) in enumerate(zip(sources, targets))]
    for copy in copies:
        copy.start()
    for copy in copies:
        copy.wait()


def hold(after, arrays):
    size = sum(4 * math.prod(a.shape) for a in arrays)
    return pl.pallas_call(
        functools.partial(hold_kernel, len(arrays)),
        in_specs=[pl.BlockSpec(memory_space=pl.ANY)] * (1 + len(arrays)),
        out_specs=[pl.BlockSpec(memory_space=pltpu.VMEM)] * len(arrays),
        out_shape=[pltpu.VMEM(a.shape, a.dtype) for a in arrays],
        scratch_shapes=[pltpu.SemaphoreType.DMA((len(arrays),))],
        compiler_params=pltpu.CompilerParams(vmem_limit_bytes=1 << 20),
        cost_estimate=pl.CostEstimate(flops=0, bytes_accessed=2 * size, transcendentals=0),
        name="hold",
    )(after, *(pltpu.with_memory_space_constraint(a, pltpu.HBM) for a in arrays))


def swap_with(x, axis, mask):
    return lax.ppermute(x, axis, [(i, i ^ mask) for i in range(lax.axis_size(axis))])


def chip_steps():
    size = lax.axis_size("dp")
    if size == 8:
        return [("dp", (2, 4, 6))]
    return [("dp", (1 << b,)) for b in range(1, size.bit_length() - 1)]


def outer_step():
    return ("outer", tuple(range(1, lax.axis_size("outer"))))


def gather_blocks(x):
    for axis, masks in [outer_step()] + chip_steps():
        x = jnp.concatenate([x] + [swap_with(x, axis, mask) for mask in masks], axis=0)
    return x, swap_with(x, "dp", 1)


def sum_halves(mine, other, beside=()):
    held = []
    mine = mine + swap_with(other, "dp", 1)
    for axis, masks in chip_steps() + [outer_step()]:
        sent = mine.astype(SEND)
        if beside and axis == "outer":
            held = in_vmem(*hold(sent, beside))
        mine = sent.astype(F32)
        for got in [swap_with(sent, axis, mask) for mask in masks]:
            mine = mine + got.astype(F32)
    return mine, swap_with(mine, "dp", 1), *held


def per_device(
    questions, passages, q_lengths, p_lengths, positives, pos_counts, attn, w_in, w_out, gains, biases, attn_mom, w_in_mom,
    w_out_mom, gain_mom, bias_mom, attn_err, w_in_err, w_out_err, attn_start, w_in_start, w_out_start,
):
    devices = lax.axis_size("dp") * lax.axis_size("outer")
    d, ff = w_in.shape[1:]
    xq = questions.reshape(-1, TOK, d)
    xp = passages.reshape(-1, TOK, d)
    nqu, npu = xq.shape[0], xp.shape[0]
    *saved, wqkv, wo, win, wout, pooled, units = forward(
        q_lengths, p_lengths, xq, xp, attn, w_in, w_out, gains, biases, positives.T, pos_counts.reshape(1, -1)
    )
    dp, outer = lax.axis_size("dp"), lax.axis_size("outer")
    near, far = gather_blocks(units)
    loss, gp = contrast(nqu, npu, positives.shape[1], dp, outer, q_lengths, p_lengths, *in_vmem(near, far, pooled))
    starts = [jnp.swapaxes(start, -1, -2) for start in (attn_start, w_in_start, w_out_start)]
    qgrad, pgrad, attn_m, in_m, out_m, *left = backward(
        nqu // GROUP, npu // GROUP, *in_vmem(gp), in_vmem(*saved), in_vmem(wqkv, wo, win, wout), gains,
        (attn_err, w_in_err, w_out_err), starts,
    )
    weights = (attn, w_in, w_out)
    moments = (attn_mom, w_in_mom, w_out_mom)
    merged = in_vmem(attn_m, in_m, out_m)
    *left, mom_a, mom_b, mom_c = sum_halves(*left, beside=moments)
    basis, *right, vector = right_factors(*left, *merged, mom_a)
    held = in_vmem(*weights) + (mom_a, mom_b, mom_c)
    *new, attn_factor, in_factor, out_factor, norm = update(
        devices, basis, *sum_halves(*right), vector, gains, biases, gain_mom, bias_mom,
        merged, held[:3], held[3:],
    )
    weights_new, moments_new, errors_new, vectors_new = new[:3], new[3:6], new[6:9], new[9:]
    factors = [jnp.swapaxes(factor, -1, -2) for factor in (attn_factor, in_factor, out_factor)]
    return (
        loss.reshape(-1), qgrad.reshape(questions.shape), pgrad.reshape(passages.shape),
        *weights_new, *vectors_new[:2], *moments_new, *vectors_new[2:], *errors_new, *factors, norm.reshape(()),
    )


def solution(mesh):
    split = ("dp", "outer")
    share = P(split)
    return jax.shard_map(
        per_device,
        mesh=mesh,
        in_specs=(share,) * 6 + (P(),) * 10 + (share,) * 3 + (P(),) * 3,
        out_specs=(share,) * 3 + (P(),) * 10 + (share,) * 3 + (P(),) * 4,
        check_vma=False,
    )
```

```python
import functools
import math

import jax
import jax.numpy as jnp
from jax import lax
from jax.experimental import pallas as pl
from jax.experimental.pallas import tpu as pltpu
from jax.sharding import PartitionSpec as P

HEAD = 64
TOK = 256
GROUP = 2
PART = 64
ONES = 16

NORM_EPSILON = 1e-06
UNIT_EPSILON = 1e-06
SCORE_SCALE = 20.0
MOMENTUM_DECAY = 0.9
LEARNING_RATE = 10.0
CLIP_NORM = 2.0
MASKED_SCORE = -1e30
HIGHEST = lax.Precision.HIGHEST
AXES = ("dp", "outer")
F32 = jnp.float32
BF16 = jnp.bfloat16
VMEM_LIMIT = 56 << 20
FORWARD_VMEM = 20 << 20
BACKWARD_VMEM = 20 << 20
SEND = BF16


def mm(a, b, precision=None):
    return lax.dot_general(a, b, (((1,), (0,)), ((), ())), precision=precision, preferred_element_type=F32)


def mm_nt(a, b, precision=None):
    return lax.dot_general(a, b, (((1,), (1,)), ((), ())), precision=precision, preferred_element_type=F32)


def mm_tn(a, b, precision=None):
    return lax.dot_general(a, b, (((0,), (0,)), ((), ())), precision=precision, preferred_element_type=F32)


def wide(column):
    return jnp.concatenate([column] * (GROUP * TOK // 128), axis=1)


def split_two(v):
    high = v.astype(BF16)
    return high, (v - high.astype(F32)).astype(BF16)


def split_three(v):
    high = v.astype(BF16)
    rest = v - high.astype(F32)
    middle = rest.astype(BF16)
    return high, middle, (rest - middle.astype(F32)).astype(BF16)


def norm_columns(hidden, gain, shift):
    share = 1.0 / hidden.shape[0]
    center = hidden - jnp.sum(hidden, axis=0, keepdims=True) * share
    inverse = lax.rsqrt(jnp.sum(center * center, axis=0, keepdims=True) * share + NORM_EPSILON)
    normed = center * inverse
    return normed * gain + shift, normed, inverse


def norm_columns_back(grad, normed, inverse, gain):
    share = 1.0 / grad.shape[0]
    scaled = grad * gain
    mean = jnp.sum(scaled, axis=0, keepdims=True) * share
    along = jnp.sum(scaled * normed, axis=0, keepdims=True) * share
    return inverse * (scaled - mean - normed * along)


def gelu_and_slope(u):
    z = u * 0.5**0.5
    phi = 0.5 + 0.5 * lax.erf(z)
    return u * phi, phi + z * jnp.exp2(z * z * -math.log2(math.e)) * math.pi**-0.5


def forward_kernel(
    nqs, qlen, plen, xq, xp, attn, w_in, w_out, gains, biases, lists, counts,
    x_out, qk_out, v_out, p_out, ctx_out, n1_out, first_out, slope_out, act_out, n2_out, inv1_out, inv2_out, live_out, wqkv_out, wo_out, win_out, wout_out, pooled_out, units_out,
    wproj, wo_t, win_t, wout_t, bias_bc, gain_bc, qblk, xs, away, score_s, first_s, first_low_s, turn, pooled_s, w_in_s, w_out_s, w_sems,
):
    i = pl.program_id(0)
    steps = pl.num_programs(0) - 1
    d = xs.shape[1]
    ff = win_t.shape[0]
    heads = d // HEAD
    segs = TOK // HEAD
    span = GROUP * TOK
    late = jnp.maximum(i - 1, 0)

    def tower(group):
        return jnp.where(group < nqs, 0, 1)

    def eye():
        return (lax.broadcasted_iota(jnp.int32, (d, d), 0) == lax.broadcasted_iota(jnp.int32, (d, d), 1)).astype(F32).astype(BF16)

    def spread(at, row):
        bias_bc[at : at + d, :] = jnp.broadcast_to(row, (128, d)).T

    def feed_weights(tower_at):
        return [
            pltpu.make_async_copy(w_in.at[tower_at], w_in_s, w_sems.at[0]),
            pltpu.make_async_copy(w_out.at[tower_at], w_out_s, w_sems.at[1]),
        ]

    @pl.when(i == 0)
    def _():
        for copy in feed_weights(0):
            copy.start()
        qblk[...] = jnp.zeros_like(qblk)

    @pl.when((i == 0) | (i == nqs))
    def _():
        one = eye()
        t = tower(i)
        for j in range(3):
            low = attn[0, j].astype(BF16)
            wqkv_out[t, :, j * d : (j + 1) * d] = low
            wproj[j * d : (j + 1) * d, :] = mm_nt(one, low).astype(BF16)
            if j:
                wproj[(3 + j) * d : (4 + j) * d, :] = low
        wproj[3 * d : 4 * d, :] = one
        low = attn[0, 3].astype(BF16)
        wo_out[t] = low
        wo_t[...] = mm_nt(one, low).astype(BF16)
        for c in range(4):
            spread(c * d, biases[pl.ds(t, 1), c * d : (c + 1) * d])
        gain_bc[0:d, :] = jnp.broadcast_to(gains[t, 0:1, :], (128, d)).T

    @pl.when((i == 1) | (i == nqs + 1))
    def _():
        one = eye()
        t = tower(late)
        for copy in feed_weights(t):
            copy.wait()
        for c in range(ff // d):
            at = slice(c * d, (c + 1) * d)
            low = w_in_s[:, at].astype(BF16)
            win_out[t, :, at] = low
            win_t[at, :] = mm_nt(one, low).astype(BF16)
            low = w_out_s[at, :].astype(BF16)
            wout_out[t, at, :] = low
            wout_t[:, at] = mm_nt(one, low).astype(BF16)
        for c in range(4, bias_bc.shape[0] // d):
            spread(c * d, biases[pl.ds(t, 1), c * d : (c + 1) * d])
        gain_bc[d : 2 * d, :] = jnp.broadcast_to(gains[t, 1:2, :], (128, d)).T

        @pl.when(i == 1)
        def _():
            for copy in feed_weights(1):
                copy.start()

    @pl.when(i < nqs)
    def _():
        xs[...] = xq[...].reshape(span, d)

    @pl.when(i >= nqs)
    def _():
        xs[...] = xp[...].reshape(span, d)

    def length_of(group, u, segment):
        base = (jnp.minimum(group, nqs - 1) * GROUP + u) * segs
        out = jnp.full(segment.shape, qlen[base + segs - 1], jnp.int32)
        for s in range(segs - 1):
            out = jnp.where(segment == s, qlen[base + s], out)
        return jnp.where(group < nqs, out, plen[jnp.clip(group - nqs, 0, steps - nqs - 1) * GROUP + u])

    def dead_keys(u, place):
        row = lax.broadcasted_iota(jnp.int32, (TOK, 1), 0)
        return place(row) >= length_of(i, u, row // HEAD)

    @pl.when(i < nqs)
    def _():
        key = lax.broadcasted_iota(jnp.int32, (TOK, TOK), 0)
        ask = lax.broadcasted_iota(jnp.int32, (TOK, TOK), 1)
        for u in range(GROUP):
            dead = dead_keys(u, lambda row: row % HEAD) | ((key // HEAD) != (ask // HEAD))
            away[u] = jnp.where(dead, MASKED_SCORE, 0.0)

    @pl.when((i >= nqs) & (i < steps))
    def _():
        for u in range(GROUP):
            away[u] = jnp.broadcast_to(jnp.where(dead_keys(u, lambda row: row), MASKED_SCORE, 0.0), (TOK, TOK))

    def bias(at, size):
        return wide(bias_bc[at : at + size, :])

    def attention_parts():
        x = xs[...]
        q_t = (mm_nt(wproj[0:d, :], x) + bias(0, d)).astype(BF16) * BF16(HEAD**-0.5)
        qk_out[i, 0:d, :] = q_t
        for u in range(GROUP):
            for h in range(heads):
                piece = q_t[h * HEAD : (h + 1) * HEAD, u * TOK : (u + 1) * TOK]
                qblk[u, h * HEAD : (h + 1) * HEAD, h * TOK : (h + 1) * TOK] = piece
        k_row = mm(x, wproj[4 * d : 5 * d, :]).astype(BF16)
        yield
        v_t = (mm_nt(wproj[2 * d : 3 * d, :], x) + bias(d, d)).astype(BF16)
        for u in range(GROUP):
            for h in range(heads):
                score_s[u, h] = mm(k_row[u * TOK : (u + 1) * TOK, :], qblk[u, :, h * TOK : (h + 1) * TOK])
            yield
        qk_out[i, d : 2 * d, :] = mm_nt(wproj[d : 2 * d, :], x).astype(BF16) * BF16(HEAD**-0.5)
        v_out[i] = (mm(x, wproj[5 * d : 6 * d, :]) + biases[pl.ds(tower(i), 1), d : 2 * d]).astype(BF16)
        x_t = mm_nt(wproj[3 * d : 4 * d, :], x)
        x_out[i, 0:d, :] = x_t.astype(BF16)
        yield
        for u in range(GROUP):
            for h in range(heads):
                scores = score_s[u, h] + away[u]
                exponent = jnp.exp(scores - jnp.max(scores, axis=0, keepdims=True))
                probs = exponent * (1.0 / jnp.sum(exponent, axis=0, keepdims=True))
                p_out[i, u, h] = probs.astype(BF16)
                at = slice(h * HEAD, (h + 1) * HEAD)
                over = slice(u * TOK, (u + 1) * TOK)
                ctx_out[i, at, over] = mm(v_t[at, over], p_out[i, u, h]).astype(BF16)
                if h % 2:
                    yield
        hidden = x_t + (mm(wo_t[...], ctx_out[i, 0:d, :]) + bias(2 * d, d))
        first, n1, inv1 = norm_columns(hidden, wide(gain_bc[0:d, :]), bias(3 * d, d))
        n1_out[i] = n1
        inv1_out[i] = jnp.broadcast_to(inv1, (8, span))
        ones = jnp.ones((ONES, span), BF16)
        x_out[i, d:, :] = ones
        ctx_out[i, d:, :] = ones
        first_out[i, d:, :] = ones
        yield
        first_low = first.astype(BF16)
        first_out[i, 0:d, :] = first_low
        first_low_s[...] = first_low
        first_s[...] = first

    def feed_parts():
        is_q = late < nqs
        first_low = first_low_s[...]
        hidden = first_s[...] + bias(4 * d, d)
        for c in range(ff // d):
            at = slice(c * d, (c + 1) * d)
            for half in range(2):
                rows = slice(c * d + half * (d // 2), c * d + (half + 1) * (d // 2))
                upper = mm(win_t[rows, :], first_low) + bias(6 * d + rows.start, d // 2)
                active, slope = gelu_and_slope(upper)
                slope_out[late, rows, :] = slope
                act_out[late, rows, :] = active.astype(BF16)
                yield
        hidden = hidden + mm(wout_t[...], act_out[late, 0:ff, :])
        second, n2, inv2 = norm_columns(hidden, wide(gain_bc[d : 2 * d, :]), bias(5 * d, d))
        n2_out[late] = n2
        inv2_out[late] = jnp.broadcast_to(inv2, (8, span))
        act_out[late, ff:, :] = jnp.ones((ONES, span), BF16)
        second_high, second_low = split_two(second)
        row = lax.broadcasted_iota(jnp.int32, (16, TOK), 0)
        token = lax.broadcasted_iota(jnp.int32, (16, TOK), 1)
        owner = jnp.where(is_q, token // HEAD, 0)
        place = jnp.where(is_q, token % HEAD, token)
        seg_row = lax.broadcasted_iota(jnp.int32, (16, 1), 0)
        for u in range(GROUP):
            over = slice(u * TOK, (u + 1) * TOK)
            live = ((place < length_of(late, u, token // HEAD)) & (row == owner)).astype(F32).astype(BF16)
            live_out[late, :, over] = live
            pooled = mm_nt(live, second_high[:, over]) + mm_nt(live, second_low[:, over])
            pooled_s[late * GROUP + u] = pooled / length_of(late, u, seg_row).astype(F32)

    def in_turn(*kinds):
        running = [kind() for kind in kinds]
        while running:
            running = [parts for parts in running if next(parts, running) is not running]

    @pl.when(i == 0)
    def _():
        in_turn(attention_parts)

    @pl.when((i > 0) & (i < steps))
    def _():
        in_turn(attention_parts, feed_parts)

    @pl.when(i == steps)
    def _():
        in_turn(feed_parts)
        for u in range(nqs * GROUP):
            pooled_out[u * segs : (u + 1) * segs, :] = pooled_s[u, 0:segs, :]
        for u in range(pooled_s.shape[0] - nqs * GROUP):
            at = nqs * GROUP * segs + u
            pooled_out[at : at + 1, :] = pooled_s[nqs * GROUP + u, 0:1, :]
        rows = pooled_out[...]
        unit = rows * lax.rsqrt(jnp.sum(rows * rows, axis=1, keepdims=True) + UNIT_EPSILON)
        slots, own = lists.shape
        turn[...] = jnp.zeros_like(turn)
        turn[0:slots, 0:own] = (lists[...] // PART).astype(F32)
        turn[slots : 2 * slots, 0:own] = (lists[...] % PART).astype(F32)
        turn[2 * slots : 2 * slots + 1, 0:own] = counts[...].astype(F32)
        extra = turn[...].T[0:own, :]
        sent = jnp.concatenate([unit[:, c * 128 : (c + 1) * 128] for c in range(d // 128)] + [extra], axis=0)
        units_out[0] = sent.astype(BF16)


def step_spec(*shape):
    return pl.BlockSpec((1,) + shape, lambda i, *_: (i,) + (0,) * len(shape))


def tower_spec(nqs, *shape):
    return pl.BlockSpec((1,) + shape, lambda i, *_: (jnp.where(i < nqs, 0, 1),) + (0,) * len(shape))


def whole_spec(*shape):
    return pl.BlockSpec(shape, lambda i, *_: (0,) * len(shape))


def forward(q_lengths, p_lengths, xq, xp, attn, w_in, w_out, gains, biases, positives, counts):
    nqs, nps = xq.shape[0] // GROUP, xp.shape[0] // GROUP
    steps = nqs + nps
    span = GROUP * TOK
    d, ff = w_in.shape[1:]
    heads = d // HEAD
    seqs = q_lengths.shape[0] + xp.shape[0]
    sent = seqs * d // 128 + positives.shape[1]
    early = [
        ((d + ONES, span), BF16),
        ((2 * d, span), BF16),
        ((span, d), BF16),
        ((GROUP, heads, TOK, TOK), BF16),
        ((d + ONES, span), BF16),
        ((d, span), F32),
        ((d + ONES, span), BF16),
    ]
    later = [((ff, span), F32), ((ff + ONES, span), BF16), ((d, span), F32)]
    rows = [((8, span), F32), ((8, span), F32), ((16, span), BF16)]
    outs = early + later + rows

    kept = [pltpu.VMEM((steps,) + shape, kind) for shape, kind in outs]
    kept += [pltpu.VMEM((2,) + shape, BF16) for shape in ((d, 3 * d), (d, d), (d, ff), (ff, d))]
    kept += [pltpu.VMEM((seqs, d), F32)]
    direct = pl.BlockSpec(memory_space=pltpu.VMEM)
    return pl.pallas_call(
        functools.partial(forward_kernel, nqs),
        grid_spec=pltpu.PrefetchScalarGridSpec(
            num_scalar_prefetch=2,
            grid=(steps + 1,),
            in_specs=[
                pl.BlockSpec((GROUP, TOK, d), lambda i, *_: (jnp.minimum(i, nqs - 1), 0, 0)),
                pl.BlockSpec((GROUP, TOK, d), lambda i, *_: (jnp.clip(i - nqs, 0, nps - 1), 0, 0)),
                tower_spec(nqs, 4, d, d),
                pl.BlockSpec(memory_space=pl.ANY),
                pl.BlockSpec(memory_space=pl.ANY),
                whole_spec(2, 2, d),
                whole_spec(2, biases.shape[1]),
                whole_spec(*positives.shape),
                whole_spec(1, positives.shape[1]),
            ],
            out_specs=[direct] * (len(kept) + 1),
            scratch_shapes=[
                pltpu.VMEM((6 * d, d), BF16),
                pltpu.VMEM((d, d), BF16),
                pltpu.VMEM((ff, d), BF16),
                pltpu.VMEM((d, ff), BF16),
                pltpu.VMEM((biases.shape[1], 128), F32),
                pltpu.VMEM((2 * d, 128), F32),
                pltpu.VMEM((GROUP, d, heads * TOK), BF16),
                pltpu.VMEM((span, d), BF16),
                pltpu.VMEM((GROUP, TOK, TOK), F32),
                pltpu.VMEM((GROUP, heads, TOK, TOK), F32),
                pltpu.VMEM((d, span), F32),
                pltpu.VMEM((d, span), BF16),
                pltpu.VMEM((128, 128), F32),
                pltpu.VMEM((steps * GROUP, 16, d), F32),
                pltpu.VMEM((d, ff), F32),
                pltpu.VMEM((ff, d), F32),
                pltpu.SemaphoreType.DMA((2,)),
            ],
        ),
        out_shape=kept + [jax.ShapeDtypeStruct((1, sent, 128), BF16)],
        compiler_params=pltpu.CompilerParams(vmem_limit_bytes=FORWARD_VMEM),
        name="forward",
    )(q_lengths, p_lengths, xq, xp, attn, w_in, w_out, gains, biases, positives, counts)


def contrast_kernel(
    nqu, slots, dp, outer, qlen, plen, near, far, pooled, loss_out, gp_out, low_rows, gup_rows, gp_rows, turn
):
    devices = dp * outer
    seqs, d = pooled.shape
    own = qlen.shape[0]
    pown = seqs - own
    both = jnp.concatenate([near[...], far[...]], axis=0).astype(F32)
    parts = range(0, seqs * d // 128, seqs)
    uq = jnp.concatenate([both[:, at : at + own, :] for at in parts], axis=2).reshape(devices * own, d).astype(BF16)
    up = jnp.concatenate([both[:, at + own : at + seqs, :] for at in parts], axis=2).reshape(devices * pown, d).astype(BF16)
    lists = both[:, seqs * d // 128 :, :].reshape(devices * own, 128)
    scores = SCORE_SCALE * mm_nt(uq, up)
    place = lax.broadcasted_iota(jnp.int32, (1, devices * pown), 1)
    block = place // pown
    along = ((block // outer) % (dp // 2)) * 2 + block // (devices // 2)
    device = (lax.axis_index("dp") ^ along) * outer + (lax.axis_index("outer") ^ (block % outer))
    columns = (device * pown + place % pown).astype(F32)
    positive = None
    for k in range(slots):
        listed = lists[:, k : k + 1] * PART + lists[:, slots + k : slots + k + 1]
        hit = (listed == columns) & (lists[:, 2 * slots : 2 * slots + 1] > k)
        positive = hit if positive is None else positive | hit
    highest = jnp.max(scores, axis=1, keepdims=True)
    whole = highest + jnp.log(jnp.sum(jnp.exp(scores - highest), axis=1, keepdims=True))
    chosen = jnp.where(positive, scores, MASKED_SCORE)
    top = jnp.max(chosen, axis=1, keepdims=True)
    within = top + jnp.log(jnp.sum(jnp.exp(chosen - top), axis=1, keepdims=True))
    low = (SCORE_SCALE * (jnp.exp(scores - whole) - jnp.exp(chosen - within))).astype(BF16)
    low_rows[:, : scores.shape[1]] = low.astype(F32)
    low_rows[:, scores.shape[1] :] = jnp.broadcast_to(whole - within, (scores.shape[0], 128))
    turn[...] = jnp.zeros_like(turn)
    turn[0:own, :] = low_rows[0:own, scores.shape[1] :]
    loss_out[...] = turn[...].T[0:1, 0:own]
    grad_q = mm(low_rows[0:own, : scores.shape[1]].astype(BF16), up)
    gup_rows[...] = mm_tn(low, uq)
    grad_p = gup_rows[0:pown, :]
    grad = jnp.concatenate([grad_q, grad_p], axis=0)
    rows = pooled[...]
    inverse = lax.rsqrt(jnp.sum(rows * rows, axis=1, keepdims=True) + UNIT_EPSILON)
    grad = inverse * grad - inverse * inverse * inverse * rows * jnp.sum(rows * grad, axis=1, keepdims=True)
    segs = own // nqu
    gp_rows[...] = jnp.zeros_like(gp_rows)
    for s in range(own):
        gp_rows[s // segs, s % segs : s % segs + 1, :] = grad[s : s + 1, :] / jnp.full((1, d), qlen[s], jnp.int32).astype(F32)
    for s in range(pown):
        gp_rows[nqu + s, 0:1, :] = grad[own + s : own + s + 1, :] / jnp.full((1, d), plen[s], jnp.int32).astype(F32)
    for term, value in enumerate(split_three(gp_rows[...])):
        gp_out[:, term * 16 : (term + 1) * 16, :] = value


def contrast(nqu, npu, slots, dp, outer, q_lengths, p_lengths, near, far, pooled):
    devices = dp * outer
    seqs, d = pooled.shape
    own = q_lengths.shape[0]
    passages = devices * (seqs - own)
    vmem = pl.BlockSpec(memory_space=pltpu.VMEM)
    return pl.pallas_call(
        functools.partial(contrast_kernel, nqu, slots, dp, outer),
        in_specs=[pl.BlockSpec(memory_space=pltpu.SMEM)] * 2 + [vmem] * 3,
        out_specs=[vmem, vmem],
        out_shape=[jax.ShapeDtypeStruct((1, own), F32), pltpu.VMEM((nqu + npu, 48, d), BF16)],
        scratch_shapes=[
            pltpu.VMEM((devices * own, passages + 128), F32),
            pltpu.VMEM((passages, d), F32),
            pltpu.VMEM((nqu + npu, 16, d), F32),
            pltpu.VMEM((128, 128), F32),
        ],
        compiler_params=pltpu.CompilerParams(vmem_limit_bytes=min(VMEM_LIMIT, (6 << 20) + 32 * devices * own * passages)),
        name="contrast",
    )(q_lengths, p_lengths, near, far, pooled)


def left_rows(start_t, matrix):
    s_high, s_low = split_two(start_t)
    m_high, m_low = split_two(matrix)
    both = mm_nt(jnp.concatenate([s_high, s_low], axis=0), m_high)
    return both[:8] + both[8:] + mm_nt(jnp.concatenate([s_high, s_high], axis=0), m_low)[:8]


def right_rows(basis, matrix):
    b_high, b_low = split_two(basis)
    m_high, m_low = split_two(matrix)
    both = mm(jnp.concatenate([b_high, b_low], axis=0), m_high)
    return both[:8] + both[8:] + mm(jnp.concatenate([b_high, b_high], axis=0), m_low)[:8]


def own_core():
    return lax.axis_index("dp") % 2


def part_halves(core, whole, mine, other):
    half = whole.shape[1] // 2
    for c in range(2):

        @pl.when(core == c)
        def _(c=c):
            mine[...] = whole[:, c * half : (c + 1) * half]
            other[...] = whole[:, (1 - c) * half : (2 - c) * half]


def join_halves(core, whole, mine, other):
    half = whole.shape[1] // 2
    for c in range(2):

        @pl.when(core == c)
        def _(c=c):
            whole[:, c * half : (c + 1) * half] = mine[...]
            whole[:, (1 - c) * half : (2 - c) * half] = other[...]


def backward_kernel(
    nqs, gp, x_in, qk_in, v_in, p_in, ctx_in, n1_in, first_in, slope_in, act_in, n2_in, inv1_in, inv2_in, live_in,
    wqkv, wo, win, wout, gains, attn_err, in_err, out_err, attn_start, in_start, out_start,
    qgrad, pgrad, attn_m, in_m, out_m, left_mine, left_other,
    left, gain_bc, gz, up_s, gp_s, graw_s, gqkv, acc_qkv, acc_o, acc_in, acc_out, acc_gain, err_sems,
):
    i = pl.program_id(0)
    last = pl.num_programs(0) - 1
    is_q = i < nqs
    t = jnp.where(is_q, 0, 1)
    d = wo.shape[1]
    ff = wout.shape[1]
    errors = [
        pltpu.make_async_copy(source.at[0, tower], target.at[tower], err_sems.at[tower, k])
        for tower in range(2)
        for k, (source, target) in enumerate(((attn_err, attn_m), (in_err, in_m), (out_err, out_m)))
    ]
    heads = d // HEAD
    span = GROUP * TOK

    @pl.when(i == 0)
    def _():
        for copy in errors:
            copy.start()
        gz[...] = jnp.zeros_like(gz)

    @pl.when((i == 0) | (i == nqs))
    def _():
        for c in range(2):
            row = gains[t, c : c + 1, :]
            gain_bc[c * d : (c + 1) * d, :] = jnp.broadcast_to(row, (128, d)).T
        acc_qkv[...] = jnp.zeros_like(acc_qkv)
        acc_o[...] = jnp.zeros_like(acc_o)
        acc_in[...] = jnp.zeros_like(acc_in)
        acc_out[...] = jnp.zeros_like(acc_out)
        acc_gain[...] = jnp.zeros_like(acc_gain)

    def add_gain(at, value):
        total = value[:, :128]
        for c in range(1, span // 128):
            total = total + value[:, c * 128 : (c + 1) * 128]
        acc_gain[at * d : (at + 1) * d, :] += total

    pieces = []
    for u in range(GROUP):
        live = live_in[i, :, u * TOK : (u + 1) * TOK]
        pieces.append(mm_tn(gp[i * GROUP + u], jnp.concatenate([live, live, live], axis=0)))
    grad_second = jnp.concatenate(pieces, axis=1)
    n2 = n2_in[i]
    grad_two = norm_columns_back(grad_second, n2, inv2_in[i, 0:1, :], wide(gain_bc[d : 2 * d, :]))
    down_low = grad_two.astype(BF16)
    grad_first = grad_two
    for c in range(ff // d):
        at = slice(c * d, (c + 1) * d)
        up_low = (mm(wout[t, at, :], down_low) * slope_in[i, at, :]).astype(BF16)
        up_s[at, :] = up_low
    add_gain(1, grad_second * n2)
    add_gain(3, grad_second)
    acc_in[...] += mm_nt(first_in[i], up_s[...])
    grad_first = grad_two + mm(win[t], up_s[...])
    n1 = n1_in[i]
    grad_one = norm_columns_back(grad_first, n1, inv1_in[i, 0:1, :], wide(gain_bc[0:d, :]))
    branch_low = grad_one.astype(BF16)
    grad_context = mm(wo[t], branch_low).astype(BF16)
    for u in range(GROUP):
        for h in range(heads):
            at = slice(h * HEAD, (h + 1) * HEAD)
            gz[u, at, h * TOK : (h + 1) * TOK] = grad_context[at, u * TOK : (u + 1) * TOK]
    for u in range(GROUP):
        for h in range(heads):
            gp_s[u, h] = mm(v_in[i, u * TOK : (u + 1) * TOK, :], gz[u, :, h * TOK : (h + 1) * TOK])
    acc_out[...] += mm_nt(act_in[i], down_low)
    add_gain(0, grad_first * n1)
    add_gain(2, grad_first)
    acc_o[...] += mm_nt(ctx_in[i], branch_low)
    for u in range(GROUP):
        for h in range(heads):
            probs = p_in[i, u, h].astype(F32)
            grad_probs = gp_s[u, h]
            inner = jnp.sum(grad_probs * probs, axis=0, keepdims=True)
            graw_s[u, h] = (probs * (grad_probs - inner)).astype(BF16)
    for u in range(GROUP):
        over = slice(u * TOK, (u + 1) * TOK)
        for h in range(heads):
            at = slice(h * HEAD, (h + 1) * HEAD)
            later = slice(d + h * HEAD, d + (h + 1) * HEAD)
            last_at = slice(2 * d + h * HEAD, 2 * d + (h + 1) * HEAD)
            gqkv[last_at, over] = mm_nt(grad_context[at, over], p_in[i, u, h]).astype(BF16)
            gqkv[at, over] = mm(qk_in[i, later, over], graw_s[u, h]).astype(BF16)
            gqkv[later, over] = mm_nt(qk_in[i, at, over], graw_s[u, h]).astype(BF16)
    acc_qkv[...] += mm_nt(x_in[i], gqkv[...])
    result = (grad_one + mm(wqkv[t], gqkv[...])).T.reshape(GROUP, TOK, d)

    @pl.when(is_q)
    def _():
        qgrad[...] = result

    @pl.when(jnp.logical_not(is_q))
    def _():
        pgrad[...] = result

    @pl.when((i == nqs - 1) | (i == last))
    def _():
        for tower in range(2):

            @pl.when(t == tower)
            def _(tower=tower):
                for copy in errors[3 * tower : 3 * tower + 3]:
                    copy.wait()

        base_in = 8 * d
        base_out = base_in + 2 * d
        base_vec = base_out + 2 * ff
        for j in range(4):
            grad = acc_o[0:d, :] if j == 3 else acc_qkv[0:d, j * d : (j + 1) * d]
            merged = grad + attn_m[t, j]
            attn_m[t, j] = merged
            left[:, pl.ds(pl.multiple_of((t * 4 + j) * d, 128), d)] = left_rows(attn_start[t, j], merged)
        merged = acc_in[0:d, :] + in_m[t]
        in_m[t] = merged
        left[:, pl.ds(pl.multiple_of(base_in + t * d, 128), d)] = left_rows(in_start[t], merged)
        merged = acc_out[0:ff, :] + out_m[t]
        out_m[t] = merged
        left[:, pl.ds(pl.multiple_of(base_out + t * ff, 128), ff)] = left_rows(out_start[t], merged)
        sums = mm_nt(jnp.ones((8, 128), F32), acc_gain[...], HIGHEST)

        def vectors():
            yield sums[0:1, 0:d]
            yield sums[0:1, d : 2 * d]
            yield acc_qkv[d : d + 1, 0:d]
            yield acc_qkv[d : d + 1, 2 * d : 3 * d]
            yield acc_o[d : d + 1, :]
            yield sums[0:1, 2 * d : 3 * d]
            yield acc_out[ff : ff + 1, :]
            yield sums[0:1, 3 * d : 4 * d]
            for c in range(ff // d):
                yield acc_in[d : d + 1, c * d : (c + 1) * d]

        for tower in range(2):

            @pl.when(t == tower)
            def _(tower=tower):
                for v, vector in enumerate(vectors()):
                    at = tower * 12 + v
                    left[at // 3 : at // 3 + 1, base_vec + (at % 3) * d : base_vec + (at % 3 + 1) * d] = vector

    @pl.when(i == last)
    def _():
        part_halves(own_core(), left, left_mine, left_other)


def backward(nqs, nps, gp, saved, low_weights, gains, errors, starts):
    steps = nqs + nps
    nqu, npu = nqs * GROUP, nps * GROUP
    span = GROUP * TOK
    d, ff = errors[1].shape[2:]
    heads = d // HEAD
    width = 8 * d + 2 * d + 2 * ff + 3 * d
    direct = pl.BlockSpec(memory_space=pltpu.VMEM)
    far = pl.BlockSpec(memory_space=pl.ANY)
    return pl.pallas_call(
        functools.partial(backward_kernel, nqs),
        grid=(steps,),
        in_specs=[direct] * (len(saved) + 6) + [far] * 3 + [direct] * 3,
        out_specs=[
            pl.BlockSpec((GROUP, TOK, d), lambda i: (jnp.minimum(i, nqs - 1), 0, 0)),
            pl.BlockSpec((GROUP, TOK, d), lambda i: (jnp.maximum(i - nqs, 0), 0, 0)),
        ]
        + [direct] * 5,
        out_shape=[
            jax.ShapeDtypeStruct((nqu, TOK, d), F32),
            jax.ShapeDtypeStruct((npu, TOK, d), F32),
            pltpu.VMEM((2, 4, d, d), F32),
            pltpu.VMEM((2, d, ff), F32),
            pltpu.VMEM((2, ff, d), F32),
            jax.ShapeDtypeStruct((8, width // 2), F32),
            jax.ShapeDtypeStruct((8, width // 2), F32),
        ],
        scratch_shapes=[
            pltpu.VMEM((8, width), F32),
            pltpu.VMEM((2 * d, 128), F32),
            pltpu.VMEM((GROUP, d, heads * TOK), BF16),
            pltpu.VMEM((ff, span), BF16),
            pltpu.VMEM((GROUP, heads, TOK, TOK), F32),
            pltpu.VMEM((GROUP, heads, TOK, TOK), BF16),
            pltpu.VMEM((3 * d, span), BF16),
            pltpu.VMEM((d + ONES, 3 * d), F32),
            pltpu.VMEM((d + ONES, d), F32),
            pltpu.VMEM((d + ONES, ff), F32),
            pltpu.VMEM((ff + ONES, d), F32),
            pltpu.VMEM((4 * d, 128), F32),
            pltpu.SemaphoreType.DMA((2, 3)),
        ],
        compiler_params=pltpu.CompilerParams(vmem_limit_bytes=BACKWARD_VMEM),
        name="backward",
    )(gp, *saved, *low_weights, gains, *errors, *starts)


def gram(rows):
    terms = split_three(rows)
    high, middle, low = terms
    left = jnp.concatenate([high, high, middle, high, middle, low], axis=1)
    right = jnp.concatenate([high, middle, high, low, middle, high], axis=1)
    return mm_nt(left, right)


def right_kernel(
    left_mine, left_other, attn_m, in_m, out_m, attn_mom, in_mom, out_mom,
    basis, right_mine, right_other, vector, grams, attn_held, in_held, out_held, left, right, sems,
):
    moments = [
        pltpu.make_async_copy(source, target, sems.at[k])
        for k, (source, target) in enumerate(((attn_mom, attn_held), (in_mom, in_held), (out_mom, out_held)))
    ]
    for copy in moments:
        copy.start()
    d, ff = in_m.shape[1:]
    core = own_core()
    join_halves(core, left, left_mine, left_other)
    vector[...] = left[:, 10 * d + 2 * ff :]
    places = [(j * d, d) for j in range(8)] + [(8 * d + t * d, d) for t in range(2)] + [(10 * d + t * ff, ff) for t in range(2)]
    blocks = [left[:, at : at + size] for at, size in places]
    for j in range(8):
        for b, block in enumerate(blocks):
            order = lax.broadcasted_iota(jnp.int32, (8, 1), 0)
            column = block[j : j + 1, :]
            dots = jnp.sum(block * column, axis=1, keepdims=True)
            scale = lax.rsqrt(dots[j : j + 1, :] + 1e-06)
            unit = column * scale
            step = jnp.where(order > j, dots * scale, 0.0)
            blocks[b] = jnp.where(order == j, unit, block - step * unit)
    for k, ((at, size), block) in enumerate(zip(places, blocks)):
        basis[:, at : at + size] = block
        grams[k] = gram(block)
    for j in range(8):
        right[:, j * d : (j + 1) * d] = right_rows(blocks[j], attn_m[j // 4, j % 4])
    for t in range(2):
        right[:, 8 * d + t * ff : 8 * d + (t + 1) * ff] = right_rows(blocks[8 + t], in_m[t])
        right[:, 8 * d + 2 * ff + t * d : 8 * d + 2 * ff + (t + 1) * d] = right_rows(blocks[10 + t], out_m[t])
    part_halves(core, right, right_mine, right_other)
    for copy in moments:
        copy.wait()


def right_factors(left_mine, left_other, merged, moments):
    d, ff = merged[1].shape[1:]
    vmem = pl.BlockSpec(memory_space=pltpu.VMEM)
    width = 10 * d + 2 * ff
    rows = functools.partial(jax.ShapeDtypeStruct, dtype=F32)
    return pl.pallas_call(
        right_kernel,
        in_specs=[vmem] * 5 + [pl.BlockSpec(memory_space=pl.ANY)] * 3,
        out_specs=[vmem] * 8,
        out_shape=[rows((8, width)), rows((8, width // 2)), rows((8, width // 2)), rows((8, 3 * d)), rows((12, 8, 8))]
        + [pltpu.VMEM(a.shape, F32) for a in moments],
        scratch_shapes=[pltpu.VMEM((8, width + 3 * d), F32), pltpu.VMEM((8, width), F32), pltpu.SemaphoreType.DMA((3,))],
        compiler_params=pltpu.CompilerParams(vmem_limit_bytes=12 << 20),
        name="right",
    )(left_mine, left_other, *merged, *(pltpu.with_memory_space_constraint(a, pltpu.HBM) for a in moments))


def update_kernel(
    replicas, basis, right_mine, right_other, vector, grams, gains, biases, gain_mom, bias_mom,
    attn_m, in_m, out_m, attn, w_in, w_out, attn_mom, in_mom, out_mom,
    attn_new, in_new, out_new, attn_mom_new, in_mom_new, out_mom_new, attn_err, in_err, out_err,
    gains_new, biases_new, gain_mom_new, bias_mom_new, attn_factor, in_factor, out_factor, norm_out,
    right, clip_s,
):
    i = pl.program_id(0)
    d, ff = w_in.shape[1:]
    t, c = i // 4, i % 4

    @pl.when(i == 0)
    def _():
        join_halves(own_core(), right, right_mine, right_other)
        for j in range(8):
            attn_factor[j // 4, j % 4] = right[:, j * d : (j + 1) * d]
        for s in range(2):
            in_factor[s] = right[:, 8 * d + s * ff : 8 * d + (s + 1) * ff]
            out_factor[s] = right[:, 8 * d + 2 * ff + s * d : 8 * d + 2 * ff + (s + 1) * d]
        places = [(j * d, d) for j in range(8)]
        places += [(8 * d + s * ff, ff) for s in range(2)] + [(8 * d + 2 * ff + s * d, d) for s in range(2)]
        total = jnp.zeros((8, 8), F32)
        for k, (at, size) in enumerate(places):
            total = total + grams[k] * gram(right[:, at : at + size])
        sums = vector[...]
        square = jnp.sum(jnp.sum(total, axis=1, keepdims=True), axis=0, keepdims=True)
        square = square + jnp.sum(jnp.sum(sums * sums, axis=1, keepdims=True), axis=0, keepdims=True)
        norm = jnp.sqrt(jnp.broadcast_to(square, (8, 128)))
        norm_out[0] = norm[0, 0]
        clip_s[...] = jnp.minimum(1.0, CLIP_NORM / norm)
        held = clip_s[0:1, 0:1]
        for s in range(2):
            for v in range(12):
                at = s * 12 + v
                reduced = vector[at // 3 : at // 3 + 1, (at % 3) * d : (at % 3 + 1) * d]
                if v < 2:
                    moved = MOMENTUM_DECAY * gain_mom[s, v : v + 1, :] + held * reduced
                    gain_mom_new[s, v : v + 1, :] = moved
                    gains_new[s, v : v + 1, :] = gains[s, v : v + 1, :] - LEARNING_RATE * moved
                else:
                    over = slice((v - 2) * d, (v - 1) * d)
                    moved = MOMENTUM_DECAY * bias_mom[s : s + 1, over] + held * reduced
                    bias_mom_new[s : s + 1, over] = moved
                    biases_new[s : s + 1, over] = biases[s : s + 1, over] - LEARNING_RATE * moved

    clip = clip_s[0:1, 0:1]

    def step(b_at, r_at, merged, weight, moment, weight_new, moment_new, error):
        b1, b2, b3 = split_three(basis[:, pl.ds(pl.multiple_of(b_at, 128), d)])
        r1, r2, r3 = split_three(right[:, pl.ds(pl.multiple_of(r_at, 128), d)])
        approx = mm_tn(jnp.concatenate([b1, b1, b2, b1, b2, b3], axis=0), jnp.concatenate([r1, r2, r1, r3, r2, r1], axis=0))
        moved = MOMENTUM_DECAY * moment + clip * approx
        moment_new[...] = moved.reshape(moment_new.shape)
        weight_new[...] = (weight - LEARNING_RATE * moved).reshape(weight_new.shape)
        error[...] = (merged - approx * (1.0 / replicas)).reshape(error.shape)

    across = pl.ds(pl.multiple_of(c * d, 128), d)
    step(i * d, i * d, attn_m[t, c], attn[t, c], attn_mom[t, c], attn_new, attn_mom_new, attn_err)
    step((8 + t) * d, 8 * d + t * ff + c * d, in_m[t, :, across], w_in[t, :, across], in_mom[t, :, across], in_new, in_mom_new, in_err)
    step(10 * d + t * ff + c * d, 8 * d + 2 * ff + t * d, out_m[t, across, :], w_out[t, across, :], out_mom[t, across, :], out_new, out_mom_new, out_err)


def update(replicas, basis, right_mine, right_other, vector, grams, gains, biases, gain_mom, bias_mom, merged, weights, moments):
    d, ff = weights[1].shape[1:]
    a_spec = pl.BlockSpec((1, 1, d, d), lambda i: (i // 4, i % 4, 0, 0))
    i_spec = pl.BlockSpec((1, d, d), lambda i: (i // 4, 0, i % 4))
    o_spec = pl.BlockSpec((1, d, d), lambda i: (i // 4, i % 4, 0))
    ae_spec = pl.BlockSpec((1, 1, 1, d, d), lambda i: (0, i // 4, i % 4, 0, 0))
    ie_spec = pl.BlockSpec((1, 1, d, d), lambda i: (0, i // 4, 0, i % 4))
    oe_spec = pl.BlockSpec((1, 1, d, d), lambda i: (0, i // 4, i % 4, 0))
    rows = functools.partial(jax.ShapeDtypeStruct, dtype=F32)
    small = (basis, right_mine, right_other, vector, grams, gains, biases, gain_mom, bias_mom)
    direct = pl.BlockSpec(memory_space=pltpu.VMEM)
    finals = [gains.shape, biases.shape] * 2 + [(2, 4, 8, d), (2, 8, ff), (2, 8, d)]
    return pl.pallas_call(
        functools.partial(update_kernel, replicas),
        grid=(8,),
        in_specs=[direct] * (len(small) + 9),
        out_specs=[a_spec, i_spec, o_spec] * 2
        + [ae_spec, ie_spec, oe_spec]
        + [whole_spec(*shape) for shape in finals]
        + [pl.BlockSpec(memory_space=pltpu.SMEM)],
        out_shape=[rows(a.shape) for a in weights * 2]
        + [rows((1,) + a.shape) for a in weights]
        + [rows(shape) for shape in finals]
        + [rows((1,))],
        scratch_shapes=[pltpu.VMEM(basis.shape, F32), pltpu.VMEM((8, 128), F32)],
        compiler_params=pltpu.CompilerParams(vmem_limit_bytes=14 << 20),
        name="update",
    )(*small, *merged, *weights, *moments)


def in_vmem(*arrays):
    return tuple(pltpu.with_memory_space_constraint(a, pltpu.VMEM) for a in arrays)


def swap_with(x, axis, mask):
    return lax.ppermute(x, axis, [(i, i ^ mask) for i in range(lax.axis_size(axis))])


def chip_steps():
    size = lax.axis_size("dp")
    if size == 8:
        return [("dp", (2, 4, 6))]
    return [("dp", (1 << b,)) for b in range(1, size.bit_length() - 1)]


def outer_step():
    return ("outer", tuple(range(1, lax.axis_size("outer"))))


def gather_blocks(x):
    for axis, masks in [outer_step()] + chip_steps():
        x = jnp.concatenate([x] + [swap_with(x, axis, mask) for mask in masks], axis=0)
    return x, swap_with(x, "dp", 1)


def sum_halves(mine, other):
    mine = mine + swap_with(other, "dp", 1)
    for axis, masks in chip_steps() + [outer_step()]:
        sent = mine.astype(SEND)
        mine = sent.astype(F32)
        for got in [swap_with(sent, axis, mask) for mask in masks]:
            mine = mine + got.astype(F32)
    return mine, swap_with(mine, "dp", 1)


def per_device(
    questions, passages, q_lengths, p_lengths, positives, pos_counts, attn, w_in, w_out, gains, biases, attn_mom, w_in_mom,
    w_out_mom, gain_mom, bias_mom, attn_err, w_in_err, w_out_err, attn_start, w_in_start, w_out_start,
):
    devices = lax.axis_size("dp") * lax.axis_size("outer")
    d, ff = w_in.shape[1:]
    xq = questions.reshape(-1, TOK, d)
    xp = passages.reshape(-1, TOK, d)
    nqu, npu = xq.shape[0], xp.shape[0]
    *saved, wqkv, wo, win, wout, pooled, units = forward(
        q_lengths, p_lengths, xq, xp, attn, w_in, w_out, gains, biases, positives.T, pos_counts.reshape(1, -1)
    )
    dp, outer = lax.axis_size("dp"), lax.axis_size("outer")
    near, far = gather_blocks(units)
    loss, gp = contrast(nqu, npu, positives.shape[1], dp, outer, q_lengths, p_lengths, *in_vmem(near, far, pooled))
    starts = [jnp.swapaxes(start, -1, -2) for start in (attn_start, w_in_start, w_out_start)]
    qgrad, pgrad, attn_m, in_m, out_m, *left = backward(
        nqu // GROUP, npu // GROUP, *in_vmem(gp), in_vmem(*saved), in_vmem(wqkv, wo, win, wout), gains,
        (attn_err, w_in_err, w_out_err), starts,
    )
    weights = (attn, w_in, w_out)
    moments = (attn_mom, w_in_mom, w_out_mom)
    merged = in_vmem(attn_m, in_m, out_m)
    basis, *right, vector, grams, mom_a, mom_b, mom_c = right_factors(*sum_halves(*left), merged, moments)
    held = in_vmem(*weights, mom_a, mom_b, mom_c)
    *new, attn_factor, in_factor, out_factor, norm = update(
        devices, basis, *sum_halves(*right), vector, grams, gains, biases, gain_mom, bias_mom,
        merged, held[:3], held[3:],
    )
    weights_new, moments_new, errors_new, vectors_new = new[:3], new[3:6], new[6:9], new[9:]
    factors = [jnp.swapaxes(factor, -1, -2) for factor in (attn_factor, in_factor, out_factor)]
    return (
        loss.reshape(-1), qgrad.reshape(questions.shape), pgrad.reshape(passages.shape),
        *weights_new, *vectors_new[:2], *moments_new, *vectors_new[2:], *errors_new, *factors, norm.reshape(()),
    )


def solution(mesh):
    split = ("dp", "outer")
    share = P(split)
    return jax.shard_map(
        per_device,
        mesh=mesh,
        in_specs=(share,) * 6 + (P(),) * 10 + (share,) * 3 + (P(),) * 3,
        out_specs=(share,) * 3 + (P(),) * 10 + (share,) * 3 + (P(),) * 4,
        check_vma=False,
    )
```

```python
import functools
import math

import jax
import jax.numpy as jnp
from jax import lax
from jax.experimental import pallas as pl
from jax.experimental.pallas import tpu as pltpu
from jax.sharding import PartitionSpec as P

HEAD = 64
TOK = 256
GROUP = 2
PART = 64
ONES = 16

NORM_EPSILON = 1e-06
UNIT_EPSILON = 1e-06
SCORE_SCALE = 20.0
MOMENTUM_DECAY = 0.9
LEARNING_RATE = 10.0
CLIP_NORM = 2.0
MASKED_SCORE = -1e30
HIGHEST = lax.Precision.HIGHEST
AXES = ("dp", "outer")
F32 = jnp.float32
BF16 = jnp.bfloat16
VMEM_LIMIT = 56 << 20
FORWARD_VMEM = 20 << 20
BACKWARD_VMEM = 20 << 20
SEND = BF16


def mm(a, b, precision=None):
    return lax.dot_general(a, b, (((1,), (0,)), ((), ())), precision=precision, preferred_element_type=F32)


def mm_nt(a, b, precision=None):
    return lax.dot_general(a, b, (((1,), (1,)), ((), ())), precision=precision, preferred_element_type=F32)


def mm_tn(a, b, precision=None):
    return lax.dot_general(a, b, (((0,), (0,)), ((), ())), precision=precision, preferred_element_type=F32)


def wide(column):
    return jnp.concatenate([column] * (GROUP * TOK // 128), axis=1)


def split_two(v):
    high = v.astype(BF16)
    return high, (v - high.astype(F32)).astype(BF16)


def split_three(v):
    high = v.astype(BF16)
    rest = v - high.astype(F32)
    middle = rest.astype(BF16)
    return high, middle, (rest - middle.astype(F32)).astype(BF16)


def norm_columns(hidden, gain, shift):
    share = 1.0 / hidden.shape[0]
    center = hidden - jnp.sum(hidden, axis=0, keepdims=True) * share
    inverse = lax.rsqrt(jnp.sum(center * center, axis=0, keepdims=True) * share + NORM_EPSILON)
    normed = center * inverse
    return normed * gain + shift, normed, inverse


def norm_columns_back(grad, normed, inverse, gain):
    share = 1.0 / grad.shape[0]
    scaled = grad * gain
    mean = jnp.sum(scaled, axis=0, keepdims=True) * share
    along = jnp.sum(scaled * normed, axis=0, keepdims=True) * share
    return inverse * (scaled - mean - normed * along)


def gelu_and_slope(u):
    z = u * 0.5**0.5
    phi = 0.5 + 0.5 * lax.erf(z)
    return u * phi, phi + z * jnp.exp2(z * z * -math.log2(math.e)) * math.pi**-0.5


def forward_kernel(
    nqs, qlen, plen, xq, xp, attn, w_in, w_out, gains, biases, lists, counts,
    x_out, qk_out, v_out, p_out, ctx_out, n1_out, first_out, slope_out, act_out, n2_out, inv1_out, inv2_out, live_out, wqkv_out, wo_out, win_out, wout_out, pooled_out, units_out,
    wproj, wo_t, win_t, wout_t, bias_bc, gain_bc, qblk, xs, away, score_s, first_s, first_low_s, turn, pooled_s, w_in_s, w_out_s, w_sems,
):
    i = pl.program_id(0)
    steps = pl.num_programs(0) - 1
    d = xs.shape[1]
    ff = win_t.shape[0]
    heads = d // HEAD
    segs = TOK // HEAD
    span = GROUP * TOK
    late = jnp.maximum(i - 1, 0)

    def tower(group):
        return jnp.where(group < nqs, 0, 1)

    def eye():
        return (lax.broadcasted_iota(jnp.int32, (d, d), 0) == lax.broadcasted_iota(jnp.int32, (d, d), 1)).astype(F32).astype(BF16)

    def spread(at, row):
        bias_bc[at : at + d, :] = jnp.broadcast_to(row, (128, d)).T

    def feed_weights(tower_at):
        return [
            pltpu.make_async_copy(w_in.at[tower_at], w_in_s, w_sems.at[0]),
            pltpu.make_async_copy(w_out.at[tower_at], w_out_s, w_sems.at[1]),
        ]

    @pl.when(i == 0)
    def _():
        for copy in feed_weights(0):
            copy.start()
        qblk[...] = jnp.zeros_like(qblk)

    @pl.when((i == 0) | (i == nqs))
    def _():
        one = eye()
        t = tower(i)
        for j in range(3):
            low = attn[0, j].astype(BF16)
            wqkv_out[t, :, j * d : (j + 1) * d] = low
            wproj[j * d : (j + 1) * d, :] = mm_nt(one, low).astype(BF16)
            if j:
                wproj[(3 + j) * d : (4 + j) * d, :] = low
        wproj[3 * d : 4 * d, :] = one
        low = attn[0, 3].astype(BF16)
        wo_out[t] = low
        wo_t[...] = mm_nt(one, low).astype(BF16)
        for c in range(4):
            spread(c * d, biases[pl.ds(t, 1), c * d : (c + 1) * d])
        gain_bc[0:d, :] = jnp.broadcast_to(gains[t, 0:1, :], (128, d)).T

    @pl.when((i == 1) | (i == nqs + 1))
    def _():
        one = eye()
        t = tower(late)
        for copy in feed_weights(t):
            copy.wait()
        for c in range(ff // d):
            at = slice(c * d, (c + 1) * d)
            low = w_in_s[:, at].astype(BF16)
            win_out[t, :, at] = low
            win_t[at, :] = mm_nt(one, low).astype(BF16)
            low = w_out_s[at, :].astype(BF16)
            wout_out[t, at, :] = low
            wout_t[:, at] = mm_nt(one, low).astype(BF16)
        for c in range(4, bias_bc.shape[0] // d):
            spread(c * d, biases[pl.ds(t, 1), c * d : (c + 1) * d])
        gain_bc[d : 2 * d, :] = jnp.broadcast_to(gains[t, 1:2, :], (128, d)).T

        @pl.when(i == 1)
        def _():
            for copy in feed_weights(1):
                copy.start()

    @pl.when(i < nqs)
    def _():
        xs[...] = xq[...].reshape(span, d)

    @pl.when(i >= nqs)
    def _():
        xs[...] = xp[...].reshape(span, d)

    def length_of(group, u, segment):
        base = (jnp.minimum(group, nqs - 1) * GROUP + u) * segs
        out = jnp.full(segment.shape, qlen[base + segs - 1], jnp.int32)
        for s in range(segs - 1):
            out = jnp.where(segment == s, qlen[base + s], out)
        return jnp.where(group < nqs, out, plen[jnp.clip(group - nqs, 0, steps - nqs - 1) * GROUP + u])

    def dead_keys(u, place):
        row = lax.broadcasted_iota(jnp.int32, (TOK, 1), 0)
        return place(row) >= length_of(i, u, row // HEAD)

    @pl.when(i < nqs)
    def _():
        key = lax.broadcasted_iota(jnp.int32, (TOK, TOK), 0)
        ask = lax.broadcasted_iota(jnp.int32, (TOK, TOK), 1)
        for u in range(GROUP):
            dead = dead_keys(u, lambda row: row % HEAD) | ((key // HEAD) != (ask // HEAD))
            away[u] = jnp.where(dead, MASKED_SCORE, 0.0)

    @pl.when((i >= nqs) & (i < steps))
    def _():
        for u in range(GROUP):
            away[u] = jnp.broadcast_to(jnp.where(dead_keys(u, lambda row: row), MASKED_SCORE, 0.0), (TOK, TOK))

    def bias(at, size):
        return wide(bias_bc[at : at + size, :])

    def attention_parts():
        x = xs[...]
        q_t = (mm_nt(wproj[0:d, :], x) + bias(0, d)).astype(BF16) * BF16(HEAD**-0.5)
        qk_out[i, 0:d, :] = q_t
        for u in range(GROUP):
            for h in range(heads):
                piece = q_t[h * HEAD : (h + 1) * HEAD, u * TOK : (u + 1) * TOK]
                qblk[u, h * HEAD : (h + 1) * HEAD, h * TOK : (h + 1) * TOK] = piece
        k_row = mm(x, wproj[4 * d : 5 * d, :]).astype(BF16)
        yield
        v_t = (mm_nt(wproj[2 * d : 3 * d, :], x) + bias(d, d)).astype(BF16)
        for u in range(GROUP):
            for h in range(heads):
                score_s[u, h] = mm(k_row[u * TOK : (u + 1) * TOK, :], qblk[u, :, h * TOK : (h + 1) * TOK])
            yield
        qk_out[i, d : 2 * d, :] = mm_nt(wproj[d : 2 * d, :], x).astype(BF16) * BF16(HEAD**-0.5)
        v_out[i] = (mm(x, wproj[5 * d : 6 * d, :]) + biases[pl.ds(tower(i), 1), d : 2 * d]).astype(BF16)
        x_t = mm_nt(wproj[3 * d : 4 * d, :], x)
        x_out[i, 0:d, :] = x_t.astype(BF16)
        yield
        for u in range(GROUP):
            for h in range(heads):
                scores = score_s[u, h] + away[u]
                exponent = jnp.exp(scores - jnp.max(scores, axis=0, keepdims=True))
                probs = exponent * (1.0 / jnp.sum(exponent, axis=0, keepdims=True))
                p_out[i, u, h] = probs.astype(BF16)
                at = slice(h * HEAD, (h + 1) * HEAD)
                over = slice(u * TOK, (u + 1) * TOK)
                ctx_out[i, at, over] = mm(v_t[at, over], p_out[i, u, h]).astype(BF16)
                if h % 2:
                    yield
        hidden = x_t + (mm(wo_t[...], ctx_out[i, 0:d, :]) + bias(2 * d, d))
        first, n1, inv1 = norm_columns(hidden, wide(gain_bc[0:d, :]), bias(3 * d, d))
        n1_out[i] = n1
        inv1_out[i] = jnp.broadcast_to(inv1, (8, span))
        ones = jnp.ones((ONES, span), BF16)
        x_out[i, d:, :] = ones
        ctx_out[i, d:, :] = ones
        first_out[i, d:, :] = ones
        yield
        first_low = first.astype(BF16)
        first_out[i, 0:d, :] = first_low
        first_low_s[...] = first_low
        first_s[...] = first

    def feed_parts():
        is_q = late < nqs
        first_low = first_low_s[...]
        hidden = first_s[...] + bias(4 * d, d)
        for c in range(ff // d):
            at = slice(c * d, (c + 1) * d)
            for half in range(2):
                rows = slice(c * d + half * (d // 2), c * d + (half + 1) * (d // 2))
                upper = mm(win_t[rows, :], first_low) + bias(6 * d + rows.start, d // 2)
                active, slope = gelu_and_slope(upper)
                slope_out[late, rows, :] = slope
                act_out[late, rows, :] = active.astype(BF16)
                yield
        hidden = hidden + mm(wout_t[...], act_out[late, 0:ff, :])
        second, n2, inv2 = norm_columns(hidden, wide(gain_bc[d : 2 * d, :]), bias(5 * d, d))
        n2_out[late] = n2
        inv2_out[late] = jnp.broadcast_to(inv2, (8, span))
        act_out[late, ff:, :] = jnp.ones((ONES, span), BF16)
        second_high, second_low = split_two(second)
        row = lax.broadcasted_iota(jnp.int32, (16, TOK), 0)
        token = lax.broadcasted_iota(jnp.int32, (16, TOK), 1)
        owner = jnp.where(is_q, token // HEAD, 0)
        place = jnp.where(is_q, token % HEAD, token)
        seg_row = lax.broadcasted_iota(jnp.int32, (16, 1), 0)
        for u in range(GROUP):
            over = slice(u * TOK, (u + 1) * TOK)
            live = ((place < length_of(late, u, token // HEAD)) & (row == owner)).astype(F32).astype(BF16)
            live_out[late, :, over] = live
            pooled = mm_nt(live, second_high[:, over]) + mm_nt(live, second_low[:, over])
            pooled_s[late * GROUP + u] = pooled / length_of(late, u, seg_row).astype(F32)

    def in_turn(*kinds):
        running = [kind() for kind in kinds]
        while running:
            running = [parts for parts in running if next(parts, running) is not running]

    @pl.when(i == 0)
    def _():
        in_turn(attention_parts)

    @pl.when((i > 0) & (i < steps))
    def _():
        in_turn(attention_parts, feed_parts)

    @pl.when(i == steps)
    def _():
        in_turn(feed_parts)
        for u in range(nqs * GROUP):
            pooled_out[u * segs : (u + 1) * segs, :] = pooled_s[u, 0:segs, :]
        for u in range(pooled_s.shape[0] - nqs * GROUP):
            at = nqs * GROUP * segs + u
            pooled_out[at : at + 1, :] = pooled_s[nqs * GROUP + u, 0:1, :]
        rows = pooled_out[...]
        unit = rows * lax.rsqrt(jnp.sum(rows * rows, axis=1, keepdims=True) + UNIT_EPSILON)
        slots, own = lists.shape
        turn[...] = jnp.zeros_like(turn)
        turn[0:slots, 0:own] = (lists[...] // PART).astype(F32)
        turn[slots : 2 * slots, 0:own] = (lists[...] % PART).astype(F32)
        turn[2 * slots : 2 * slots + 1, 0:own] = counts[...].astype(F32)
        extra = turn[...].T[0:own, :]
        sent = jnp.concatenate([unit[:, c * 128 : (c + 1) * 128] for c in range(d // 128)] + [extra], axis=0)
        units_out[0] = sent.astype(BF16)


def step_spec(*shape):
    return pl.BlockSpec((1,) + shape, lambda i, *_: (i,) + (0,) * len(shape))


def tower_spec(nqs, *shape):
    return pl.BlockSpec((1,) + shape, lambda i, *_: (jnp.where(i < nqs, 0, 1),) + (0,) * len(shape))


def whole_spec(*shape):
    return pl.BlockSpec(shape, lambda i, *_: (0,) * len(shape))


def forward(q_lengths, p_lengths, xq, xp, attn, w_in, w_out, gains, biases, positives, counts):
    nqs, nps = xq.shape[0] // GROUP, xp.shape[0] // GROUP
    steps = nqs + nps
    span = GROUP * TOK
    d, ff = w_in.shape[1:]
    heads = d // HEAD
    seqs = q_lengths.shape[0] + xp.shape[0]
    sent = seqs * d // 128 + positives.shape[1]
    early = [
        ((d + ONES, span), BF16),
        ((2 * d, span), BF16),
        ((span, d), BF16),
        ((GROUP, heads, TOK, TOK), BF16),
        ((d + ONES, span), BF16),
        ((d, span), F32),
        ((d + ONES, span), BF16),
    ]
    later = [((ff, span), F32), ((ff + ONES, span), BF16), ((d, span), F32)]
    rows = [((8, span), F32), ((8, span), F32), ((16, span), BF16)]
    outs = early + later + rows

    kept = [pltpu.VMEM((steps,) + shape, kind) for shape, kind in outs]
    kept += [pltpu.VMEM((2,) + shape, BF16) for shape in ((d, 3 * d), (d, d), (d, ff), (ff, d))]
    kept += [pltpu.VMEM((seqs, d), F32)]
    direct = pl.BlockSpec(memory_space=pltpu.VMEM)
    return pl.pallas_call(
        functools.partial(forward_kernel, nqs),
        grid_spec=pltpu.PrefetchScalarGridSpec(
            num_scalar_prefetch=2,
            grid=(steps + 1,),
            in_specs=[
                pl.BlockSpec((GROUP, TOK, d), lambda i, *_: (jnp.minimum(i, nqs - 1), 0, 0)),
                pl.BlockSpec((GROUP, TOK, d), lambda i, *_: (jnp.clip(i - nqs, 0, nps - 1), 0, 0)),
                tower_spec(nqs, 4, d, d),
                pl.BlockSpec(memory_space=pl.ANY),
                pl.BlockSpec(memory_space=pl.ANY),
                whole_spec(2, 2, d),
                whole_spec(2, biases.shape[1]),
                whole_spec(*positives.shape),
                whole_spec(1, positives.shape[1]),
            ],
            out_specs=[direct] * (len(kept) + 1),
            scratch_shapes=[
                pltpu.VMEM((6 * d, d), BF16),
                pltpu.VMEM((d, d), BF16),
                pltpu.VMEM((ff, d), BF16),
                pltpu.VMEM((d, ff), BF16),
                pltpu.VMEM((biases.shape[1], 128), F32),
                pltpu.VMEM((2 * d, 128), F32),
                pltpu.VMEM((GROUP, d, heads * TOK), BF16),
                pltpu.VMEM((span, d), BF16),
                pltpu.VMEM((GROUP, TOK, TOK), F32),
                pltpu.VMEM((GROUP, heads, TOK, TOK), F32),
                pltpu.VMEM((d, span), F32),
                pltpu.VMEM((d, span), BF16),
                pltpu.VMEM((128, 128), F32),
                pltpu.VMEM((steps * GROUP, 16, d), F32),
                pltpu.VMEM((d, ff), F32),
                pltpu.VMEM((ff, d), F32),
                pltpu.SemaphoreType.DMA((2,)),
            ],
        ),
        out_shape=kept + [jax.ShapeDtypeStruct((1, sent, 128), BF16)],
        compiler_params=pltpu.CompilerParams(vmem_limit_bytes=FORWARD_VMEM),
        name="forward",
    )(q_lengths, p_lengths, xq, xp, attn, w_in, w_out, gains, biases, positives, counts)


def contrast_kernel(
    nqu, slots, dp, outer, qlen, plen, near, far, pooled, loss_out, gp_out, low_rows, gup_rows, gp_rows, turn
):
    devices = dp * outer
    seqs, d = pooled.shape
    own = qlen.shape[0]
    pown = seqs - own
    both = jnp.concatenate([near[...], far[...]], axis=0).astype(F32)
    parts = range(0, seqs * d // 128, seqs)
    uq = jnp.concatenate([both[:, at : at + own, :] for at in parts], axis=2).reshape(devices * own, d).astype(BF16)
    up = jnp.concatenate([both[:, at + own : at + seqs, :] for at in parts], axis=2).reshape(devices * pown, d).astype(BF16)
    lists = both[:, seqs * d // 128 :, :].reshape(devices * own, 128)
    scores = SCORE_SCALE * mm_nt(uq, up)
    place = lax.broadcasted_iota(jnp.int32, (1, devices * pown), 1)
    block = place // pown
    along = ((block // outer) % (dp // 2)) * 2 + block // (devices // 2)
    device = (lax.axis_index("dp") ^ along) * outer + (lax.axis_index("outer") ^ (block % outer))
    columns = (device * pown + place % pown).astype(F32)
    positive = None
    for k in range(slots):
        listed = lists[:, k : k + 1] * PART + lists[:, slots + k : slots + k + 1]
        hit = (listed == columns) & (lists[:, 2 * slots : 2 * slots + 1] > k)
        positive = hit if positive is None else positive | hit
    highest = jnp.max(scores, axis=1, keepdims=True)
    whole = highest + jnp.log(jnp.sum(jnp.exp(scores - highest), axis=1, keepdims=True))
    chosen = jnp.where(positive, scores, MASKED_SCORE)
    top = jnp.max(chosen, axis=1, keepdims=True)
    within = top + jnp.log(jnp.sum(jnp.exp(chosen - top), axis=1, keepdims=True))
    low = (SCORE_SCALE * (jnp.exp(scores - whole) - jnp.exp(chosen - within))).astype(BF16)
    low_rows[:, : scores.shape[1]] = low.astype(F32)
    low_rows[:, scores.shape[1] :] = jnp.broadcast_to(whole - within, (scores.shape[0], 128))
    turn[...] = jnp.zeros_like(turn)
    turn[0:own, :] = low_rows[0:own, scores.shape[1] :]
    loss_out[...] = turn[...].T[0:1, 0:own]
    grad_q = mm(low_rows[0:own, : scores.shape[1]].astype(BF16), up)
    gup_rows[...] = mm_tn(low, uq)
    grad_p = gup_rows[0:pown, :]
    grad = jnp.concatenate([grad_q, grad_p], axis=0)
    rows = pooled[...]
    inverse = lax.rsqrt(jnp.sum(rows * rows, axis=1, keepdims=True) + UNIT_EPSILON)
    grad = inverse * grad - inverse * inverse * inverse * rows * jnp.sum(rows * grad, axis=1, keepdims=True)
    segs = own // nqu
    gp_rows[...] = jnp.zeros_like(gp_rows)
    for s in range(own):
        gp_rows[s // segs, s % segs : s % segs + 1, :] = grad[s : s + 1, :] / jnp.full((1, d), qlen[s], jnp.int32).astype(F32)
    for s in range(pown):
        gp_rows[nqu + s, 0:1, :] = grad[own + s : own + s + 1, :] / jnp.full((1, d), plen[s], jnp.int32).astype(F32)
    for term, value in enumerate(split_three(gp_rows[...])):
        gp_out[:, term * 16 : (term + 1) * 16, :] = value


def contrast(nqu, npu, slots, dp, outer, q_lengths, p_lengths, near, far, pooled):
    devices = dp * outer
    seqs, d = pooled.shape
    own = q_lengths.shape[0]
    passages = devices * (seqs - own)
    vmem = pl.BlockSpec(memory_space=pltpu.VMEM)
    return pl.pallas_call(
        functools.partial(contrast_kernel, nqu, slots, dp, outer),
        in_specs=[pl.BlockSpec(memory_space=pltpu.SMEM)] * 2 + [vmem] * 3,
        out_specs=[vmem, vmem],
        out_shape=[jax.ShapeDtypeStruct((1, own), F32), pltpu.VMEM((nqu + npu, 48, d), BF16)],
        scratch_shapes=[
            pltpu.VMEM((devices * own, passages + 128), F32),
            pltpu.VMEM((passages, d), F32),
            pltpu.VMEM((nqu + npu, 16, d), F32),
            pltpu.VMEM((128, 128), F32),
        ],
        compiler_params=pltpu.CompilerParams(vmem_limit_bytes=min(VMEM_LIMIT, (6 << 20) + 32 * devices * own * passages)),
        name="contrast",
    )(q_lengths, p_lengths, near, far, pooled)


def left_rows(start_t, matrix):
    s_high, s_low = split_two(start_t)
    m_high, m_low = split_two(matrix)
    both = mm_nt(jnp.concatenate([s_high, s_low], axis=0), m_high)
    return both[:8] + both[8:] + mm_nt(jnp.concatenate([s_high, s_high], axis=0), m_low)[:8]


def right_rows(basis, matrix):
    b_high, b_low = split_two(basis)
    m_high, m_low = split_two(matrix)
    both = mm(jnp.concatenate([b_high, b_low], axis=0), m_high)
    return both[:8] + both[8:] + mm(jnp.concatenate([b_high, b_high], axis=0), m_low)[:8]


def own_core():
    return lax.axis_index("dp") % 2


def part_halves(core, whole, mine, other):
    half = whole.shape[1] // 2
    for c in range(2):

        @pl.when(core == c)
        def _(c=c):
            mine[...] = whole[:, c * half : (c + 1) * half]
            other[...] = whole[:, (1 - c) * half : (2 - c) * half]


def join_halves(core, whole, mine, other):
    half = whole.shape[1] // 2
    for c in range(2):

        @pl.when(core == c)
        def _(c=c):
            whole[:, c * half : (c + 1) * half] = mine[...]
            whole[:, (1 - c) * half : (2 - c) * half] = other[...]


def backward_kernel(
    nqs, gp, x_in, qk_in, v_in, p_in, ctx_in, n1_in, first_in, slope_in, act_in, n2_in, inv1_in, inv2_in, live_in,
    wqkv, wo, win, wout, gains, attn_err, in_err, out_err, attn_start, in_start, out_start,
    qgrad, pgrad, attn_m, in_m, out_m, left_mine, left_other,
    left, gain_bc, gz, up_s, gp_s, graw_s, gqkv, acc_qkv, acc_o, acc_in, acc_out, acc_gain, err_sems,
):
    i = pl.program_id(0)
    last = pl.num_programs(0) - 1
    is_q = i < nqs
    t = jnp.where(is_q, 0, 1)
    d = wo.shape[1]
    ff = wout.shape[1]
    errors = [
        pltpu.make_async_copy(source.at[0, tower], target.at[tower], err_sems.at[tower, k])
        for tower in range(2)
        for k, (source, target) in enumerate(((attn_err, attn_m), (in_err, in_m), (out_err, out_m)))
    ]
    heads = d // HEAD
    span = GROUP * TOK

    @pl.when(i == 0)
    def _():
        for copy in errors:
            copy.start()
        gz[...] = jnp.zeros_like(gz)

    @pl.when((i == 0) | (i == nqs))
    def _():
        for c in range(2):
            row = gains[t, c : c + 1, :]
            gain_bc[c * d : (c + 1) * d, :] = jnp.broadcast_to(row, (128, d)).T
        acc_qkv[...] = jnp.zeros_like(acc_qkv)
        acc_o[...] = jnp.zeros_like(acc_o)
        acc_in[...] = jnp.zeros_like(acc_in)
        acc_out[...] = jnp.zeros_like(acc_out)
        acc_gain[...] = jnp.zeros_like(acc_gain)

    def add_gain(at, value):
        total = value[:, :128]
        for c in range(1, span // 128):
            total = total + value[:, c * 128 : (c + 1) * 128]
        acc_gain[at * d : (at + 1) * d, :] += total

    pieces = []
    for u in range(GROUP):
        live = live_in[i, :, u * TOK : (u + 1) * TOK]
        pieces.append(mm_tn(gp[i * GROUP + u], jnp.concatenate([live, live, live], axis=0)))
    grad_second = jnp.concatenate(pieces, axis=1)
    n2 = n2_in[i]
    grad_two = norm_columns_back(grad_second, n2, inv2_in[i, 0:1, :], wide(gain_bc[d : 2 * d, :]))
    down_low = grad_two.astype(BF16)
    grad_first = grad_two
    for c in range(ff // d):
        at = slice(c * d, (c + 1) * d)
        up_low = (mm(wout[t, at, :], down_low) * slope_in[i, at, :]).astype(BF16)
        up_s[at, :] = up_low
    add_gain(1, grad_second * n2)
    add_gain(3, grad_second)
    grad_first = grad_two + mm(win[t], up_s[...])
    acc_in[...] += mm_nt(first_in[i], up_s[...])
    acc_out[...] += mm_nt(act_in[i], down_low)
    n1 = n1_in[i]
    grad_one = norm_columns_back(grad_first, n1, inv1_in[i, 0:1, :], wide(gain_bc[0:d, :]))
    branch_low = grad_one.astype(BF16)
    grad_context = mm(wo[t], branch_low).astype(BF16)
    for u in range(GROUP):
        for h in range(heads):
            at = slice(h * HEAD, (h + 1) * HEAD)
            gz[u, at, h * TOK : (h + 1) * TOK] = grad_context[at, u * TOK : (u + 1) * TOK]
    for u in range(GROUP):
        for h in range(heads):
            gp_s[u, h] = mm(v_in[i, u * TOK : (u + 1) * TOK, :], gz[u, :, h * TOK : (h + 1) * TOK])
    add_gain(0, grad_first * n1)
    add_gain(2, grad_first)
    acc_o[...] += mm_nt(ctx_in[i], branch_low)
    for u in range(GROUP):
        for h in range(heads):
            probs = p_in[i, u, h].astype(F32)
            grad_probs = gp_s[u, h]
            inner = jnp.sum(grad_probs * probs, axis=0, keepdims=True)
            graw_s[u, h] = (probs * (grad_probs - inner)).astype(BF16)
    for u in range(GROUP):
        over = slice(u * TOK, (u + 1) * TOK)
        for h in range(heads):
            at = slice(h * HEAD, (h + 1) * HEAD)
            later = slice(d + h * HEAD, d + (h + 1) * HEAD)
            last_at = slice(2 * d + h * HEAD, 2 * d + (h + 1) * HEAD)
            gqkv[last_at, over] = mm_nt(grad_context[at, over], p_in[i, u, h]).astype(BF16)
            gqkv[at, over] = mm(qk_in[i, later, over], graw_s[u, h]).astype(BF16)
            gqkv[later, over] = mm_nt(qk_in[i, at, over], graw_s[u, h]).astype(BF16)
    result = (grad_one + mm(wqkv[t], gqkv[...])).T.reshape(GROUP, TOK, d)
    acc_qkv[...] += mm_nt(x_in[i], gqkv[...])

    @pl.when(is_q)
    def _():
        qgrad[...] = result

    @pl.when(jnp.logical_not(is_q))
    def _():
        pgrad[...] = result

    @pl.when((i == nqs - 1) | (i == last))
    def _():
        for tower in range(2):

            @pl.when(t == tower)
            def _(tower=tower):
                for copy in errors[3 * tower : 3 * tower + 3]:
                    copy.wait()

        base_in = 8 * d
        base_out = base_in + 2 * d
        base_vec = base_out + 2 * ff
        for j in range(4):
            grad = acc_o[0:d, :] if j == 3 else acc_qkv[0:d, j * d : (j + 1) * d]
            merged = grad + attn_m[t, j]
            attn_m[t, j] = merged
            left[:, pl.ds(pl.multiple_of((t * 4 + j) * d, 128), d)] = left_rows(attn_start[t, j], merged)
        merged = acc_in[0:d, :] + in_m[t]
        in_m[t] = merged
        left[:, pl.ds(pl.multiple_of(base_in + t * d, 128), d)] = left_rows(in_start[t], merged)
        merged = acc_out[0:ff, :] + out_m[t]
        out_m[t] = merged
        left[:, pl.ds(pl.multiple_of(base_out + t * ff, 128), ff)] = left_rows(out_start[t], merged)
        sums = mm_nt(jnp.ones((8, 128), F32), acc_gain[...], HIGHEST)

        def vectors():
            yield sums[0:1, 0:d]
            yield sums[0:1, d : 2 * d]
            yield acc_qkv[d : d + 1, 0:d]
            yield acc_qkv[d : d + 1, 2 * d : 3 * d]
            yield acc_o[d : d + 1, :]
            yield sums[0:1, 2 * d : 3 * d]
            yield acc_out[ff : ff + 1, :]
            yield sums[0:1, 3 * d : 4 * d]
            for c in range(ff // d):
                yield acc_in[d : d + 1, c * d : (c + 1) * d]

        for tower in range(2):

            @pl.when(t == tower)
            def _(tower=tower):
                for v, vector in enumerate(vectors()):
                    at = tower * 12 + v
                    left[at // 3 : at // 3 + 1, base_vec + (at % 3) * d : base_vec + (at % 3 + 1) * d] = vector

    @pl.when(i == last)
    def _():
        part_halves(own_core(), left, left_mine, left_other)


def backward(nqs, nps, gp, saved, low_weights, gains, errors, starts):
    steps = nqs + nps
    nqu, npu = nqs * GROUP, nps * GROUP
    span = GROUP * TOK
    d, ff = errors[1].shape[2:]
    heads = d // HEAD
    width = 8 * d + 2 * d + 2 * ff + 3 * d
    direct = pl.BlockSpec(memory_space=pltpu.VMEM)
    far = pl.BlockSpec(memory_space=pl.ANY)
    return pl.pallas_call(
        functools.partial(backward_kernel, nqs),
        grid=(steps,),
        in_specs=[direct] * (len(saved) + 6) + [far] * 3 + [direct] * 3,
        out_specs=[
            pl.BlockSpec((GROUP, TOK, d), lambda i: (jnp.minimum(i, nqs - 1), 0, 0)),
            pl.BlockSpec((GROUP, TOK, d), lambda i: (jnp.maximum(i - nqs, 0), 0, 0)),
        ]
        + [direct] * 5,
        out_shape=[
            jax.ShapeDtypeStruct((nqu, TOK, d), F32),
            jax.ShapeDtypeStruct((npu, TOK, d), F32),
            pltpu.VMEM((2, 4, d, d), F32),
            pltpu.VMEM((2, d, ff), F32),
            pltpu.VMEM((2, ff, d), F32),
            jax.ShapeDtypeStruct((8, width // 2), F32),
            jax.ShapeDtypeStruct((8, width // 2), F32),
        ],
        scratch_shapes=[
            pltpu.VMEM((8, width), F32),
            pltpu.VMEM((2 * d, 128), F32),
            pltpu.VMEM((GROUP, d, heads * TOK), BF16),
            pltpu.VMEM((ff, span), BF16),
            pltpu.VMEM((GROUP, heads, TOK, TOK), F32),
            pltpu.VMEM((GROUP, heads, TOK, TOK), BF16),
            pltpu.VMEM((3 * d, span), BF16),
            pltpu.VMEM((d + ONES, 3 * d), F32),
            pltpu.VMEM((d + ONES, d), F32),
            pltpu.VMEM((d + ONES, ff), F32),
            pltpu.VMEM((ff + ONES, d), F32),
            pltpu.VMEM((4 * d, 128), F32),
            pltpu.SemaphoreType.DMA((2, 3)),
        ],
        compiler_params=pltpu.CompilerParams(vmem_limit_bytes=BACKWARD_VMEM),
        name="backward",
    )(gp, *saved, *low_weights, gains, *errors, *starts)


def gram(rows):
    terms = split_three(rows)
    high, middle, low = terms
    left = jnp.concatenate([high, high, middle, high, middle, low], axis=1)
    right = jnp.concatenate([high, middle, high, low, middle, high], axis=1)
    return mm_nt(left, right)


def right_kernel(
    left_mine, left_other, attn_m, in_m, out_m, attn_mom, in_mom, out_mom,
    basis, right_mine, right_other, vector, grams, attn_held, in_held, out_held, left, right, sems,
):
    moments = [
        pltpu.make_async_copy(source, target, sems.at[k])
        for k, (source, target) in enumerate(((attn_mom, attn_held), (in_mom, in_held), (out_mom, out_held)))
    ]
    for copy in moments:
        copy.start()
    d, ff = in_m.shape[1:]
    core = own_core()
    join_halves(core, left, left_mine, left_other)
    vector[...] = left[:, 10 * d + 2 * ff :]
    places = [(j * d, d) for j in range(8)] + [(8 * d + t * d, d) for t in range(2)] + [(10 * d + t * ff, ff) for t in range(2)]
    blocks = [left[:, at : at + size] for at, size in places]
    for j in range(8):
        for b, block in enumerate(blocks):
            order = lax.broadcasted_iota(jnp.int32, (8, 1), 0)
            column = block[j : j + 1, :]
            dots = jnp.sum(block * column, axis=1, keepdims=True)
            scale = lax.rsqrt(dots[j : j + 1, :] + 1e-06)
            unit = column * scale
            step = jnp.where(order > j, dots * scale, 0.0)
            blocks[b] = jnp.where(order == j, unit, block - step * unit)
    for k, ((at, size), block) in enumerate(zip(places, blocks)):
        basis[:, at : at + size] = block
        grams[k] = gram(block)
    for j in range(8):
        right[:, j * d : (j + 1) * d] = right_rows(blocks[j], attn_m[j // 4, j % 4])
    for t in range(2):
        right[:, 8 * d + t * ff : 8 * d + (t + 1) * ff] = right_rows(blocks[8 + t], in_m[t])
        right[:, 8 * d + 2 * ff + t * d : 8 * d + 2 * ff + (t + 1) * d] = right_rows(blocks[10 + t], out_m[t])
    part_halves(core, right, right_mine, right_other)
    for copy in moments:
        copy.wait()


def right_factors(left_mine, left_other, merged, moments):
    d, ff = merged[1].shape[1:]
    vmem = pl.BlockSpec(memory_space=pltpu.VMEM)
    width = 10 * d + 2 * ff
    rows = functools.partial(jax.ShapeDtypeStruct, dtype=F32)
    return pl.pallas_call(
        right_kernel,
        in_specs=[vmem] * 5 + [pl.BlockSpec(memory_space=pl.ANY)] * 3,
        out_specs=[vmem] * 8,
        out_shape=[rows((8, width)), rows((8, width // 2)), rows((8, width // 2)), rows((8, 3 * d)), rows((12, 8, 8))]
        + [pltpu.VMEM(a.shape, F32) for a in moments],
        scratch_shapes=[pltpu.VMEM((8, width + 3 * d), F32), pltpu.VMEM((8, width), F32), pltpu.SemaphoreType.DMA((3,))],
        compiler_params=pltpu.CompilerParams(vmem_limit_bytes=12 << 20),
        name="right",
    )(left_mine, left_other, *merged, *(pltpu.with_memory_space_constraint(a, pltpu.HBM) for a in moments))


def update_kernel(
    replicas, basis, right_mine, right_other, vector, grams, gains, biases, gain_mom, bias_mom,
    attn_m, in_m, out_m, attn, w_in, w_out, attn_mom, in_mom, out_mom,
    attn_new, in_new, out_new, attn_mom_new, in_mom_new, out_mom_new, attn_err, in_err, out_err,
    gains_new, biases_new, gain_mom_new, bias_mom_new, attn_factor, in_factor, out_factor, norm_out,
    right, clip_s,
):
    i = pl.program_id(0)
    d, ff = w_in.shape[1:]
    t, c = i // 2, i % 2

    @pl.when(i == 0)
    def _():
        join_halves(own_core(), right, right_mine, right_other)
        for j in range(8):
            attn_factor[j // 4, j % 4] = right[:, j * d : (j + 1) * d]
        for s in range(2):
            in_factor[s] = right[:, 8 * d + s * ff : 8 * d + (s + 1) * ff]
            out_factor[s] = right[:, 8 * d + 2 * ff + s * d : 8 * d + 2 * ff + (s + 1) * d]
        places = [(j * d, d) for j in range(8)]
        places += [(8 * d + s * ff, ff) for s in range(2)] + [(8 * d + 2 * ff + s * d, d) for s in range(2)]
        total = jnp.zeros((8, 8), F32)
        for k, (at, size) in enumerate(places):
            total = total + grams[k] * gram(right[:, at : at + size])
        sums = vector[...]
        square = jnp.sum(jnp.sum(total, axis=1, keepdims=True), axis=0, keepdims=True)
        square = square + jnp.sum(jnp.sum(sums * sums, axis=1, keepdims=True), axis=0, keepdims=True)
        norm = jnp.sqrt(jnp.broadcast_to(square, (8, 128)))
        norm_out[0] = norm[0, 0]
        clip_s[...] = jnp.minimum(1.0, CLIP_NORM / norm)
        held = clip_s[0:1, 0:1]
        for s in range(2):
            for v in range(12):
                at = s * 12 + v
                reduced = vector[at // 3 : at // 3 + 1, (at % 3) * d : (at % 3 + 1) * d]
                if v < 2:
                    moved = MOMENTUM_DECAY * gain_mom[s, v : v + 1, :] + held * reduced
                    gain_mom_new[s, v : v + 1, :] = moved
                    gains_new[s, v : v + 1, :] = gains[s, v : v + 1, :] - LEARNING_RATE * moved
                else:
                    over = slice((v - 2) * d, (v - 1) * d)
                    moved = MOMENTUM_DECAY * bias_mom[s : s + 1, over] + held * reduced
                    bias_mom_new[s : s + 1, over] = moved
                    biases_new[s : s + 1, over] = biases[s : s + 1, over] - LEARNING_RATE * moved

    clip = clip_s[0:1, 0:1]

    def step(b_at, b_size, r_at, r_size, merged, weight, moment, weight_new, moment_new, error):
        b1, b2, b3 = split_three(basis[:, pl.ds(pl.multiple_of(b_at, 128), b_size)])
        r1, r2, r3 = split_three(right[:, pl.ds(pl.multiple_of(r_at, 128), r_size)])
        approx = mm_tn(jnp.concatenate([b1, b1, b2, b1, b2, b3], axis=0), jnp.concatenate([r1, r2, r1, r3, r2, r1], axis=0))
        moved = MOMENTUM_DECAY * moment + clip * approx
        moment_new[...] = moved.reshape(moment_new.shape)
        weight_new[...] = (weight - LEARNING_RATE * moved).reshape(weight_new.shape)
        error[...] = (merged - approx * (1.0 / replicas)).reshape(error.shape)

    wider = ff // 2
    across = pl.ds(pl.multiple_of(c * wider, 128), wider)
    for j in range(2):
        k = c * 2 + j
        step(
            (t * 4 + k) * d, d, (t * 4 + k) * d, d, attn_m[t, k], attn[t, k], attn_mom[t, k],
            attn_new.at[0, j], attn_mom_new.at[0, j], attn_err.at[0, 0, j],
        )
    step(
        (8 + t) * d, d, 8 * d + t * ff + c * wider, wider,
        in_m[t, :, across], w_in[t, :, across], in_mom[t, :, across], in_new, in_mom_new, in_err,
    )
    step(
        10 * d + t * ff + c * wider, wider, 8 * d + 2 * ff + t * d, d,
        out_m[t, across, :], w_out[t, across, :], out_mom[t, across, :], out_new, out_mom_new, out_err,
    )


def update(replicas, basis, right_mine, right_other, vector, grams, gains, biases, gain_mom, bias_mom, merged, weights, moments):
    d, ff = weights[1].shape[1:]
    half = ff // 2
    a_spec = pl.BlockSpec((1, 2, d, d), lambda i: (i // 2, i % 2, 0, 0))
    i_spec = pl.BlockSpec((1, d, half), lambda i: (i // 2, 0, i % 2))
    o_spec = pl.BlockSpec((1, half, d), lambda i: (i // 2, i % 2, 0))
    ae_spec = pl.BlockSpec((1, 1, 2, d, d), lambda i: (0, i // 2, i % 2, 0, 0))
    ie_spec = pl.BlockSpec((1, 1, d, half), lambda i: (0, i // 2, 0, i % 2))
    oe_spec = pl.BlockSpec((1, 1, half, d), lambda i: (0, i // 2, i % 2, 0))
    rows = functools.partial(jax.ShapeDtypeStruct, dtype=F32)
    small = (basis, right_mine, right_other, vector, grams, gains, biases, gain_mom, bias_mom)
    direct = pl.BlockSpec(memory_space=pltpu.VMEM)
    finals = [gains.shape, biases.shape] * 2 + [(2, 4, 8, d), (2, 8, ff), (2, 8, d)]
    return pl.pallas_call(
        functools.partial(update_kernel, replicas),
        grid=(4,),
        in_specs=[direct] * (len(small) + 9),
        out_specs=[a_spec, i_spec, o_spec] * 2
        + [ae_spec, ie_spec, oe_spec]
        + [whole_spec(*shape) for shape in finals]
        + [pl.BlockSpec(memory_space=pltpu.SMEM)],
        out_shape=[rows(a.shape) for a in weights * 2]
        + [rows((1,) + a.shape) for a in weights]
        + [rows(shape) for shape in finals]
        + [rows((1,))],
        scratch_shapes=[pltpu.VMEM(basis.shape, F32), pltpu.VMEM((8, 128), F32)],
        compiler_params=pltpu.CompilerParams(vmem_limit_bytes=22 << 20),
        name="update",
    )(*small, *merged, *weights, *moments)


def in_vmem(*arrays):
    return tuple(pltpu.with_memory_space_constraint(a, pltpu.VMEM) for a in arrays)


def swap_with(x, axis, mask):
    return lax.ppermute(x, axis, [(i, i ^ mask) for i in range(lax.axis_size(axis))])


def chip_steps():
    size = lax.axis_size("dp")
    if size == 8:
        return [("dp", (2, 4, 6))]
    return [("dp", (1 << b,)) for b in range(1, size.bit_length() - 1)]


def outer_step():
    return ("outer", tuple(range(1, lax.axis_size("outer"))))


def gather_blocks(x):
    for axis, masks in [outer_step()] + chip_steps():
        x = jnp.concatenate([x] + [swap_with(x, axis, mask) for mask in masks], axis=0)
    return x, swap_with(x, "dp", 1)


def sum_halves(mine, other):
    mine = mine + swap_with(other, "dp", 1)
    for axis, masks in chip_steps() + [outer_step()]:
        sent = mine.astype(SEND)
        mine = sent.astype(F32)
        for got in [swap_with(sent, axis, mask) for mask in masks]:
            mine = mine + got.astype(F32)
    return mine, swap_with(mine, "dp", 1)


def per_device(
    questions, passages, q_lengths, p_lengths, positives, pos_counts, attn, w_in, w_out, gains, biases, attn_mom, w_in_mom,
    w_out_mom, gain_mom, bias_mom, attn_err, w_in_err, w_out_err, attn_start, w_in_start, w_out_start,
):
    devices = lax.axis_size("dp") * lax.axis_size("outer")
    d, ff = w_in.shape[1:]
    xq = questions.reshape(-1, TOK, d)
    xp = passages.reshape(-1, TOK, d)
    nqu, npu = xq.shape[0], xp.shape[0]
    *saved, wqkv, wo, win, wout, pooled, units = forward(
        q_lengths, p_lengths, xq, xp, attn, w_in, w_out, gains, biases, positives.T, pos_counts.reshape(1, -1)
    )
    dp, outer = lax.axis_size("dp"), lax.axis_size("outer")
    near, far = gather_blocks(units)
    loss, gp = contrast(nqu, npu, positives.shape[1], dp, outer, q_lengths, p_lengths, *in_vmem(near, far, pooled))
    starts = [jnp.swapaxes(start, -1, -2) for start in (attn_start, w_in_start, w_out_start)]
    qgrad, pgrad, attn_m, in_m, out_m, *left = backward(
        nqu // GROUP, npu // GROUP, *in_vmem(gp), in_vmem(*saved), in_vmem(wqkv, wo, win, wout), gains,
        (attn_err, w_in_err, w_out_err), starts,
    )
    weights = (attn, w_in, w_out)
    moments = (attn_mom, w_in_mom, w_out_mom)
    merged = in_vmem(attn_m, in_m, out_m)
    basis, *right, vector, grams, mom_a, mom_b, mom_c = right_factors(*sum_halves(*left), merged, moments)
    held = in_vmem(*weights, mom_a, mom_b, mom_c)
    *new, attn_factor, in_factor, out_factor, norm = update(
        devices, basis, *sum_halves(*right), vector, grams, gains, biases, gain_mom, bias_mom,
        merged, held[:3], held[3:],
    )
    weights_new, moments_new, errors_new, vectors_new = new[:3], new[3:6], new[6:9], new[9:]
    factors = [jnp.swapaxes(factor, -1, -2) for factor in (attn_factor, in_factor, out_factor)]
    return (
        loss.reshape(-1), qgrad.reshape(questions.shape), pgrad.reshape(passages.shape),
        *weights_new, *vectors_new[:2], *moments_new, *vectors_new[2:], *errors_new, *factors, norm.reshape(()),
    )


def solution(mesh):
    split = ("dp", "outer")
    share = P(split)
    return jax.shard_map(
        per_device,
        mesh=mesh,
        in_specs=(share,) * 6 + (P(),) * 10 + (share,) * 3 + (P(),) * 3,
        out_specs=(share,) * 3 + (P(),) * 10 + (share,) * 3 + (P(),) * 4,
        check_vma=False,
    )
```
